32 devices in a mesh: dp: 8 (over z, y), mp: 4 (over x, core).
Axes of the slice: x: 2, y: 2, z: 4, core: 2. Of those that a mesh axis runs over, the one named last changes fastest.
Arguments:
- patches: bfloat16 [4, 8192, 768], P(None, ('dp', 'mp')), may hold values from -6 to 6
- heights: int32 [4, 512], P(None, ('dp', 'mp')), may hold values from 0 to 32, as said below
- widths: int32 [4, 512], P(None, ('dp', 'mp')), may hold values from 0 to 32, as said below
- labels: int32 [4, 512], P(None, 'dp'), may hold values from 0 to 999
- res_weights: int32 [4, 512], P(None, 'dp'), may hold values from 0 to 8, as said below
- w_embed: float32 [1024, 768], P(('dp', 'mp'))
- w_qkv: float32 [768, 2304], P(('dp', 'mp')), may hold values from -0.21875 to 0.21875
- w_out: float32 [768, 768], P(('dp', 'mp')), may hold values from -0.875 to 0.875
- w_up: float32 [768, 3072], P(('dp', 'mp')), may hold values from -0.21875 to 0.21875
- w_down: float32 [3072, 768], P(('dp', 'mp')), may hold values from -0.109375 to 0.109375
- vectors: float32 [6, 768], P(None, ('dp', 'mp'))
- w_cls: float32 [768, 1000], P('dp', 'mp')
- m_embed: float32 [1024, 768], P(('dp', 'mp')), may hold values from -2.3841858e-06 to 2.3841858e-06
- v_embed: float32 [1024, 768], P(('dp', 'mp')), may hold values from 1.1578191e-14 to 4.6312763e-14
- m_qkv: float32 [768, 2304], P(('dp', 'mp')), may hold values from -2.3841858e-06 to 2.3841858e-06
- v_qkv: float32 [768, 2304], P(('dp', 'mp')), may hold values from 1.1578191e-14 to 4.6312763e-14
- m_out: float32 [768, 768], P(('dp', 'mp')), may hold values from -2.3841858e-06 to 2.3841858e-06
- v_out: float32 [768, 768], P(('dp', 'mp')), may hold values from 1.1578191e-14 to 4.6312763e-14
- m_up: float32 [768, 3072], P(('dp', 'mp')), may hold values from -2.3841858e-06 to 2.3841858e-06
- v_up: float32 [768, 3072], P(('dp', 'mp')), may hold values from 1.1578191e-14 to 4.6312763e-14
- m_down: float32 [3072, 768], P(('dp', 'mp')), may hold values from -2.3841858e-06 to 2.3841858e-06
- v_down: float32 [3072, 768], P(('dp', 'mp')), may hold values from 1.1578191e-14 to 4.6312763e-14
- m_vectors: float32 [6, 768], P(None, ('dp', 'mp')), may hold values from -3.8146973e-06 to 3.8146973e-06
- v_vectors: float32 [6, 768], P(None, ('dp', 'mp')), may hold values from 2.8945477e-14 to 1.1578191e-13
- m_cls: float32 [768, 1000], P('dp', 'mp'), may hold values from -2.3841858e-06 to 2.3841858e-06
- v_cls: float32 [768, 1000], P('dp', 'mp'), may hold values from 1.1578191e-14 to 4.6312763e-14
Outputs:
- loss_terms: float32 [2], replicated
- clip_norm: float32 [], replicated
- lamb_norms: float32 [12, 2], replicated
- embed_new: float32 [1024, 768], P(('dp', 'mp'))
- embed_first: float32 [1024, 768], P(('dp', 'mp'))
- embed_second: float32 [1024, 768], P(('dp', 'mp'))
- qkv_new: float32 [768, 2304], P(('dp', 'mp'))
- qkv_first: float32 [768, 2304], P(('dp', 'mp'))
- qkv_second: float32 [768, 2304], P(('dp', 'mp'))
- out_new: float32 [768, 768], P(('dp', 'mp'))
- out_first: float32 [768, 768], P(('dp', 'mp'))
- out_second: float32 [768, 768], P(('dp', 'mp'))
- up_new: float32 [768, 3072], P(('dp', 'mp'))
- up_first: float32 [768, 3072], P(('dp', 'mp'))
- up_second: float32 [768, 3072], P(('dp', 'mp'))
- down_new: float32 [3072, 768], P(('dp', 'mp'))
- down_first: float32 [3072, 768], P(('dp', 'mp'))
- down_second: float32 [3072, 768], P(('dp', 'mp'))
- vectors_new: float32 [6, 768], P(None, ('dp', 'mp'))
- vectors_first: float32 [6, 768], P(None, ('dp', 'mp'))
- vectors_second: float32 [6, 768], P(None, ('dp', 'mp'))
- cls_new: float32 [768, 1000], P('dp', 'mp')
- cls_first: float32 [768, 1000], P('dp', 'mp')
- cls_second: float32 [768, 1000], P('dp', 'mp')
The draws below stay inside these ranges and needn't reach their ends.
Inputs may be any that keep to these rules, and one draw needn't show every extreme that they name: In each device's slots of a micro-batch the filled slots come first and the last slot is empty; a slot is filled exactly when its height and width are 2 or more, and then height times width is at most 256; the filled slots' heights times widths add up to at most 256, and empty slots have height and width 0. `widths`: zero exactly where heights is zero. `res_weights`: zero exactly on empty slots, 1 or more on filled ones.
All inputs are finite; a program needn't handle non-finite values.
Results may differ from the reference program's by a relative error of at most 0.025.
The reference program's roundings to bfloat16 on the way count: a program that leaves them out, or rounds other values in their place, can miss the bound.
Values may be sent and summed in bfloat16 or wider, within the bound.
A program may use at most 192 MiB of HBM per device.

```python
import jax
import jax.numpy as jnp
from jax import lax

D = 768
HEADS = 12
HEAD = 64
FF = 3072
PIX = 768
CLASSES = 1000
POS = 128
EROWS = 1024
TOK_DEV = 256
IMG_DEV = 16
MAXSIDE = 32
MICRO = 4
STEP = 10
TOKENS = 8192
IMAGES = 512
PARAMS = 8636928
N_DP = 8
N_MP = 4


def pack_layout(key):
    device_count = IMAGES // IMG_DEV
    pack_count = MICRO * device_count
    key_height, key_width, key_target, key_weight = jax.random.split(key, 4)
    heights = jax.random.randint(key_height, (pack_count, IMG_DEV), 2, MAXSIDE + 1)
    heights = heights.at[0, 0].set(MAXSIDE).at[1, 0].set(2)
    widest = jnp.minimum(MAXSIDE, TOK_DEV // heights)
    widths = jax.random.randint(key_width, (pack_count, IMG_DEV), 2, widest + 1)
    widths = widths.at[1, 0].set(MAXSIDE)
    lengths = heights * widths
    target = jax.random.randint(key_target, (pack_count, 1), TOK_DEV // 2, TOK_DEV + 1)
    target = jnp.maximum(target, lengths[:, :1])
    keep = jnp.cumsum(lengths, axis=1) <= target
    keep = keep.at[:, IMG_DEV - 1].set(False)
    device = jnp.arange(pack_count, dtype=jnp.int32) % device_count
    upper = 2 + 4 * (device // N_MP) // N_DP + 4 * (device % N_MP) // N_MP
    weights = jax.random.randint(key_weight, (pack_count, IMG_DEV), 1, upper[:, None] + 1)
    weights = weights.at[device_count - 1, 0].set(upper[device_count - 1])
    zero_fill = jnp.zeros_like(heights)
    target_shape = (MICRO, IMAGES)
    return (jnp.where(keep, heights, zero_fill).reshape(target_shape), jnp.where(keep, widths, zero_fill).reshape(target_shape), jnp.where(keep, weights, zero_fill).reshape(target_shape))


def draw_heights(key, part):
    packed = pack_layout(key)
    return packed[0]


def draw_widths(key, part):
    packed = pack_layout(key)
    return packed[1]


def draw_res_weights(key, part):
    packed = pack_layout(key)
    return packed[2]


def draw_w_embed(key, part):
    key = jax.random.fold_in(key, 5)
    values = jax.random.normal(key, (EROWS, D), jnp.float32)
    row_scale = jnp.where(jnp.arange(EROWS)[:, None] < PIX, PIX ** (-0.5), 0.5)
    return values * row_scale


def draw_vectors(key, part):
    key = jax.random.fold_in(key, 7)
    key_gain, key_norm, key_probe = jax.random.split(key, 3)
    place = jnp.arange(D, dtype=jnp.float32) / D
    gains = (1.0 + 2.0 * place) * jax.random.uniform(key_gain, (3, D), jnp.float32, 0.75, 1.25)
    probe = jax.random.normal(key_probe, (1, D), jnp.float32)
    norm_gains = jax.random.uniform(key_norm, (2, D), jnp.float32, 0.8, 1.6)
    return jnp.concatenate([gains, norm_gains, probe], axis=0)


def draw_w_cls(key, part):
    key = jax.random.fold_in(key, 9)
    place = jnp.arange(CLASSES, dtype=jnp.float32) / CLASSES
    values = jax.random.normal(key, (D, CLASSES), jnp.float32)
    column_scale = 1.0 + 2.0 * place
    return values * column_scale[None, :] * D ** (-0.5)


def set_ends(array, own_key, least, top_value):
    spot = [jax.random.randint(jax.random.fold_in(own_key, axis), (), 0, length) for axis, length in enumerate(array.shape)]
    widest = array.shape.index(max(array.shape))
    beside = spot[:widest] + [(spot[widest] + 1) % array.shape[widest]] + spot[widest + 1:]
    return array.at[tuple(spot)].set(least).at[tuple(beside)].set(top_value)


def block_levels(rng, dims, pieces, low, top_value):
    loudness, own = 1.0, jax.random.fold_in(rng, 6)
    for dim, shards_of in pieces:
        steps = jnp.exp(jax.random.uniform(jax.random.fold_in(own, dim), (shards_of,), jnp.float32, low / len(pieces), top_value / len(pieces)))
        loudness = loudness * jnp.repeat(steps, dims[dim] // shards_of).reshape([-1 if axis == dim else 1 for axis in range(len(dims))])
    return loudness


def gaussian(key, dims, scale, limit, cuts=(), held_as=jnp.bfloat16):
    entries = scale * jax.random.normal(key, dims, jnp.float32)
    if cuts:
        entries = entries * block_levels(key, dims, cuts, -0.22, 0.18)
    return jnp.clip(entries, -limit, limit).astype(held_as)


def setup_inputs(seed: int = 0) -> dict:
    splits = jax.random.split(jax.random.key(seed), 27)
    patches = gaussian(splits[0], (MICRO, TOKENS, PIX), 1.0, 6.0, ((1, 32),))
    heights = draw_heights(jax.random.fold_in(splits[26], 71), 0)
    widths = draw_widths(jax.random.fold_in(splits[26], 71), 0)
    labels = set_ends(jax.random.randint(splits[3], (MICRO, IMAGES), 0, CLASSES), jax.random.fold_in(splits[3], 1), 0, CLASSES - 1).astype(jnp.int32)
    res_weights = draw_res_weights(jax.random.fold_in(splits[26], 71), 0)
    w_embed = draw_w_embed(jax.random.fold_in(splits[26], 71), 0)
    w_qkv = gaussian(splits[6], (D, 3 * D), D ** -0.5, 0.21875, ((0, 32),), jnp.float32)
    w_out = gaussian(splits[7], (D, D), (D // 16) ** -0.5, 0.875, ((0, 32),), jnp.float32)
    w_up = gaussian(splits[8], (D, FF), D ** -0.5, 0.21875, ((0, 32),), jnp.float32)
    w_down = gaussian(splits[9], (FF, D), FF ** -0.5, 0.109375, ((0, 32),), jnp.float32)
    vectors = draw_vectors(jax.random.fold_in(splits[26], 71), 0)
    w_cls = draw_w_cls(jax.random.fold_in(splits[26], 71), 0)
    m_embed = gaussian(splits[12], (EROWS, D), (0.0011 * PARAMS ** -0.5), 2.384185791015625e-06, ((0, 32),), jnp.float32)
    v_embed = jnp.clip(1.1578190764807966e-14 + 3.4734572294423897e-14 * jax.random.uniform(splits[13], (EROWS, D), jnp.float32) ** block_levels(splits[13], (EROWS, D), ((0, 32),), -0.2, 0.2), 1.1578190764807966e-14, 4.631276305923186e-14)
    m_qkv = gaussian(splits[14], (D, 3 * D), (0.0011 * PARAMS ** -0.5), 2.384185791015625e-06, ((0, 32),), jnp.float32)
    v_qkv = jnp.clip(1.1578190764807966e-14 + 3.4734572294423897e-14 * jax.random.uniform(splits[15], (D, 3 * D), jnp.float32) ** block_levels(splits[15], (D, 3 * D), ((0, 32),), -0.2, 0.2), 1.1578190764807966e-14, 4.631276305923186e-14)
    m_out = gaussian(splits[16], (D, D), (0.0011 * PARAMS ** -0.5), 2.384185791015625e-06, ((0, 32),), jnp.float32)
    v_out = jnp.clip(1.1578190764807966e-14 + 3.4734572294423897e-14 * jax.random.uniform(splits[17], (D, D), jnp.float32) ** block_levels(splits[17], (D, D), ((0, 32),), -0.2, 0.2), 1.1578190764807966e-14, 4.631276305923186e-14)
    m_up = gaussian(splits[18], (D, FF), (0.0011 * PARAMS ** -0.5), 2.384185791015625e-06, ((0, 32),), jnp.float32)
    v_up = jnp.clip(1.1578190764807966e-14 + 3.4734572294423897e-14 * jax.random.uniform(splits[19], (D, FF), jnp.float32) ** block_levels(splits[19], (D, FF), ((0, 32),), -0.2, 0.2), 1.1578190764807966e-14, 4.631276305923186e-14)
    m_down = gaussian(splits[20], (FF, D), (0.0011 * PARAMS ** -0.5), 2.384185791015625e-06, ((0, 32),), jnp.float32)
    v_down = jnp.clip(1.1578190764807966e-14 + 3.4734572294423897e-14 * jax.random.uniform(splits[21], (FF, D), jnp.float32) ** block_levels(splits[21], (FF, D), ((0, 32),), -0.2, 0.2), 1.1578190764807966e-14, 4.631276305923186e-14)
    m_vectors = gaussian(splits[22], (6, D), (0.002 * PARAMS ** -0.5), 3.814697265625e-06, ((1, 32),), jnp.float32)
    v_vectors = jnp.clip(2.894547733553639e-14 + 8.683643200660916e-14 * jax.random.uniform(splits[23], (6, D), jnp.float32) ** block_levels(splits[23], (6, D), ((1, 32),), -0.2, 0.2), 2.894547733553639e-14, 1.1578190934214555e-13)
    m_cls = gaussian(splits[24], (D, CLASSES), (0.0011 * PARAMS ** -0.5), 2.384185791015625e-06, ((0, 8), (1, 4)), jnp.float32)
    v_cls = jnp.clip(1.1578190764807966e-14 + 3.4734572294423897e-14 * jax.random.uniform(splits[25], (D, CLASSES), jnp.float32) ** block_levels(splits[25], (D, CLASSES), ((0, 8), (1, 4)), -0.2, 0.2), 1.1578190764807966e-14, 4.631276305923186e-14)
    return dict(patches=patches, heights=heights, widths=widths, labels=labels, res_weights=res_weights, w_embed=w_embed, w_qkv=w_qkv, w_out=w_out, w_up=w_up, w_down=w_down, vectors=vectors, w_cls=w_cls, m_embed=m_embed, v_embed=v_embed, m_qkv=m_qkv, v_qkv=v_qkv, m_out=m_out, v_out=v_out, m_up=m_up, v_up=v_up, m_down=m_down, v_down=v_down, m_vectors=m_vectors, v_vectors=v_vectors, m_cls=m_cls, v_cls=v_cls)


epsilon = 1e-06
clip_limit = 0.01
learn_rate = 0.3
beta_first = 0.9
beta_second = 0.999
weight_decay = 0.01
adam_floor = 1e-08
highest = lax.Precision.HIGHEST
excluded = -1e+30

@jax.custom_vjp
def low(v):
    return lax.optimization_barrier(v.astype(jnp.bfloat16)).astype(jnp.float32)

@jax.custom_vjp
def low_back(v):
    return v

def low_keep(v):
    return (low(v), None)

def low_pass(kept, grad):
    return (grad,)

def back_keep(v):
    return (v, None)

def back_low(kept, grad):
    return (low(grad),)
low.defvjp(low_keep, low_pass)
low_back.defvjp(back_keep, back_low)

def layer_norm(values, scales):
    center = values - lax.optimization_barrier(jnp.mean(values, axis=-1, keepdims=True))
    spread = lax.optimization_barrier(jnp.mean(center * center, axis=-1, keepdims=True))
    return center * lax.rsqrt(spread + epsilon) * scales

def layout(heights, widths):
    lengths = heights * widths
    image_ends = jnp.cumsum(lengths)
    starts = image_ends - lengths
    places = jnp.arange(TOK_DEV, dtype=jnp.int32)
    slot_ids = jnp.arange(IMG_DEV, dtype=jnp.int32)
    segment = lax.optimization_barrier(jnp.sum((places[:, None] >= image_ends[None, :]).astype(jnp.int32), axis=1))
    member = segment[None, :] == slot_ids[:, None]
    member_int = member.T.astype(jnp.int32)
    within = places - lax.optimization_barrier(jnp.sum(member_int * starts[None, :], axis=1))
    across = jnp.maximum(lax.optimization_barrier(jnp.sum(member_int * widths[None, :], axis=1)), 1)
    upright = jnp.maximum(lax.optimization_barrier(jnp.sum(member_int * heights[None, :], axis=1)), 1)
    col_pos = within % across * POS // across
    row_pos = within // across * POS // upright
    pos_table = jnp.arange(POS, dtype=jnp.int32)
    pos_rows = jnp.concatenate([col_pos[:, None] == pos_table[None, :], row_pos[:, None] == pos_table[None, :]], axis=1)
    return (segment, member, pos_rows)

def pack_forward(layer_low, patch_rows, heights, widths):
    embed, joined_w, out_w, up_w, down_w, vectors = layer_low
    segment, member, pos_rows = layout(heights, widths)
    row_count = patch_rows.shape[0]
    head_shape = (row_count, HEADS, HEAD)
    score_scale = HEAD ** (-0.5)
    inputs = jnp.concatenate([patch_rows, pos_rows.astype(jnp.float32)], axis=1)
    embedded = low_back(jnp.dot(inputs, embed, precision=highest))
    normed = low(layer_norm(embedded, vectors[0]))
    joined = low_back(jnp.dot(normed, joined_w, precision=highest))
    queries = low(layer_norm(joined[:, :D].reshape(head_shape), vectors[3].reshape(HEADS, HEAD)))
    key_rows = low(layer_norm(joined[:, D:2 * D].reshape(head_shape), vectors[4].reshape(HEADS, HEAD)))
    value_rows = low(joined[:, 2 * D:].reshape(head_shape))
    scores = low_back(jnp.einsum('thd,shd->hts', queries, key_rows, precision=highest) * score_scale)
    same_image = segment[:, None] == segment[None, :]
    scores = jnp.where(same_image[None], scores, excluded)
    attention = low(jax.nn.softmax(scores, axis=-1))
    mixed_heads = low(low_back(jnp.einsum('hts,shd->thd', attention, value_rows, precision=highest)))
    second = embedded + low_back(jnp.dot(mixed_heads.reshape(row_count, D), out_w, precision=highest))
    hidden = low(layer_norm(second, vectors[1]))
    upward = low_back(jnp.dot(hidden, up_w, precision=highest))
    active = low(jax.nn.gelu(upward))
    residual = second + low_back(jnp.dot(active, down_w, precision=highest))
    final_heads = low(layer_norm(residual, vectors[2])).reshape(head_shape)
    probe_scores = jnp.einsum('thd,hd->th', final_heads, vectors[5].reshape(HEADS, HEAD), precision=highest) * score_scale
    masked = jnp.where(member[:, :, None], probe_scores[None], excluded)
    pooling = low(jax.nn.softmax(masked, axis=1) * member[:, :, None].astype(jnp.float32))
    pooled = jnp.einsum('ith,thd->ihd', pooling, final_heads, precision=highest)
    return low(pooled.reshape(IMG_DEV, D))

def total_loss(params, patches, heights, widths, labels, res_weights):
    layer_low = [low(weight) for weight in params[:6]]
    class_low = low(params[6])
    pack_count = heights.shape[0] * heights.shape[1] // IMG_DEV
    patch_packs = patches.reshape(pack_count, TOK_DEV, PIX)
    height_packs = heights.reshape(pack_count, IMG_DEV)
    width_packs = widths.reshape(pack_count, IMG_DEV)
    forward = jax.checkpoint(pack_forward)

    def one_pack(running, pack):
        return (running, forward(layer_low, pack[0], pack[1], pack[2]))
    unused, pooled = lax.scan(one_pack, jnp.zeros((), jnp.float32), (patch_packs, height_packs, width_packs))
    logits = low_back(jnp.dot(pooled.reshape(-1, D), class_low, precision=highest))
    label_hit = labels.reshape(-1)[:, None] == jnp.arange(CLASSES, dtype=jnp.int32)[None, :]
    picked = lax.optimization_barrier(jnp.sum(jnp.where(label_hit, logits, 0.0), axis=1))
    losses = jax.nn.logsumexp(logits, axis=1) - picked
    image_weights = res_weights.reshape(-1).astype(jnp.float32)
    weight_sum = jnp.sum(image_weights)
    loss_sum = jnp.sum(image_weights * losses)
    return (loss_sum / weight_sum, (loss_sum, weight_sum))

def lamb_update(weight, gradient, moment_one, moment_two, factor):
    gradient = gradient * factor
    moment_one = beta_first * moment_one + (1.0 - beta_first) * gradient
    moment_two = beta_second * moment_two + (1.0 - beta_second) * gradient * gradient
    update = moment_one / (1.0 - beta_first ** STEP) / (jnp.sqrt(moment_two / (1.0 - beta_second ** STEP)) + adam_floor) + weight_decay * weight
    return (moment_one, moment_two, update)

def reference(patches, heights, widths, labels, res_weights, w_embed, w_qkv, w_out, w_up, w_down, vectors, w_cls, m_embed, v_embed, m_qkv, v_qkv, m_out, v_out, m_up, v_up, m_down, v_down, m_vectors, v_vectors, m_cls, v_cls):
    params = [w_embed, w_qkv, w_out, w_up, w_down, vectors, w_cls]
    moments = [(m_embed, v_embed), (m_qkv, v_qkv), (m_out, v_out), (m_up, v_up), (m_down, v_down), (m_vectors, v_vectors), (m_cls, v_cls)]
    patch_values = patches.astype(jnp.float32)

    def loss_of(weights):
        return total_loss(weights, patch_values, heights, widths, labels, res_weights)
    loss_value, pullback, loss_parts = jax.vjp(loss_of, params, has_aux=True)
    gradients = pullback(jnp.ones((), jnp.float32))[0]
    squares = jnp.stack([jnp.sum(gradient * gradient) for gradient in gradients])
    clip_norm = jnp.sqrt(jnp.sum(squares))
    factor = jnp.minimum(1.0, clip_limit / clip_norm)
    outputs = []
    matrix_rows = []
    vector_rows = None
    for position in range(7):
        moment_one, moment_two, update = lamb_update(params[position], gradients[position], moments[position][0], moments[position][1], factor)
        if position == 5:
            weight_norm = jnp.sqrt(lax.optimization_barrier(jnp.sum(params[5] * params[5], axis=1, keepdims=True)))
            update_norm = jnp.sqrt(lax.optimization_barrier(jnp.sum(update * update, axis=1, keepdims=True)))
            vector_rows = jnp.concatenate([weight_norm, update_norm], axis=1)
        else:
            weight_norm = jnp.sqrt(jnp.sum(params[position] * params[position]))
            update_norm = jnp.sqrt(jnp.sum(update * update))
            matrix_rows.append(jnp.stack([weight_norm, update_norm]))
        new_weight = params[position] - learn_rate * (weight_norm / update_norm) * update
        outputs += [new_weight, moment_one, moment_two]
    norms = jnp.concatenate([jnp.stack(matrix_rows), vector_rows], axis=0)
    loss_terms = jnp.stack([loss_parts[0], loss_parts[1]])
    return tuple([loss_terms, clip_norm, norms] + outputs)
```

```python
import functools

import jax
import jax.numpy as jnp
from jax import lax
from jax.experimental import pallas as pl
from jax.experimental.pallas import tpu as pltpu
from jax.sharding import PartitionSpec as P

HEAD = 64
POS = 128
STEP = 10


epsilon = 1e-06
clip_limit = 0.01
learn_rate = 0.3
beta_first = 0.9
beta_second = 0.999
weight_decay = 0.01
adam_floor = 1e-08
highest = lax.Precision.HIGHEST
excluded = -1e30


def merged_2(part, axis, combine):
    gathered = jax.tree.map(lambda a: lax.all_gather(a, axis), part)

    def take(source):
        return jax.tree.map(lambda a: lax.dynamic_index_in_dim(a, source, 0, False), gathered)

    return lax.fori_loop(
        1, lax.axis_size(axis), lambda source, state: combine(state, take(source)), take(0)
    )


def layer_norm(values, scales):
    center = values - jnp.mean(values, axis=-1, keepdims=True)
    spread = jnp.mean(center * center, axis=-1, keepdims=True)
    return center * lax.rsqrt(spread + epsilon) * scales


def norm_back(values, scales, upstream):
    result, pullback = jax.vjp(layer_norm, values, scales)
    return pullback(upstream)


def outer_dot(left, right):
    return lax.dot_general(
        left, right, (((0,), (0,)), ((), ())), preferred_element_type=jnp.float32
    )


def inner_dot(left, right):
    return lax.dot_general(
        left, right, (((1,), (1,)), ((), ())), preferred_element_type=jnp.float32
    )


def layout(heights, widths, row_count):
    lengths = heights * widths
    image_ends = jnp.cumsum(lengths)
    starts = image_ends - lengths
    places = jnp.arange(row_count, dtype=jnp.int32)
    slot_ids = jnp.arange(heights.shape[0], dtype=jnp.int32)
    segment = jnp.sum((places[:, None] >= image_ends[None, :]).astype(jnp.int32), axis=1)
    member = segment[None, :] == slot_ids[:, None]
    member_int = member.T.astype(jnp.int32)
    within = places - jnp.sum(member_int * starts[None, :], axis=1)
    across = jnp.maximum(jnp.sum(member_int * widths[None, :], axis=1), 1)
    upright = jnp.maximum(jnp.sum(member_int * heights[None, :], axis=1), 1)
    col_pos = within % across * POS // across
    row_pos = within // across * POS // upright
    pos_table = jnp.arange(POS, dtype=jnp.int32)
    pos_rows = jnp.concatenate(
        [col_pos[:, None] == pos_table[None, :], row_pos[:, None] == pos_table[None, :]], axis=1
    )
    return (segment, member, pos_rows)


def block_scores(queries, key_rows, segment):
    scores = jnp.einsum(
        "thd,shd->hts", queries, key_rows, preferred_element_type=jnp.float32
    ) * HEAD ** (-0.5)
    same_image = segment[:, None] == segment[None, :]
    return (queries, jnp.where(same_image[None], scores, excluded))


def attend(queries, key_rows, value_rows, segment):
    query_block, scores = block_scores(queries, key_rows, segment)
    top_score = jnp.max(scores, axis=-1, keepdims=True)
    exp_scores = jnp.exp(scores - top_score)
    exp_total = jnp.sum(exp_scores, axis=-1, keepdims=True)
    attention = (exp_scores / exp_total).astype(jnp.bfloat16)
    result = jnp.einsum("hts,shd->thd", attention, value_rows, preferred_element_type=jnp.float32)
    return (result.astype(jnp.bfloat16), (top_score + jnp.log(exp_total))[..., 0])


def attend_back(queries, key_rows, value_rows, segment, log_total, mixed_grad):
    query_block, scores = block_scores(queries, key_rows, segment)
    attention = jnp.exp(scores - log_total[..., None])
    value_grad = jnp.einsum(
        "hts,thd->shd",
        attention.astype(jnp.bfloat16),
        mixed_grad,
        preferred_element_type=jnp.float32,
    )
    prob_grad = jnp.einsum(
        "thd,shd->hts", mixed_grad, value_rows, preferred_element_type=jnp.float32
    )
    score_grad = (
        attention * (prob_grad - jnp.sum(attention * prob_grad, axis=-1, keepdims=True))
    ).astype(jnp.bfloat16)
    query_grad = jnp.einsum(
        "hts,shd->thd", score_grad, key_rows, preferred_element_type=jnp.float32
    ) * HEAD ** (-0.5)
    key_grad = jnp.einsum(
        "hts,thd->shd", score_grad, query_block, preferred_element_type=jnp.float32
    ) * HEAD ** (-0.5)
    return (query_grad, key_grad, value_grad)


def layer_forward(weights_low, vector_low, patch_rows, heights, widths):
    embed, joined_w, out_w, up_w, down_w = weights_low
    vectors = vector_low.astype(jnp.float32)
    row_count, pixel_count = patch_rows.shape
    model_width = embed.shape[1]
    head_count = model_width // HEAD
    head_shape = (row_count, head_count, HEAD)
    segment, member, pos_rows = layout(heights, widths, row_count)
    pos_low = pos_rows.astype(jnp.bfloat16)
    embedded = jnp.dot(
        patch_rows, embed[:pixel_count], preferred_element_type=jnp.float32
    ) + jnp.dot(pos_low, embed[pixel_count:], preferred_element_type=jnp.float32)
    normed = layer_norm(embedded, vectors[0]).astype(jnp.bfloat16)
    joined = jnp.dot(normed, joined_w, preferred_element_type=jnp.float32)
    query_pre = joined[:, :model_width].reshape(head_shape)
    key_pre = joined[:, model_width : 2 * model_width].reshape(head_shape)
    queries = layer_norm(query_pre, vectors[3].reshape(head_count, HEAD)).astype(jnp.bfloat16)
    key_rows = layer_norm(key_pre, vectors[4].reshape(head_count, HEAD)).astype(jnp.bfloat16)
    value_rows = joined[:, 2 * model_width :].reshape(head_shape).astype(jnp.bfloat16)
    mixed_heads, log_total = attend(queries, key_rows, value_rows, segment)
    mixed_flat = mixed_heads.reshape(row_count, model_width)
    second = embedded + jnp.dot(mixed_flat, out_w, preferred_element_type=jnp.float32)
    hidden = layer_norm(second, vectors[1]).astype(jnp.bfloat16)
    upward = jnp.dot(hidden, up_w, preferred_element_type=jnp.float32)
    active = jax.nn.gelu(upward).astype(jnp.bfloat16)
    residual = second + jnp.dot(active, down_w, preferred_element_type=jnp.float32)
    final_heads = layer_norm(residual, vectors[2]).astype(jnp.bfloat16).reshape(head_shape)
    probe_low = vector_low[5].reshape(head_count, HEAD)
    probe_scores = jnp.einsum(
        "thd,hd->th", final_heads, probe_low, preferred_element_type=jnp.float32
    ) * HEAD ** (-0.5)
    masked = jnp.where(member[:, :, None], probe_scores[None], excluded)
    pooling = jax.nn.softmax(masked, axis=1) * member[:, :, None].astype(jnp.float32)
    pool_low = pooling.astype(jnp.bfloat16)
    pooled = jnp.einsum("ith,thd->ihd", pool_low, final_heads, preferred_element_type=jnp.float32)
    saved = (
        patch_rows,
        pos_low,
        member,
        segment,
        embedded,
        normed,
        query_pre,
        key_pre,
        queries,
        key_rows,
        value_rows,
        log_total,
        mixed_flat,
        second,
        hidden,
        upward,
        active,
        residual,
        final_heads,
        pooling,
        pool_low,
    )
    return (pooled.reshape(-1, model_width).astype(jnp.bfloat16), saved)


def layer_backward(weights_low, vector_low, saved, pooled_grad):
    (
        patch_rows,
        pos_low,
        member,
        segment,
        embedded,
        normed,
        query_pre,
        key_pre,
        queries,
        key_rows,
        value_rows,
        log_total,
        mixed_flat,
        second,
        hidden,
        upward,
        active,
        residual,
        final_heads,
        pooling,
        pool_low,
    ) = saved
    embed, joined_w, out_w, up_w, down_w = weights_low
    vectors = vector_low.astype(jnp.float32)
    row_count, head_count = (final_heads.shape[0], final_heads.shape[1])
    model_width = head_count * HEAD
    image_grad = pooled_grad.reshape(-1, head_count, HEAD)
    final_wide = final_heads.astype(jnp.float32)
    weight_grad = jnp.einsum("ihd,thd->ith", image_grad, final_wide, precision=highest) * member[
        :, :, None
    ].astype(jnp.float32)
    score_grad = pooling * (weight_grad - jnp.sum(pooling * weight_grad, axis=1, keepdims=True))
    score_grad = jnp.sum(score_grad, axis=0) * HEAD ** (-0.5)
    probe = vectors[5].reshape(head_count, HEAD)
    final_grad = (
        jnp.einsum("ith,ihd->thd", pool_low.astype(jnp.float32), image_grad, precision=highest)
        + score_grad[:, :, None] * probe[None]
    )
    probe_grad = jnp.einsum("th,thd->hd", score_grad, final_wide, precision=highest)
    residual_grad, gain_final = norm_back(
        residual, vectors[2], final_grad.reshape(row_count, model_width)
    )
    down_in = residual_grad.astype(jnp.bfloat16)
    active_grad = inner_dot(down_in, down_w)
    upward_grad = jax.vjp(jax.nn.gelu, upward)[1](active_grad)[0].astype(jnp.bfloat16)
    second_back, gain_second = norm_back(second, vectors[1], inner_dot(upward_grad, up_w))
    second_grad = residual_grad + second_back
    out_in = second_grad.astype(jnp.bfloat16)
    mixed_grad = inner_dot(out_in, out_w).astype(jnp.bfloat16).reshape(row_count, head_count, HEAD)
    query_grad, key_grad, value_grad = attend_back(
        queries, key_rows, value_rows, segment, log_total, mixed_grad
    )
    query_back, gain_query = norm_back(query_pre, vectors[3].reshape(head_count, HEAD), query_grad)
    key_back, gain_key = norm_back(key_pre, vectors[4].reshape(head_count, HEAD), key_grad)
    joined_grad = jnp.concatenate(
        [
            query_back.reshape(row_count, model_width),
            key_back.reshape(row_count, model_width),
            value_grad.reshape(row_count, model_width),
        ],
        axis=1,
    ).astype(jnp.bfloat16)
    first_back, gain_first = norm_back(embedded, vectors[0], inner_dot(joined_grad, joined_w))
    embed_in = (second_grad + first_back).astype(jnp.bfloat16)
    inputs = jnp.concatenate([patch_rows, pos_low], axis=1)
    vector_grad = jnp.stack(
        [
            gain_first,
            gain_second,
            gain_final,
            gain_query.reshape(model_width),
            gain_key.reshape(model_width),
            probe_grad.reshape(model_width),
        ]
    )
    pairs = (
        (inputs, embed_in),
        (normed, joined_grad),
        (mixed_flat, out_in),
        (hidden, upward_grad),
        (active, down_in),
    )
    return (pairs, vector_grad)


def reduce_grads(fresh):
    return (
        lax.psum_scatter(fresh[0], ("dp", "mp"), scatter_dimension=0, tiled=True),
        lax.psum_scatter(fresh[1], ("dp", "mp"), scatter_dimension=0, tiled=True),
        lax.psum_scatter(fresh[2], ("dp", "mp"), scatter_dimension=0, tiled=True),
        lax.psum_scatter(fresh[3], ("dp", "mp"), scatter_dimension=0, tiled=True),
        lax.psum_scatter(fresh[4], ("dp", "mp"), scatter_dimension=0, tiled=True),
        lax.psum_scatter(fresh[5], ("dp", "mp"), scatter_dimension=1, tiled=True),
    )


def combine_stats(earlier, later_one):
    top_score = jnp.maximum(earlier[0], later_one[0])
    exp_total = earlier[1] * jnp.exp(earlier[0] - top_score) + later_one[1] * jnp.exp(
        later_one[0] - top_score
    )
    return (top_score, exp_total, earlier[2] + later_one[2])


def lamb_update(weight, gradient, moment_one, moment_two, factor):
    gradient = gradient * factor
    moment_one = beta_first * moment_one + (1.0 - beta_first) * gradient
    moment_two = beta_second * moment_two + (1.0 - beta_second) * gradient * gradient
    update = (
        moment_one
        / (1.0 - beta_first**STEP)
        / (jnp.sqrt(moment_two / (1.0 - beta_second**STEP)) + adam_floor)
        + weight_decay * weight
    )
    return (moment_one, moment_two, update)


def body(
    patches,
    heights,
    widths,
    labels,
    res_weights,
    w_embed,
    w_qkv,
    w_out,
    w_up,
    w_down,
    vectors,
    w_cls,
    m_embed,
    v_embed,
    m_qkv,
    v_qkv,
    m_out,
    v_out,
    m_up,
    v_up,
    m_down,
    v_down,
    m_vectors,
    v_vectors,
    m_cls,
    v_cls,
):
    gathered = (
        lax.all_gather(w_embed.astype(jnp.bfloat16), ("dp", "mp"), axis=0, tiled=True),
        lax.all_gather(w_qkv.astype(jnp.bfloat16), ("dp", "mp"), axis=0, tiled=True),
        lax.all_gather(w_out.astype(jnp.bfloat16), ("dp", "mp"), axis=0, tiled=True),
        lax.all_gather(w_up.astype(jnp.bfloat16), ("dp", "mp"), axis=0, tiled=True),
        lax.all_gather(w_down.astype(jnp.bfloat16), ("dp", "mp"), axis=0, tiled=True),
        lax.all_gather(vectors.astype(jnp.bfloat16), ("dp", "mp"), axis=1, tiled=True),
    )
    weights_low = gathered[:5]
    vector_low = gathered[5]
    class_low = lax.all_gather(w_cls.astype(jnp.bfloat16), "dp", axis=0, tiled=True)
    member_index = lax.axis_index("mp")
    slot_count = heights.shape[1]
    own_start = member_index * slot_count
    own_weights = lax.dynamic_slice_in_dim(res_weights, own_start, slot_count, 1).astype(
        jnp.float32
    )
    weight_sum = lax.psum(jnp.sum(own_weights), ("dp", "mp"))
    class_count = class_low.shape[1]
    class_ids = member_index * class_count + jnp.arange(class_count, dtype=jnp.int32)
    loss_local = jnp.zeros((), jnp.float32)
    class_grad = jnp.zeros(class_low.shape, jnp.float32)
    summed = None
    for micro_index in range(patches.shape[0]):
        pooled, saved = layer_forward(
            weights_low, vector_low, patches[micro_index], heights[micro_index], widths[micro_index]
        )
        group_rows = lax.all_gather(pooled, "mp", axis=0, tiled=True)
        logits = jnp.dot(group_rows, class_low, preferred_element_type=jnp.float32)
        label_hit = labels[micro_index][:, None] == class_ids[None, :]
        top_score = jnp.max(logits, axis=1)
        exp_total = jnp.sum(jnp.exp(logits - top_score[:, None]), axis=1)
        picked = jnp.sum(jnp.where(label_hit, logits, 0.0), axis=1)
        merged = merged_2((top_score, exp_total, picked), "mp", combine_stats)
        log_total = merged[0] + jnp.log(merged[1])
        group_weights = res_weights[micro_index].astype(jnp.float32)
        weighted = group_weights * (log_total - merged[2])
        loss_local = loss_local + jnp.sum(
            lax.dynamic_slice_in_dim(weighted, own_start, slot_count, 0)
        )
        logit_grad = (
            (jnp.exp(logits - log_total[:, None]) - label_hit.astype(jnp.float32))
            * (group_weights / weight_sum)[:, None]
        ).astype(jnp.bfloat16)
        class_grad = class_grad + outer_dot(group_rows, logit_grad)
        pooled_grad = lax.psum_scatter(
            inner_dot(logit_grad, class_low), "mp", scatter_dimension=0, tiled=True
        )
        pairs, vector_grad = layer_backward(weights_low, vector_low, saved, pooled_grad)
        fresh = tuple(outer_dot(left, right) for left, right in pairs) + (vector_grad,)
        summed = fresh if summed is None else jax.tree.map(jnp.add, summed, fresh)
    summed = reduce_grads(summed)
    class_shard = lax.psum_scatter(class_grad, "dp", scatter_dimension=0, tiled=True)
    params = (w_embed, w_qkv, w_out, w_up, w_down, vectors, w_cls)
    moments = (
        (m_embed, v_embed),
        (m_qkv, v_qkv),
        (m_out, v_out),
        (m_up, v_up),
        (m_down, v_down),
        (m_vectors, v_vectors),
        (m_cls, v_cls),
    )
    gradients = (summed[0], summed[1], summed[2], summed[3], summed[4], summed[5], class_shard)
    matrix_order = (0, 1, 2, 3, 4, 6)
    grad_squares = jnp.concatenate(
        [
            jnp.stack(
                [jnp.sum(gradients[position] * gradients[position]) for position in matrix_order]
            ),
            jnp.sum(gradients[5] * gradients[5], axis=1),
        ]
    )
    square_sums, loss_total = lax.psum((grad_squares, loss_local), ("dp", "mp"))
    clip_norm = jnp.sqrt(jnp.sum(square_sums))
    factor = jnp.minimum(1.0, clip_limit / clip_norm)
    updated = [
        lamb_update(
            params[position],
            gradients[position],
            moments[position][0],
            moments[position][1],
            factor,
        )
        for position in range(7)
    ]
    matrix_parts = jnp.stack(
        [
            jnp.stack(
                [
                    jnp.sum(params[position] * params[position]),
                    jnp.sum(updated[position][2] * updated[position][2]),
                ]
            )
            for position in matrix_order
        ]
    )
    vector_parts = jnp.stack(
        [jnp.sum(params[5] * params[5], axis=1), jnp.sum(updated[5][2] * updated[5][2], axis=1)],
        axis=1,
    )
    norms = jnp.sqrt(lax.psum(jnp.concatenate([matrix_parts, vector_parts], axis=0), ("dp", "mp")))
    ratios = norms[:, 0] / norms[:, 1]
    outputs = [jnp.stack([loss_total, weight_sum]), clip_norm, norms]
    for position in range(7):
        if position == 5:
            ratio = ratios[6:][:, None]
        else:
            ratio = ratios[matrix_order.index(position)]
        moment_one, moment_two, update = updated[position]
        outputs += [params[position] - learn_rate * ratio * update, moment_one, moment_two]
    return tuple(outputs)


MESH_ID = pl.DeviceIdType.MESH
CORES = 2
ALL = slice(None)
LOW = jnp.bfloat16
FULL = jnp.float32


class Place:
    def __init__(self, dims):
        self.sizes = dict(dims, c=CORES)
        dp, mp = lax.axis_index("dp"), lax.axis_index("mp")
        wide = self.sizes["y"]
        self.at = {"z": dp // wide, "y": dp % wide, "x": mp // CORES, "c": mp % CORES}

    def peer(self, axis, step):
        at = dict(self.at)
        at[axis] = self.source(axis, -step)
        return (at["z"] * self.sizes["y"] + at["y"], at["x"] * CORES + at["c"])

    def source(self, axis, step):
        size = self.sizes[axis]
        return (self.at[axis] + (size - step) % size) % size

    def steps(self, axis):
        return range(1, self.sizes[axis])

    def greet(self):
        barrier = pltpu.get_barrier_semaphore()
        count = 0
        for axis in "cxyz":
            for step in self.steps(axis):
                pl.semaphore_signal(
                    barrier, inc=1, device_id=self.peer(axis, step), device_id_type=MESH_ID
                )
                count += 1
        pl.semaphore_wait(barrier, count)


class Courier:
    def __init__(self, place, send, recv):
        self.place, self.send, self.recv, self.sent = place, send, recv, []

    def start(self, axis, step, source, target):
        slot = len(self.sent)
        copy = pltpu.make_async_remote_copy(
            src_ref=source,
            dst_ref=target,
            send_sem=self.send.at[slot],
            recv_sem=self.recv.at[slot],
            device_id=self.place.peer(axis, step),
            device_id_type=MESH_ID,
        )
        copy.start()
        self.sent.append(copy)
        return copy

    def finish(self):
        for copy in self.sent:
            copy.wait_send()


class Spread:
    def __init__(self, courier, view, order):
        self.courier, self.place, self.view, self.order = courier, courier.place, view, order
        self.relayed = []

    def part(self, stage, **fixed):
        where = {axis: self.place.at[axis] for axis in "xyz"}
        for axis in ("z" + self.order)[:stage]:
            where[axis] = ALL
        where.update(fixed)
        return self.view(**where)

    def send(self, axis, stage):
        part = self.part(stage)
        return [self.courier.start(axis, step, part, part) for step in self.place.steps(axis)]

    def relay(self, part):
        self.relayed.append(self.courier.start("c", 1, part, part))

    def begin(self):
        self.coming = self.send("z", 0)

    def middle(self, stage):
        for copy in self.coming:
            copy.wait_recv()
        if stage == 1:
            self.relay(self.part(1))
        else:
            axis = self.order[stage - 2]
            for step in self.place.steps(axis):
                self.relay(self.part(stage - 1, **{axis: self.place.source(axis, step)}))
        self.coming = self.send(self.order[stage - 1], stage) if stage < 3 else []

    def done(self):
        for copy in self.relayed:
            copy.wait_recv()


class Fold:
    def __init__(self, courier, view, order, stage_refs, axes):
        self.courier, self.place, self.view, self.order = courier, courier.place, view, order
        self.held, self.first, self.second, self.third = stage_refs
        self.axes = axes

    def key(self, **fixed):
        return tuple(fixed.get(axis, ALL) for axis in self.axes)

    def begin(self):
        place = self.place
        self.coming = [self.courier.start("c", 1, self.view(1 - place.at["c"]), self.held)]

    def landed(self):
        for copy in self.coming:
            copy.wait_recv()

    def send(self, axis, target, **fixed):
        place = self.place
        self.coming = [
            self.courier.start(
                axis,
                step,
                self.held.at[self.key(**{axis: place.source(axis, -step)}, **fixed)],
                target.at[step - 1],
            )
            for step in place.steps(axis)
        ]

    def between_cores(self):
        self.landed()
        mine = self.view(self.place.at["c"])
        held = self.held
        count = held.shape[0]

        def one(lead, carry):
            held[lead] = (mine[lead].astype(FULL) + held[lead].astype(FULL)).astype(LOW)
            return carry

        lax.fori_loop(0, count, one, 0)
        self.send(self.order[0], self.first)

    def along_first(self):
        self.landed()
        axis = self.order[0]
        here = self.held.at[self.key(**{axis: self.place.at[axis]})]
        came = self.first

        def one(lead, carry):
            total = here[lead].astype(FULL)
            for step in range(came.shape[0]):
                total = total + came[step, lead].astype(FULL)
            here[lead] = total.astype(LOW)
            return carry

        lax.fori_loop(0, here.shape[0], one, 0)
        self.send(self.order[1], self.second, **{axis: self.place.at[axis]})

    def along_second(self):
        self.landed()
        place = self.place
        here = self.held.at[self.key(x=place.at["x"], y=place.at["y"])]
        came = self.second

        def one(lead, carry):
            total = here[lead].astype(FULL)
            for step in range(came.shape[0]):
                total = total + came[step, lead].astype(FULL)
            here[lead] = total.astype(LOW)
            return carry

        lax.fori_loop(0, here.shape[0], one, 0)
        self.send("z", self.third, x=place.at["x"], y=place.at["y"])

    def along_z(self):
        self.landed()
        place = self.place
        total = self.held[self.key(x=place.at["x"], y=place.at["y"], z=place.at["z"])].astype(FULL)
        for step in range(self.third.shape[0]):
            total = total + self.third[step].astype(FULL)
        return total


class Total:
    def __init__(self, courier, slots):
        self.courier, self.place, self.slots = courier, courier.place, slots
        self.axes = list("cxyz")

    def begin(self, block):
        self.send("c", block)

    def send(self, axis, block):
        place, slots = self.place, self.slots["cxyz".index(axis)]
        mine = slots.at[place.at[axis]]
        mine[...] = block
        self.coming = [self.courier.start(axis, step, mine, mine) for step in place.steps(axis)]

    def sum(self, axis):
        for copy in self.coming:
            copy.wait_recv()
        slots = self.slots["cxyz".index(axis)]
        total = slots[0]
        for index in range(1, slots.shape[0]):
            total = total + slots[index]
        return total

    def advance(self, axis):
        following = "cxyz".index(axis) + 1
        total = self.sum(axis)
        if following < 4:
            self.send("cxyz"[following], total)
        return total

    def through(self, block):
        self.begin(block)
        for axis in "cxyz":
            total = self.advance(axis)
        return total


def total_slots(dims, shape):
    sizes = dict(dims, c=CORES)
    return [pltpu.VMEM((sizes[axis],) + shape, FULL) for axis in "cxyz"]


def cut(rows, width, parts):
    if rows % (16 * parts) == 0:
        size = rows // parts
        return [((part * size, size), (0, width)) for part in range(parts)]
    units = width // 128
    marks = [units * part // parts * 128 for part in range(parts + 1)]
    return [((0, rows), (low, high - low)) for low, high in zip(marks, marks[1:]) if high > low]


def pieces_of(blocks, class_block):
    found = []
    turn = 0
    for index, (rows, width) in enumerate(blocks + [class_block]):
        parts = max(2, min(4, rows * width * 2 // 32768 // 2 * 2))
        for row_range, column_range in cut(rows, width, parts):
            found.append((index, row_range, column_range, ("xy", "yx")[turn % 2]))
            turn += 1
    return found


def block_ref(ref, class_ref, place, piece, core):
    index, rows, columns, _ = piece

    def of_matrix(z, y, x):
        half = ref.shape[-1] // CORES
        across = pl.ds(pl.multiple_of(core * half + columns[0], 128), columns[1])
        return ref.at[z, y, x, pl.ds(rows[0], rows[1]), across]

    def of_classes(z, y, x):
        return class_ref.at[x, core, z, y, pl.ds(rows[0], rows[1])]

    return of_matrix if ref is not None else of_classes


def gather_kernel(dims, pieces, *refs):
    shards, (vectors, weights, w_cls), refs = refs[:5], refs[5:8], refs[8:]
    full, (g_cls, g_vec), refs = refs[:5], refs[5:7], refs[7:]
    pairs, (send, recv) = refs[:5], refs[5:]
    place = Place(dims)
    place.greet()
    courier = Courier(place, send, recv)
    z, y, x, core = (place.at[axis] for axis in "zyxc")
    arriving = []
    for shard, pair in zip(shards, pairs):
        rows, half = shard.shape[0], shard.shape[1] // CORES
        at = pl.ds(pl.multiple_of(core * rows, 8), rows)
        other = pl.ds(pl.multiple_of((1 - core) * half, 128), half)
        arriving.append(courier.start("c", 1, shard.at[:, other], pair.at[at]))
        pair[at] = shard[:, pl.ds(pl.multiple_of(core * half, 128), half)]
    small = jnp.zeros((8, 128), FULL)
    g_vec[z, y, x, core] = small
    count = vectors.shape[1]
    g_vec[z, y, x, core, pl.ds(0, 6), pl.ds(0, count)] = vectors[...].astype(LOW).astype(FULL)
    width = weights.shape[1]
    slots = width // (dims["x"] * CORES)
    own = (x * CORES + core) * slots
    lanes = lax.broadcasted_iota(jnp.int32, weights.shape, 1)
    inside = (lanes >= own) & (lanes < own + slots)
    counted = jnp.sum(jnp.where(inside, weights[...], 0).astype(FULL), axis=0, keepdims=True)
    g_vec[z, y, x, core, pl.ds(6, 1), pl.ds(0, width)] = counted
    block = g_cls.at[x, core, z, y]
    block[...] = jnp.zeros(block.shape, LOW)
    block[:, pl.ds(0, w_cls.shape[1])] = w_cls[...].astype(LOW)
    spreads = [Spread(courier, lambda z, y, x: g_vec.at[z, y, x, core], "xy")]
    first_of = {}
    for piece in pieces:
        index = piece[0]
        if index < 5:
            first_of.setdefault(index, len(spreads))
        view = block_ref(full[index] if index < 5 else None, g_cls, place, piece, core)
        spreads.append(Spread(courier, view, piece[3]))
    ready = {position: index for index, position in first_of.items()}

    def begin(position):
        if position in ready:
            index = ready[position]
            arriving[index].wait_recv()
            half = pairs[index].shape[1]
            across = pl.ds(pl.multiple_of(core * half, 128), half)
            full[index][z, y, x, :, across] = pairs[index][...].astype(LOW)
        spreads[position].begin()

    count = len(spreads)
    steps = ((-2, begin), (0, lambda i: spreads[i].middle(1)), (2, lambda i: spreads[i].middle(2)))
    steps += ((4, lambda i: spreads[i].middle(3)), (6, lambda i: spreads[i].done()))
    for turn in range(-2, count + 6):
        for lag, action in steps:
            if 0 <= turn - lag < count:
                action(turn - lag)
    courier.finish()


def copies_per_piece(dims):
    X, Y, Z = (dims[axis] for axis in "xyz")
    return (Z - 1) + 2 * (X - 1) + 2 * (Y - 1) + 1


def gather_weights(dims, mats, vectors, weights, w_cls):
    X, Y, Z = (dims[axis] for axis in "xyz")
    blocks = [(CORES * w.shape[0], w.shape[1] // CORES) for w in mats]
    padded = -(-w_cls.shape[1] // 128) * 128
    pieces = pieces_of(blocks, (w_cls.shape[0], padded))
    outs = [jax.ShapeDtypeStruct((Z, Y, X, CORES * w.shape[0], w.shape[1]), LOW) for w in mats]
    outs.append(jax.ShapeDtypeStruct((X, CORES, Z, Y, w_cls.shape[0], padded), LOW))
    outs.append(jax.ShapeDtypeStruct((Z, Y, X, CORES, 8, 128), FULL))
    count = 5 + (1 + len(pieces)) * copies_per_piece(dims)
    scratch = [pltpu.VMEM(block, FULL) for block in blocks]
    scratch += [pltpu.SemaphoreType.DMA((count,)), pltpu.SemaphoreType.DMA((count,))]
    whole = pl.BlockSpec(memory_space=pltpu.VMEM)
    return pl.pallas_call(
        functools.partial(gather_kernel, dims, pieces),
        out_shape=outs,
        in_specs=[whole] * 8,
        out_specs=[whole] * 7,
        scratch_shapes=scratch,
        compiler_params=pltpu.CompilerParams(
            collective_id=0, has_side_effects=True, vmem_limit_bytes=60 << 20
        ),
    )(*mats, vectors, weights, w_cls)


def squares(values):
    rows, width = values.shape
    total = jnp.zeros((1, 128), FULL)
    whole = width // 128 * 128
    for low in range(0, whole, 128):
        part = values[:, low : low + 128]
        total = total + jnp.sum(part * part, axis=0, keepdims=True)
    if whole < width:
        part = values[:, whole:]
        rest = jnp.sum(part * part, axis=0, keepdims=True)
        total = total + jnp.concatenate([rest, jnp.zeros((1, 128 - rest.shape[1]), FULL)], axis=1)
    return total


def wide_rows(values):
    squared = values * values
    return jnp.concatenate([squared, jnp.zeros((squared.shape[0], 128 - squared.shape[1]), FULL)], axis=1)


def moments_step(gradient, moment_one, moment_two):
    first = beta_first * moment_one + (1.0 - beta_first) * gradient
    second = beta_second * moment_two + (1.0 - beta_second) * gradient * gradient
    return first, second


def update_of(first, second, weight):
    return (
        first
        / (1.0 - beta_first**STEP)
        / (jnp.sqrt(second / (1.0 - beta_second**STEP)) + adam_floor)
        + weight_decay * weight
    )


def step_kernel(dims, pieces, *refs):
    grads, (g_cls, g_vec), refs = refs[:5], refs[5:7], refs[7:]
    params, moments, refs = refs[:7], refs[7:21], refs[21:]
    (loss_out, clip_out, norm_out), outs, refs = refs[:3], refs[3:24], refs[24:]
    shards, wholes, refs = refs[:7], refs[7:12], refs[12:]
    updates, refs = refs[:7], refs[7:]
    slots_vec, slots_one, slots_two, refs = refs[:4], refs[4:8], refs[8:12], refs[12:]
    (send, recv), stage_refs = refs[:2], refs[2:]
    place = Place(dims)
    place.greet()
    courier = Courier(place, send, recv)
    z, y, x, core = (place.at[axis] for axis in "zyxc")
    folds = []
    for position, piece in enumerate(pieces):
        index = piece[0]
        ref = grads[index] if index < 5 else None

        def view(core, piece=piece, ref=ref):
            return block_ref(ref, g_cls, place, piece, core)(ALL, ALL, ALL)

        axes = "zyx" if index < 5 else "xzy"
        folds.append(Fold(courier, view, piece[3], stage_refs[4 * position : 4 * position + 4], axes))
    left = {index: sum(piece[0] == index for piece in pieces) for index in range(6)}
    closing = {}

    def finish(position):
        index, rows, columns, _ = pieces[position]
        total = folds[position].along_z()
        if index == 5:
            own = shards[6]
            own[pl.ds(rows[0], rows[1])] = total[:, : own.shape[1]]
            return
        whole, own = wholes[index], shards[index]
        whole[pl.ds(rows[0], rows[1]), pl.ds(columns[0], columns[1])] = total
        left[index] -= 1
        if left[index] == 0:
            count, half = own.shape[0], own.shape[1] // CORES
            across = pl.ds(pl.multiple_of(core * half, 128), half)
            other = whole.at[pl.ds(pl.multiple_of((1 - core) * count, 8), count)]
            closing[index] = courier.start("c", 1, other, own.at[:, across])
            own[:, across] = whole[pl.ds(pl.multiple_of(core * count, 8), count)]

    vec_total = Total(courier, slots_vec)
    vec_total.begin(g_vec[...])
    count = len(folds)
    steps = ((-3, lambda i: folds[i].begin()), (0, lambda i: folds[i].between_cores()))
    steps += ((2, lambda i: folds[i].along_first()), (4, lambda i: folds[i].along_second()), (6, finish))
    for turn in range(-3, count + 6):
        for lag, action in steps:
            if 0 <= turn - lag < count:
                action(turn - lag)
    for axis in "cxyz":
        vec_sum = vec_total.advance(axis)
    for index in range(5):
        closing[index].wait_recv()
    vec_count = params[5].shape[1]
    own = ((z * dims["y"] + y) * dims["x"] + x) * CORES + core
    at_row = lax.broadcasted_iota(jnp.int32, (vec_sum.shape[1], 128), 0)
    at_lane = lax.broadcasted_iota(jnp.int32, (vec_sum.shape[1], 128), 1)
    chosen = ((at_row == own * vec_count + at_lane) & (at_lane < vec_count)).astype(FULL)
    picked = jnp.dot(vec_sum, chosen, precision=highest, preferred_element_type=FULL)
    shards[5][...] = picked[:6, :vec_count]
    mats = (0, 1, 2, 3, 4, 6)
    blank = jnp.zeros((6, 128), FULL)
    parts = [squares(shards[i][...]) for i in mats] + [squares(params[i][...]) for i in mats]
    block = jnp.concatenate(parts + [wide_rows(params[5][...]), blank], axis=0)
    block = Total(courier, slots_one).through(block)
    sums = jnp.sum(block, axis=1, keepdims=True)
    vec_squares = jnp.sum(vec_sum * vec_sum, axis=1, keepdims=True)
    loss_out[...] = vec_sum[6:7, :2]
    clip_norm = jnp.sqrt(
        jnp.sum(sums[:6], axis=0, keepdims=True) + jnp.sum(vec_squares[:6], axis=0, keepdims=True)
    )
    clip_out[...] = clip_norm
    factor = jnp.minimum(1.0, clip_limit / clip_norm)
    for index in range(7):
        weight = params[index][...]
        first, second = moments_step(
            shards[index][...] * factor, moments[2 * index][...], moments[2 * index + 1][...]
        )
        outs[3 * index + 1][...] = first
        outs[3 * index + 2][...] = second
        updates[index][...] = update_of(first, second, weight)
    parts = [squares(updates[i][...]) for i in mats]
    block = jnp.concatenate(parts + [wide_rows(updates[5][...]), jnp.zeros((4, 128), FULL)], axis=0)
    block = Total(courier, slots_two).through(block)
    grown = jnp.sqrt(jnp.sum(block, axis=1, keepdims=True))
    weight_norms = jnp.sqrt(sums[6:18])
    norm_out[:, 0:1] = weight_norms
    norm_out[:, 1:2] = grown[:12]
    ratios = weight_norms / grown[:12]
    for row, index in enumerate(mats):
        ratio = learn_rate * ratios[row : row + 1]
        outs[3 * index][...] = params[index][...] - ratio * updates[index][...]
    outs[15][...] = params[5][...] - learn_rate * ratios[6:12] * updates[5][...]
    courier.finish()


def take_step(dims, grads, g_cls, g_vec, params, moments):
    X, Y, Z = (dims[axis] for axis in "xyz")
    mats = params[:5]
    blocks = [(CORES * w.shape[0], w.shape[1] // CORES) for w in mats]
    class_block = g_cls.shape[-2:]
    pieces = pieces_of(blocks, class_block)
    pieces = [piece for index in (5, 4, 3, 2, 1, 0) for piece in pieces if piece[0] == index]
    outs = [jax.ShapeDtypeStruct((1, 2), FULL), jax.ShapeDtypeStruct((1, 1), FULL)]
    outs.append(jax.ShapeDtypeStruct((12, 2), FULL))
    for param in params:
        outs += [jax.ShapeDtypeStruct(param.shape, FULL)] * 3
    scratch = [pltpu.VMEM(param.shape, FULL) for param in params]
    scratch += [pltpu.VMEM(block, FULL) for block in blocks]
    scratch += [pltpu.VMEM(param.shape, FULL) for param in params]
    scratch += total_slots(dims, g_vec.shape) + total_slots(dims, (24, 128)) + total_slots(dims, (16, 128))
    count = 5 + 3 * (1 + X - 1 + Y - 1 + Z - 1) + len(pieces) * (1 + X - 1 + Y - 1 + Z - 1)
    scratch += [pltpu.SemaphoreType.DMA((count,)), pltpu.SemaphoreType.DMA((count,))]
    for index, rows, columns, order in pieces:
        piece = (rows[1], columns[1])
        axes = "zyx" if index < 5 else "xzy"

        def rest(dropped):
            return tuple(dims[axis] for axis in axes if axis not in dropped)

        one, two = order
        scratch += [
            pltpu.VMEM(rest("") + piece, LOW),
            pltpu.VMEM((dims[one] - 1,) + rest(one) + piece, LOW),
            pltpu.VMEM((dims[two] - 1,) + rest("xy") + piece, LOW),
            pltpu.VMEM((Z - 1,) + piece, LOW),
        ]
    whole = pl.BlockSpec(memory_space=pltpu.VMEM)
    return pl.pallas_call(
        functools.partial(step_kernel, dims, pieces),
        out_shape=outs,
        in_specs=[whole] * 28,
        out_specs=[whole] * 24,
        scratch_shapes=scratch,
        compiler_params=pltpu.CompilerParams(
            collective_id=1, has_side_effects=True, vmem_limit_bytes=60 << 20
        ),
    )(*grads, g_cls, g_vec, *params, *moments)

def fast_body(dims, patches, heights, widths, labels, res_weights, *params_moments):
    params, moments = params_moments[:7], params_moments[7:]
    mats, vectors, w_cls = params[:5], params[5], params[6]
    across, groups = dims["x"], dims["x"] * CORES
    count = dims["z"] * dims["y"] * groups
    *full, g_cls, g_vec = gather_weights(dims, mats, vectors, res_weights, w_cls)
    weights_low = tuple(g.reshape(-1, g.shape[-1]) for g in full)
    small = g_vec.reshape(count, 8, 128)
    vec_count = vectors.shape[1]
    vector_low = small[:, :6, :vec_count].transpose(1, 0, 2).reshape(6, -1).astype(LOW)
    weight_sum = jnp.sum(small[:, 6])
    classes, padded = w_cls.shape[1], g_cls.shape[-1]
    class_low = g_cls.reshape(groups, -1, padded).transpose(1, 0, 2).reshape(-1, groups * padded)
    slots = heights.shape[1]
    own_start = lax.axis_index("mp") * slots
    own_labels = lax.dynamic_slice_in_dim(labels, own_start, slots, 1).reshape(-1)
    own_weights = lax.dynamic_slice_in_dim(res_weights, own_start, slots, 1)
    own_weights = own_weights.astype(FULL).reshape(-1)
    columns = jnp.arange(groups * padded, dtype=jnp.int32)
    place_in = columns % padded
    class_ids = jnp.where(place_in < classes, columns // padded * classes + place_in, -1)
    pooled, saved = jax.vmap(layer_forward, in_axes=(None, None, 0, 0, 0))(
        weights_low, vector_low, patches, heights, widths
    )
    pooled = pooled.reshape(-1, pooled.shape[-1])
    logits = jnp.dot(pooled, class_low, preferred_element_type=FULL)
    logits = jnp.where(class_ids[None] >= 0, logits, excluded)
    hit = own_labels[:, None] == class_ids[None, :]
    top = jnp.max(logits, axis=1)
    log_total = top + jnp.log(jnp.sum(jnp.exp(logits - top[:, None]), axis=1))
    losses = log_total - jnp.sum(jnp.where(hit, logits, 0.0), axis=1)
    loss_local = jnp.sum(own_weights * losses)
    logit_grad = (
        (jnp.exp(logits - log_total[:, None]) - hit.astype(FULL)) * (own_weights / weight_sum)[:, None]
    ).astype(LOW)
    class_grad = outer_dot(pooled, logit_grad).astype(LOW)
    class_grad = class_grad.reshape(-1, groups, padded).transpose(1, 0, 2).reshape(g_cls.shape)
    pooled_grad = inner_dot(logit_grad, class_low).reshape(heights.shape[0], slots, -1)
    pairs, vector_grad = jax.vmap(layer_backward, in_axes=(None, None, 0, 0))(
        weights_low, vector_low, saved, pooled_grad
    )
    grads = []
    for (left, right), like in zip(pairs, full):
        left = left.reshape(-1, left.shape[-1])
        right = right.reshape(-1, right.shape[-1])
        grads.append(outer_dot(left, right).astype(LOW).reshape(like.shape))
    vector_grad = jnp.sum(vector_grad, axis=0)
    rest = jnp.zeros((2, vector_grad.shape[1]), FULL)
    rest = rest.at[0, 0].set(loss_local).at[0, 1].set(weight_sum / count)
    g_small = jnp.concatenate([vector_grad, rest], axis=0)
    loss_terms, clip_norm, *updated = take_step(dims, grads, class_grad, g_small, params, moments)
    return (loss_terms.reshape(2), clip_norm.reshape(()), *updated)


def chip_dims(mesh):
    across, along = mesh.shape["mp"] // CORES, mesh.shape["dp"]
    return {"x": across, "y": across, "z": along // across}


def fits(mesh, width):
    devices = mesh.shape["dp"] * mesh.shape["mp"]
    dims = chip_dims(mesh)
    same = dims["x"] * dims["y"] * dims["z"] * CORES == devices
    return same and width % (8 * devices) == 0 and width // devices * CORES % 16 == 0


def solution(mesh):
    placed = (
        P(None, ("dp", "mp"), None),
        P(None, ("dp", "mp")),
        P(None, ("dp", "mp")),
        P(None, "dp"),
        P(None, "dp"),
        P(("dp", "mp"), None),
        P(("dp", "mp"), None),
        P(("dp", "mp"), None),
        P(("dp", "mp"), None),
        P(("dp", "mp"), None),
        P(None, ("dp", "mp")),
        P("dp", "mp"),
        P(("dp", "mp"), None),
        P(("dp", "mp"), None),
        P(("dp", "mp"), None),
        P(("dp", "mp"), None),
        P(("dp", "mp"), None),
        P(("dp", "mp"), None),
        P(("dp", "mp"), None),
        P(("dp", "mp"), None),
        P(("dp", "mp"), None),
        P(("dp", "mp"), None),
        P(None, ("dp", "mp")),
        P(None, ("dp", "mp")),
        P("dp", "mp"),
        P("dp", "mp"),
    )
    run = body
    if fits(mesh, 768):
        run = functools.partial(fast_body, chip_dims(mesh))
    return jax.shard_map(
        run,
        mesh=mesh,
        in_specs=placed,
        out_specs=(
            P(),
            P(),
            P(),
            P(("dp", "mp"), None),
            P(("dp", "mp"), None),
            P(("dp", "mp"), None),
            P(("dp", "mp"), None),
            P(("dp", "mp"), None),
            P(("dp", "mp"), None),
            P(("dp", "mp"), None),
            P(("dp", "mp"), None),
            P(("dp", "mp"), None),
            P(("dp", "mp"), None),
            P(("dp", "mp"), None),
            P(("dp", "mp"), None),
            P(("dp", "mp"), None),
            P(("dp", "mp"), None),
            P(("dp", "mp"), None),
            P(None, ("dp", "mp")),
            P(None, ("dp", "mp")),
            P(None, ("dp", "mp")),
            P("dp", "mp"),
            P("dp", "mp"),
            P("dp", "mp"),
        ),
        check_vma=False,
    )
```

```python
import functools
import itertools
import types

import jax
import jax.numpy as jnp
from jax import lax
from jax.experimental import pallas as pl
from jax.experimental.pallas import tpu as pltpu
from jax.sharding import PartitionSpec as P

HEAD = 64
POS = 128
STEP = 10


epsilon = 1e-06
clip_limit = 0.01
learn_rate = 0.3
beta_first = 0.9
beta_second = 0.999
weight_decay = 0.01
adam_floor = 1e-08
highest = lax.Precision.HIGHEST
excluded = -1e30


def merged_2(part, axis, combine):
    gathered = jax.tree.map(lambda a: lax.all_gather(a, axis), part)

    def take(source):
        return jax.tree.map(lambda a: lax.dynamic_index_in_dim(a, source, 0, False), gathered)

    return lax.fori_loop(
        1, lax.axis_size(axis), lambda source, state: combine(state, take(source)), take(0)
    )


def layer_norm(values, scales):
    center = values - jnp.mean(values, axis=-1, keepdims=True)
    spread = jnp.mean(center * center, axis=-1, keepdims=True)
    return center * lax.rsqrt(spread + epsilon) * scales


def norm_back(values, scales, upstream):
    result, pullback = jax.vjp(layer_norm, values, scales)
    return pullback(upstream)


def outer_dot(left, right):
    return lax.dot_general(
        left, right, (((0,), (0,)), ((), ())), preferred_element_type=jnp.float32
    )


def inner_dot(left, right):
    return lax.dot_general(
        left, right, (((1,), (1,)), ((), ())), preferred_element_type=jnp.float32
    )


def layout(heights, widths, row_count):
    lengths = heights * widths
    image_ends = jnp.cumsum(lengths)
    starts = image_ends - lengths
    places = jnp.arange(row_count, dtype=jnp.int32)
    slot_ids = jnp.arange(heights.shape[0], dtype=jnp.int32)
    segment = jnp.sum((places[:, None] >= image_ends[None, :]).astype(jnp.int32), axis=1)
    member = segment[None, :] == slot_ids[:, None]
    member_int = member.T.astype(jnp.int32)
    within = places - jnp.sum(member_int * starts[None, :], axis=1)
    across = jnp.maximum(jnp.sum(member_int * widths[None, :], axis=1), 1)
    upright = jnp.maximum(jnp.sum(member_int * heights[None, :], axis=1), 1)
    col_pos = within % across * POS // across
    row_pos = within // across * POS // upright
    pos_table = jnp.arange(POS, dtype=jnp.int32)
    pos_rows = jnp.concatenate(
        [col_pos[:, None] == pos_table[None, :], row_pos[:, None] == pos_table[None, :]], axis=1
    )
    return (segment, member, pos_rows)


def block_scores(queries, key_rows, segment):
    scores = jnp.einsum(
        "thd,shd->hts", queries, key_rows, preferred_element_type=jnp.float32
    ) * HEAD ** (-0.5)
    same_image = segment[:, None] == segment[None, :]
    return (queries, jnp.where(same_image[None], scores, excluded))


def attend(queries, key_rows, value_rows, segment):
    block_rows = min(512, queries.shape[0])

    def one_block(block_index):
        query_block, scores = block_scores(queries, key_rows, segment)
        top_score = jnp.max(scores, axis=-1, keepdims=True)
        exp_scores = jnp.exp(scores - top_score)
        exp_total = jnp.sum(exp_scores, axis=-1, keepdims=True)
        attention = (exp_scores / exp_total).astype(jnp.bfloat16)
        result = jnp.einsum(
            "hts,shd->thd", attention, value_rows, preferred_element_type=jnp.float32
        )
        return (result.astype(jnp.bfloat16), (top_score + jnp.log(exp_total))[..., 0])

    mixed_heads, log_total = lax.map(one_block, jnp.arange(queries.shape[0] // block_rows))
    return (mixed_heads.reshape(queries.shape), log_total)


def attend_back(queries, key_rows, value_rows, segment, log_total, mixed_grad):
    block_rows = min(512, queries.shape[0])

    def one_block(running, block_index):
        key_grad, value_grad = running
        query_block, scores = block_scores(queries, key_rows, segment)
        attention = jnp.exp(scores - log_total[block_index][..., None])
        value_grad = value_grad + jnp.einsum(
            "hts,thd->shd",
            attention.astype(jnp.bfloat16),
            mixed_grad,
            preferred_element_type=jnp.float32,
        )
        prob_grad = jnp.einsum(
            "thd,shd->hts", mixed_grad, value_rows, preferred_element_type=jnp.float32
        )
        score_grad = (
            attention * (prob_grad - jnp.sum(attention * prob_grad, axis=-1, keepdims=True))
        ).astype(jnp.bfloat16)
        query_grad = jnp.einsum(
            "hts,shd->thd", score_grad, key_rows, preferred_element_type=jnp.float32
        ) * HEAD ** (-0.5)
        key_grad = key_grad + jnp.einsum(
            "hts,thd->shd", score_grad, query_block, preferred_element_type=jnp.float32
        ) * HEAD ** (-0.5)
        return ((key_grad, value_grad), query_grad)

    zero_grad = jnp.zeros(key_rows.shape, jnp.float32)
    sums, query_grad = lax.scan(
        one_block, (zero_grad, zero_grad), jnp.arange(queries.shape[0] // block_rows)
    )
    return (query_grad.reshape(queries.shape), sums[0], sums[1])


def layer_forward(weights_low, vector_low, patch_rows, heights, widths):
    embed, joined_w, out_w, up_w, down_w = weights_low
    vectors = vector_low.astype(jnp.float32)
    row_count, pixel_count = patch_rows.shape
    model_width = embed.shape[1]
    head_count = model_width // HEAD
    head_shape = (row_count, head_count, HEAD)
    segment, member, pos_rows = layout(heights, widths, row_count)
    pos_low = pos_rows.astype(jnp.bfloat16)
    embedded = jnp.dot(
        patch_rows, embed[:pixel_count], preferred_element_type=jnp.float32
    ) + jnp.dot(pos_low, embed[pixel_count:], preferred_element_type=jnp.float32)
    normed = layer_norm(embedded, vectors[0]).astype(jnp.bfloat16)
    joined = jnp.dot(normed, joined_w, preferred_element_type=jnp.float32)
    query_pre = joined[:, :model_width].reshape(head_shape)
    key_pre = joined[:, model_width : 2 * model_width].reshape(head_shape)
    queries = layer_norm(query_pre, vectors[3].reshape(head_count, HEAD)).astype(jnp.bfloat16)
    key_rows = layer_norm(key_pre, vectors[4].reshape(head_count, HEAD)).astype(jnp.bfloat16)
    value_rows = joined[:, 2 * model_width :].reshape(head_shape).astype(jnp.bfloat16)
    mixed_heads, log_total = attend(queries, key_rows, value_rows, segment)
    mixed_flat = mixed_heads.reshape(row_count, model_width)
    second = embedded + jnp.dot(mixed_flat, out_w, preferred_element_type=jnp.float32)
    hidden = layer_norm(second, vectors[1]).astype(jnp.bfloat16)
    upward = jnp.dot(hidden, up_w, preferred_element_type=jnp.float32)
    active = jax.nn.gelu(upward).astype(jnp.bfloat16)
    residual = second + jnp.dot(active, down_w, preferred_element_type=jnp.float32)
    final_heads = layer_norm(residual, vectors[2]).astype(jnp.bfloat16).reshape(head_shape)
    probe_low = vector_low[5].reshape(head_count, HEAD)
    probe_scores = jnp.einsum(
        "thd,hd->th", final_heads, probe_low, preferred_element_type=jnp.float32
    ) * HEAD ** (-0.5)
    masked = jnp.where(member[:, :, None], probe_scores[None], excluded)
    pooling = jax.nn.softmax(masked, axis=1) * member[:, :, None].astype(jnp.float32)
    pool_low = pooling.astype(jnp.bfloat16)
    pooled = jnp.einsum("ith,thd->ihd", pool_low, final_heads, preferred_element_type=jnp.float32)
    saved = (
        patch_rows,
        pos_low,
        member,
        segment,
        embedded,
        normed,
        query_pre,
        key_pre,
        queries,
        key_rows,
        value_rows,
        log_total,
        mixed_flat,
        second,
        hidden,
        upward,
        active,
        residual,
        final_heads,
        pooling,
        pool_low,
    )
    return (pooled.reshape(-1, model_width).astype(jnp.bfloat16), saved)


def layer_backward(weights_low, vector_low, saved, pooled_grad):
    (
        patch_rows,
        pos_low,
        member,
        segment,
        embedded,
        normed,
        query_pre,
        key_pre,
        queries,
        key_rows,
        value_rows,
        log_total,
        mixed_flat,
        second,
        hidden,
        upward,
        active,
        residual,
        final_heads,
        pooling,
        pool_low,
    ) = saved
    embed, joined_w, out_w, up_w, down_w = weights_low
    vectors = vector_low.astype(jnp.float32)
    row_count, head_count = (final_heads.shape[0], final_heads.shape[1])
    model_width = head_count * HEAD
    image_grad = pooled_grad.reshape(-1, head_count, HEAD)
    final_wide = final_heads.astype(jnp.float32)
    weight_grad = jnp.einsum("ihd,thd->ith", image_grad, final_wide, precision=highest) * member[
        :, :, None
    ].astype(jnp.float32)
    score_grad = pooling * (weight_grad - jnp.sum(pooling * weight_grad, axis=1, keepdims=True))
    score_grad = jnp.sum(score_grad, axis=0) * HEAD ** (-0.5)
    probe = vectors[5].reshape(head_count, HEAD)
    final_grad = (
        jnp.einsum("ith,ihd->thd", pool_low.astype(jnp.float32), image_grad, precision=highest)
        + score_grad[:, :, None] * probe[None]
    )
    probe_grad = jnp.einsum("th,thd->hd", score_grad, final_wide, precision=highest)
    residual_grad, gain_final = norm_back(
        residual, vectors[2], final_grad.reshape(row_count, model_width)
    )
    down_in = residual_grad.astype(jnp.bfloat16)
    down_grad = outer_dot(active, down_in)
    active_grad = inner_dot(down_in, down_w)
    upward_grad = jax.vjp(jax.nn.gelu, upward)[1](active_grad)[0].astype(jnp.bfloat16)
    up_grad = outer_dot(hidden, upward_grad)
    second_back, gain_second = norm_back(second, vectors[1], inner_dot(upward_grad, up_w))
    second_grad = residual_grad + second_back
    out_in = second_grad.astype(jnp.bfloat16)
    out_grad = outer_dot(mixed_flat, out_in)
    mixed_grad = inner_dot(out_in, out_w).astype(jnp.bfloat16).reshape(row_count, head_count, HEAD)
    query_grad, key_grad, value_grad = attend_back(
        queries, key_rows, value_rows, segment, log_total, mixed_grad
    )
    query_back, gain_query = norm_back(query_pre, vectors[3].reshape(head_count, HEAD), query_grad)
    key_back, gain_key = norm_back(key_pre, vectors[4].reshape(head_count, HEAD), key_grad)
    joined_grad = jnp.concatenate(
        [
            query_back.reshape(row_count, model_width),
            key_back.reshape(row_count, model_width),
            value_grad.reshape(row_count, model_width),
        ],
        axis=1,
    ).astype(jnp.bfloat16)
    joined_w_grad = outer_dot(normed, joined_grad)
    first_back, gain_first = norm_back(embedded, vectors[0], inner_dot(joined_grad, joined_w))
    embed_in = (second_grad + first_back).astype(jnp.bfloat16)
    embed_grad = jnp.concatenate(
        [outer_dot(patch_rows, embed_in), outer_dot(pos_low, embed_in)], axis=0
    )
    vector_grad = jnp.stack(
        [
            gain_first,
            gain_second,
            gain_final,
            gain_query.reshape(model_width),
            gain_key.reshape(model_width),
            probe_grad.reshape(model_width),
        ]
    )
    return (embed_grad, joined_w_grad, out_grad, up_grad, down_grad, vector_grad)


def reduce_grads(fresh):
    return (
        lax.psum_scatter(fresh[0], ("dp", "mp"), scatter_dimension=0, tiled=True),
        lax.psum_scatter(fresh[1], ("dp", "mp"), scatter_dimension=0, tiled=True),
        lax.psum_scatter(fresh[2], ("dp", "mp"), scatter_dimension=0, tiled=True),
        lax.psum_scatter(fresh[3], ("dp", "mp"), scatter_dimension=0, tiled=True),
        lax.psum_scatter(fresh[4], ("dp", "mp"), scatter_dimension=0, tiled=True),
        lax.psum_scatter(fresh[5], ("dp", "mp"), scatter_dimension=1, tiled=True),
    )


def combine_stats(earlier, later_one):
    top_score = jnp.maximum(earlier[0], later_one[0])
    exp_total = earlier[1] * jnp.exp(earlier[0] - top_score) + later_one[1] * jnp.exp(
        later_one[0] - top_score
    )
    return (top_score, exp_total, earlier[2] + later_one[2])


def lamb_update(weight, gradient, moment_one, moment_two, factor):
    gradient = gradient * factor
    moment_one = beta_first * moment_one + (1.0 - beta_first) * gradient
    moment_two = beta_second * moment_two + (1.0 - beta_second) * gradient * gradient
    update = (
        moment_one
        / (1.0 - beta_first**STEP)
        / (jnp.sqrt(moment_two / (1.0 - beta_second**STEP)) + adam_floor)
        + weight_decay * weight
    )
    return (moment_one, moment_two, update)


def body(
    patches,
    heights,
    widths,
    labels,
    res_weights,
    w_embed,
    w_qkv,
    w_out,
    w_up,
    w_down,
    vectors,
    w_cls,
    m_embed,
    v_embed,
    m_qkv,
    v_qkv,
    m_out,
    v_out,
    m_up,
    v_up,
    m_down,
    v_down,
    m_vectors,
    v_vectors,
    m_cls,
    v_cls,
):
    gathered = (
        lax.all_gather(w_embed.astype(jnp.bfloat16), ("dp", "mp"), axis=0, tiled=True),
        lax.all_gather(w_qkv.astype(jnp.bfloat16), ("dp", "mp"), axis=0, tiled=True),
        lax.all_gather(w_out.astype(jnp.bfloat16), ("dp", "mp"), axis=0, tiled=True),
        lax.all_gather(w_up.astype(jnp.bfloat16), ("dp", "mp"), axis=0, tiled=True),
        lax.all_gather(w_down.astype(jnp.bfloat16), ("dp", "mp"), axis=0, tiled=True),
        lax.all_gather(vectors.astype(jnp.bfloat16), ("dp", "mp"), axis=1, tiled=True),
    )
    weights_low = gathered[:5]
    vector_low = gathered[5]
    class_low = lax.all_gather(w_cls.astype(jnp.bfloat16), "dp", axis=0, tiled=True)
    member_index = lax.axis_index("mp")
    slot_count = heights.shape[1]
    own_start = member_index * slot_count
    own_weights = lax.dynamic_slice_in_dim(res_weights, own_start, slot_count, 1).astype(
        jnp.float32
    )
    weight_sum = lax.psum(jnp.sum(own_weights), ("dp", "mp"))
    class_count = class_low.shape[1]
    class_ids = member_index * class_count + jnp.arange(class_count, dtype=jnp.int32)
    loss_local = jnp.zeros((), jnp.float32)
    class_grad = jnp.zeros(class_low.shape, jnp.float32)
    summed = None
    for micro_index in range(patches.shape[0]):
        pooled, saved = layer_forward(
            weights_low, vector_low, patches[micro_index], heights[micro_index], widths[micro_index]
        )
        group_rows = lax.all_gather(pooled, "mp", axis=0, tiled=True)
        logits = jnp.dot(group_rows, class_low, preferred_element_type=jnp.float32)
        label_hit = labels[micro_index][:, None] == class_ids[None, :]
        top_score = jnp.max(logits, axis=1)
        exp_total = jnp.sum(jnp.exp(logits - top_score[:, None]), axis=1)
        picked = jnp.sum(jnp.where(label_hit, logits, 0.0), axis=1)
        merged = merged_2((top_score, exp_total, picked), "mp", combine_stats)
        log_total = merged[0] + jnp.log(merged[1])
        group_weights = res_weights[micro_index].astype(jnp.float32)
        weighted = group_weights * (log_total - merged[2])
        loss_local = loss_local + jnp.sum(
            lax.dynamic_slice_in_dim(weighted, own_start, slot_count, 0)
        )
        logit_grad = (
            (jnp.exp(logits - log_total[:, None]) - label_hit.astype(jnp.float32))
            * (group_weights / weight_sum)[:, None]
        ).astype(jnp.bfloat16)
        class_grad = class_grad + outer_dot(group_rows, logit_grad)
        pooled_grad = lax.psum_scatter(
            inner_dot(logit_grad, class_low), "mp", scatter_dimension=0, tiled=True
        )
        fresh = layer_backward(weights_low, vector_low, saved, pooled_grad)
        summed = fresh if summed is None else jax.tree.map(jnp.add, summed, fresh)
    summed = reduce_grads(summed)
    class_shard = lax.psum_scatter(class_grad, "dp", scatter_dimension=0, tiled=True)
    params = (w_embed, w_qkv, w_out, w_up, w_down, vectors, w_cls)
    moments = (
        (m_embed, v_embed),
        (m_qkv, v_qkv),
        (m_out, v_out),
        (m_up, v_up),
        (m_down, v_down),
        (m_vectors, v_vectors),
        (m_cls, v_cls),
    )
    gradients = (summed[0], summed[1], summed[2], summed[3], summed[4], summed[5], class_shard)
    matrix_order = (0, 1, 2, 3, 4, 6)
    grad_squares = jnp.concatenate(
        [
            jnp.stack(
                [jnp.sum(gradients[position] * gradients[position]) for position in matrix_order]
            ),
            jnp.sum(gradients[5] * gradients[5], axis=1),
        ]
    )
    square_sums, loss_total = lax.psum((grad_squares, loss_local), ("dp", "mp"))
    clip_norm = jnp.sqrt(jnp.sum(square_sums))
    factor = jnp.minimum(1.0, clip_limit / clip_norm)
    updated = [
        lamb_update(
            params[position],
            gradients[position],
            moments[position][0],
            moments[position][1],
            factor,
        )
        for position in range(7)
    ]
    matrix_parts = jnp.stack(
        [
            jnp.stack(
                [
                    jnp.sum(params[position] * params[position]),
                    jnp.sum(updated[position][2] * updated[position][2]),
                ]
            )
            for position in matrix_order
        ]
    )
    vector_parts = jnp.stack(
        [jnp.sum(params[5] * params[5], axis=1), jnp.sum(updated[5][2] * updated[5][2], axis=1)],
        axis=1,
    )
    norms = jnp.sqrt(lax.psum(jnp.concatenate([matrix_parts, vector_parts], axis=0), ("dp", "mp")))
    ratios = norms[:, 0] / norms[:, 1]
    outputs = [jnp.stack([loss_total, weight_sum]), clip_norm, norms]
    for position in range(7):
        if position == 5:
            ratio = ratios[6:][:, None]
        else:
            ratio = ratios[matrix_order.index(position)]
        moment_one, moment_two, update = updated[position]
        outputs += [params[position] - learn_rate * ratio * update, moment_one, moment_two]
    return tuple(outputs)


MESH_ID = pl.DeviceIdType.MESH
CORES = 2
ALL = slice(None)
LOW = jnp.bfloat16
FULL = jnp.float32
NN = (((1,), (0,)), ((), ()))
NT = (((1,), (1,)), ((), ()))
TN = (((0,), (0,)), ((), ()))
COLUMNS = 768


class Place:
    def __init__(self, dims):
        self.sizes = dict(dims, c=CORES)
        dp, mp = lax.axis_index("dp"), lax.axis_index("mp")
        wide = self.sizes["y"]
        self.at = {"z": dp // wide, "y": dp % wide, "x": mp // CORES, "c": mp % CORES}

    def source(self, axis, step):
        size = self.sizes[axis]
        return (self.at[axis] + (size - step) % size) % size

    def peer(self, axis, step):
        at = dict(self.at)
        at[axis] = self.source(axis, -step)
        return (at["z"] * self.sizes["y"] + at["y"], at["x"] * CORES + at["c"])

    def steps(self, axis):
        return range(1, self.sizes[axis])

    def tell(self, semaphore):
        count = 0
        for axis in "cxyz":
            for step in self.steps(axis):
                pl.semaphore_signal(
                    semaphore, inc=1, device_id=self.peer(axis, step), device_id_type=MESH_ID
                )
                count += 1
        return count


class Courier:
    def __init__(self, place, send, recv):
        self.place, self.send, self.recv, self.open, self.count = place, send, recv, [], 0

    def start(self, axis, step, source, target):
        slot = self.count
        self.count += 1
        copy = pltpu.make_async_remote_copy(
            src_ref=source,
            dst_ref=target,
            send_sem=self.send.at[slot],
            recv_sem=self.recv.at[slot],
            device_id=self.place.peer(axis, step),
            device_id_type=MESH_ID,
        )
        copy.start()
        self.open.append(copy)
        return copy

    def sent(self, copies):
        for copy in copies:
            copy.wait_send()
            self.open = [other for other in self.open if other is not copy]

    def finish(self):
        self.sent(list(self.open))


class Spread:
    def __init__(self, courier, view, order):
        self.courier, self.place, self.view, self.order = courier, courier.place, view, order
        self.relayed = []

    def part(self, stage, **fixed):
        where = {axis: self.place.at[axis] for axis in "xyz"}
        for axis in ("z" + self.order)[:stage]:
            where[axis] = ALL
        where.update(fixed)
        return self.view(**where)

    def send(self, axis, stage):
        part = self.part(stage)
        return [self.courier.start(axis, step, part, part) for step in self.place.steps(axis)]

    def relay(self, part):
        self.relayed.append(self.courier.start("c", 1, part, part))

    def begin(self):
        self.coming = self.send("z", 0)

    def middle(self, stage):
        for copy in self.coming:
            copy.wait_recv()
        if stage == 1:
            self.relay(self.part(1))
        else:
            axis = self.order[stage - 2]
            for step in self.place.steps(axis):
                self.relay(self.part(stage - 1, **{axis: self.place.source(axis, step)}))
        self.coming = self.send(self.order[stage - 1], stage) if stage < 3 else []

    def done(self):
        for copy in self.relayed:
            copy.wait_recv()


class Pool:
    def __init__(self, ref, axes, rows, held, rest, width):
        self.ref, self.axes, self.rows, self.marks, self.width = ref, axes, rows, (held, rest), width

    def at(self, half, **where):
        key = tuple(where.get(axis, ALL) for axis in self.axes)
        return self.ref.at[key + (pl.ds(*self.rows), pl.ds(self.marks[half], self.width))]


class Fold:
    def __init__(self, courier, view, order, pool, finish):
        self.courier, self.place, self.view, self.order = courier, courier.place, view, order
        self.pool, self.finish, self.copies, self.stage = pool, finish, [], 0

    def start(self, axis, step, source, target):
        copy = self.courier.start(axis, step, source, target)
        self.copies.append(copy)
        self.coming.append(copy)

    def landing(self, stage, step):
        first, second = self.order
        sizes = self.place.sizes
        if stage == 1:
            return self.pool.at(1, **{first: step - 1})
        if stage == 2:
            return self.pool.at(1, **{first: sizes[first] - 1, second: step - 1})
        return self.pool.at(1, **{first: sizes[first] - 1, second: sizes[second] - 1, "z": step - 1})

    def send(self, stage):
        axis = (self.order + "z")[stage - 1]
        fixed = {a: self.place.at[a] for a in self.order[: stage - 1]}
        self.coming = []
        for step in self.place.steps(axis):
            source = self.pool.at(0, **{axis: self.place.source(axis, -step)}, **fixed)
            self.start(axis, step, source, self.landing(stage, step))

    def begin(self):
        self.coming = []
        self.start("c", 1, self.view(1 - self.place.at["c"]), self.pool.at(0))

    def advance(self):
        for copy in self.coming:
            copy.wait_recv()
        stage, place = self.stage, self.place
        self.stage += 1
        if stage == 3:
            here = self.pool.at(0, **place_of(place, "xyz"))
            total = here[...].astype(FULL)
            for step in place.steps("z"):
                total = total + self.landing(3, step)[...].astype(FULL)
            self.finish(total)
            return True
        here = self.pool.at(0, **place_of(place, self.order[:stage]))
        if stage == 0:
            came = [self.view(place.at["c"])]
        else:
            came = [self.landing(stage, step) for step in place.steps(self.order[stage - 1])]

        def one(lead, carry):
            total = here[lead].astype(FULL)
            for part in came:
                total = total + part[lead].astype(FULL)
            here[lead] = total.astype(LOW)
            return carry

        lax.fori_loop(0, here.shape[0], one, 0)
        self.send(stage + 1)
        return False


def place_of(place, axes):
    return {axis: place.at[axis] for axis in axes}


class Total:
    def __init__(self, courier, slots):
        self.courier, self.place, self.slots = courier, courier.place, dict(zip("cxyz", slots))

    def send(self, axis, block):
        mine = self.slots[axis].at[self.place.at[axis]]
        mine[...] = block
        self.coming = [
            self.courier.start(axis, step, mine, mine) for step in self.place.steps(axis)
        ]

    def receive(self, axis):
        for copy in self.coming:
            copy.wait_recv()
        slots = self.slots[axis]
        total = slots[0]
        for index in range(1, slots.shape[0]):
            total = total + slots[index]
        return total

    def through(self, block):
        for axis in "cxyz":
            self.send(axis, block)
            block = self.receive(axis)
        return block


def total_slots(dims, shape):
    sizes = dict(dims, c=CORES)
    return [pltpu.VMEM((sizes[axis],) + shape, FULL) for axis in "cxyz"]


def cut(rows, width, parts):
    if rows % (16 * parts) == 0:
        size = rows // parts
        return [((part * size, size), (0, width)) for part in range(parts)]
    units = width // 128
    marks = [units * part // parts * 128 for part in range(parts + 1)]
    return [((0, rows), (low, high - low)) for low, high in zip(marks, marks[1:]) if high > low]


def pieces_of(blocks):
    found = []
    for index, (rows, width) in enumerate(blocks):
        parts = max(2, min(4, rows * width // 16384 // 2 * 2))
        for row_range, column_range in cut(rows, width, parts):
            found.append((index, row_range, column_range, ("xy", "yx")[len(found) % 2]))
    return found


def dot(left, right, form=NN):
    return lax.dot_general(left, right, form, preferred_element_type=FULL)


def halves(values):
    high = values.astype(LOW)
    return high, (values - high.astype(FULL)).astype(LOW)


def fine_dot(left, values, form):
    high, rest = halves(values)
    return dot(left, high, form) + dot(left, rest, form)


def iota(shape, axis):
    return lax.broadcasted_iota(jnp.int32, shape, axis).astype(FULL)


def normal(values, axis):
    center = values - jnp.mean(values, axis=axis, keepdims=True)
    scale = lax.rsqrt(jnp.mean(center * center, axis=axis, keepdims=True) + epsilon)
    return center * scale, scale


def normal_back(upstream, shape, scale, axis):
    mean = jnp.mean(upstream, axis=axis, keepdims=True)
    along = jnp.mean(upstream * shape, axis=axis, keepdims=True)
    return scale * (upstream - mean - shape * along)


def column_sum(values):
    return jnp.sum(values, axis=0, keepdims=True)


def row_sum(values):
    return jnp.sum(values, axis=1, keepdims=True)


def curve(values):
    return jnp.tanh(0.7978845608 * (values + 0.044715 * values * values * values))


def squares(values):
    total = jnp.zeros((1, 128), FULL)
    for low in range(0, values.shape[1], 128):
        part = values[:, low : low + 128]
        part = column_sum(part * part)
        if part.shape[1] < 128:
            part = jnp.concatenate([part, jnp.zeros((1, 128 - part.shape[1]), FULL)], axis=1)
        total = total + part
    return total


def wide_rows(values):
    squared = values * values
    rest = jnp.zeros((squared.shape[0], 128 - squared.shape[1]), FULL)
    return jnp.concatenate([squared, rest], axis=1)


def moments_step(gradient, moment_one, moment_two):
    first = beta_first * moment_one + (1.0 - beta_first) * gradient
    second = beta_second * moment_two + (1.0 - beta_second) * gradient * gradient
    return first, second


def update_of(first, second, weight):
    return (
        first
        / (1.0 - beta_first**STEP)
        / (jnp.sqrt(second / (1.0 - beta_second**STEP)) + adam_floor)
        + weight_decay * weight
    )


def loop(count, body):
    def one(index, carry):
        body(index)
        return carry

    lax.fori_loop(0, count, one, 0)


def tile(index, size):
    return pl.ds(pl.multiple_of(index * size, size), size)


class Layer:
    def __init__(self, r, place, dims):
        self.r, self.place = r, place
        self.rows, self.width = r.patches.shape
        self.packs, self.slots = r.heights.shape
        self.tokens = self.rows // self.packs
        self.head_count = self.width // HEAD
        self.hidden_units = r.g_up.shape[-1]
        self.groups = dims["x"] * CORES
        self.member_index = place.at["x"] * CORES + place.at["c"]
        self.w_embed = r.g_embed.reshape(-1, self.width)
        self.w_qkv = r.g_qkv.reshape(self.width, 3 * self.width)
        self.w_out = r.g_out.reshape(self.width, self.width)
        self.w_up = r.g_up.reshape(self.width, self.hidden_units)
        self.w_down = r.g_down.reshape(self.hidden_units, self.width)
        self.upward = r.upward.reshape(self.rows, self.hidden_units)
        self.active = r.active.reshape(self.rows, self.hidden_units)

    def span(self, pack):
        return pl.ds(pack * self.tokens, self.tokens)

    def gain(self, row):
        return self.r.vec[row : row + 1]

    def class_block(self, group):
        block = self.r.g_cls.at[group // CORES, group % CORES]
        return block.reshape(self.width, block.shape[-1])

    def head_marks(self):
        return (
            jnp.floor((iota((16, self.width), 1) + 0.5) / HEAD) == iota((16, self.width), 0)
        ).astype(FULL)

    def place_rows(self, pack):
        r, tokens, slots = self.r, self.tokens, self.slots
        high = r.heights[pack : pack + 1].astype(FULL)
        wide = r.widths[pack : pack + 1].astype(FULL)
        lengths = high * wide
        square = (slots, slots)
        below, beside = iota(square, 0), iota(square, 1)
        ends_column = row_sum(jnp.where(beside <= below, lengths, 0.0))
        length_column = row_sum(jnp.where(beside == below, lengths, 0.0))
        ends = column_sum(jnp.where(below <= beside, length_column, 0.0))
        spots = iota((tokens, slots), 0)
        segment = row_sum((spots >= ends).astype(FULL))
        member = (iota((tokens, slots), 1) == segment).astype(FULL)
        within = spots[:, :1] - row_sum(member * (ends - lengths))
        across = jnp.maximum(row_sum(member * wide), 1.0)
        upright = jnp.maximum(row_sum(member * high), 1.0)
        line = jnp.floor((within + 0.5) / across)
        column = within - line * across
        table = iota((tokens, POS), 1)
        span = self.span(pack)
        r.pos[span, :POS] = (jnp.floor((column * POS + 0.5) / across) == table).astype(LOW)
        r.pos[span, POS:] = (jnp.floor((line * POS + 0.5) / upright) == table).astype(LOW)
        r.cols[span, 0:1] = segment
        r.segment[pack : pack + 1] = column_sum((iota((slots, tokens), 1) >= ends_column).astype(FULL))

    def read_vectors(self):
        r = self.r
        blocks = r.g_vec[...].reshape(-1, 8, 128)
        count = blocks.shape[0]
        share = self.width // count
        wide = iota((128, self.width), 1)
        owner = jnp.floor((wide[:1] + 0.5) / share)
        spread = (wide - owner * share == iota((128, self.width), 0)).astype(LOW)
        everywhere = dot(blocks.reshape(count * 8, 128).astype(LOW), spread).reshape(count, 8, self.width)
        mine = lax.broadcasted_iota(jnp.int32, (count, 1, self.width), 0).astype(FULL) == owner[None]
        r.vec[...] = jnp.sum(jnp.where(mine, everywhere, 0.0), axis=0)
        r.gains[...] = r.vec[...].T
        total = jnp.sum(blocks, axis=0)[6:7]
        r.weight_sum[...] = jnp.broadcast_to(row_sum(total), (1, 128))
        r.vgrad[...] = jnp.zeros(r.vgrad.shape, FULL)
        r.gacc[...] = jnp.zeros(r.gacc.shape, FULL)

    def embed(self, pack):
        r, span = self.r, self.span(pack)
        embedded = dot(r.patches[span], self.w_embed[: self.width])
        embedded = embedded + dot(r.pos[span], self.w_embed[self.width :])
        shape, scale = normal(embedded, -1)
        r.stream[span] = embedded
        r.shape_first[span] = shape.astype(LOW)
        r.cols[span, 1:2] = scale
        r.normed[span] = (shape * self.gain(0)).astype(LOW)

    def project(self, pack):
        r, span, width = self.r, self.span(pack), self.width
        for part in range(3):
            joined = dot(r.normed[span], self.w_qkv[:, part * width : (part + 1) * width])
            if part == 2:
                r.joined[2 * width :, span] = joined.T.astype(LOW)
                continue
            r.turned[...] = joined.T

            def one_head(head, part=part):
                own = tile(head, HEAD)
                at = pl.ds(pl.multiple_of(part * width + head * HEAD, HEAD), HEAD)
                shape, scale = normal(r.turned[own], 0)
                r.shape_heads[at, span] = shape.astype(LOW)
                r.scale_heads[pl.ds(part * self.head_count + head, 1), span] = scale
                r.joined[at, span] = (shape * r.gains[own, 3 + part : 4 + part]).astype(LOW)

            loop(self.head_count, one_head)

    def mask(self, pack):
        r = self.r
        same = r.cols[self.span(pack), 0:1] == r.segment[pack : pack + 1]
        r.mask[...] = jnp.where(same, 0.0, excluded)

    def head_parts(self, head, span):
        starts = (part * self.width + head * HEAD for part in range(3))
        return [pl.ds(pl.multiple_of(start, HEAD), HEAD) for start in starts]

    def attend(self, pack):
        r, span = self.r, self.span(pack)
        self.mask(pack)

        def one_head(head):
            query, key, value = (r.joined[at, span] for at in self.head_parts(head, span))
            scores = dot(key, query, TN) * HEAD ** (-0.5) + r.mask[...]
            top = jnp.max(scores, axis=0, keepdims=True)
            grown = jnp.exp(scores - top)
            total = column_sum(grown)
            r.log_total[pl.ds(head, 1), span] = top + jnp.log(total)
            attention = (grown * (1.0 / total)).astype(LOW)
            r.mixed[tile(head, HEAD), span] = dot(value, attention).astype(LOW)

        loop(self.head_count, one_head)

    def join(self, pack):
        r, span = self.r, self.span(pack)
        second = r.stream[span] + dot(r.mixed[:, span], self.w_out[...], TN)
        shape, scale = normal(second, -1)
        r.stream[span] = second
        r.shape_second[span] = shape.astype(LOW)
        r.cols[span, 2:3] = scale
        r.hidden[span] = (shape * self.gain(1)).astype(LOW)

    def widen(self, index):
        at = tile(index, 256)
        upward = dot(self.r.hidden[...], self.w_up[:, at])
        self.upward[:, at] = upward.astype(LOW)
        self.active[:, at] = (upward * (0.5 * (1.0 + curve(upward)))).astype(LOW)

    def narrow(self, index):
        at = tile(index, 256)
        self.r.stream[:, at] += dot(self.active[...], self.w_down[:, at])

    def own_slots(self, ref, pack):
        wide = ref.shape[1]
        row = jnp.broadcast_to(ref[pack : pack + 1].astype(FULL), (self.slots, wide))
        own = self.member_index * self.slots
        lanes = lax.broadcasted_iota(jnp.int32, row.shape, 1)
        places = lax.broadcasted_iota(jnp.int32, row.shape, 0)
        return row_sum(jnp.where(lanes == own + places, row, 0.0))

    def image_spread(self, values, segment, reduce, start):
        out = jnp.full(values.shape, start, FULL)
        for slot in range(self.slots):
            inside = segment == float(slot)
            one = reduce(jnp.where(inside, values, start if reduce is jnp.max else 0.0), axis=1, keepdims=True)
            out = jnp.where(inside, one, out)
        return out

    def classify(self, pack):
        r, span, slots, width = self.r, self.span(pack), self.slots, self.width
        strip = 128
        strips = self.tokens // strip

        def strip_rows(index):
            return pl.ds(pl.multiple_of(pack * self.tokens + index * strip, strip), strip)

        def finish_norm(index):
            shape, _ = normal(r.stream[strip_rows(index)], -1)
            r.low[strip_rows(index)] = (shape * self.gain(2)).astype(LOW)

        loop(strips, finish_norm)
        final = r.low[span]
        marks = self.head_marks()
        marks_low = marks.astype(LOW)
        probe = self.gain(5)
        segment = r.segment[pack : pack + 1]
        scores = dot((marks * probe).astype(LOW), final, NT) * HEAD ** (-0.5)
        top = self.image_spread(scores, segment, jnp.max, excluded)
        grown = jnp.where(segment < float(slots), jnp.exp(scores - top), 0.0)
        pooling = grown / jnp.maximum(self.image_spread(grown, segment, jnp.sum, 1.0), 1e-30)
        member = (segment == iota((slots, self.tokens), 0)).astype(FULL)
        pool_wide = pooling.astype(LOW).astype(FULL)
        r.pool_heads[...] = pool_wide
        stacked = [member * pool_wide[head : head + 1] for head in range(self.head_count)]
        stacked = dot(jnp.concatenate(stacked, axis=0).astype(LOW), final)
        pooled = jnp.zeros((slots, width), FULL)
        for head in range(self.head_count):
            pooled = pooled + stacked[head * slots : (head + 1) * slots] * marks[head : head + 1]
        pooled = pooled.astype(LOW)
        image_span = pl.ds(pack * slots, slots)
        r.pooled[image_span] = pooled
        padded, classes = r.g_cls.shape[-1], r.w_cls.shape[1]
        logits = [dot(pooled, self.class_block(group)[...]) for group in range(self.groups)]
        logits = jnp.concatenate(logits, axis=1)
        lanes = iota(logits.shape, 1)
        block = jnp.floor((lanes + 0.5) / padded)
        within = lanes - block * padded
        logits = jnp.where(within < classes, logits, excluded)
        hit = block * classes + within == self.own_slots(r.labels, pack)
        hit = (hit & (within < classes)).astype(FULL)
        weights = self.own_slots(r.weights, pack)
        top = jnp.max(logits, axis=1, keepdims=True)
        log_total = top + jnp.log(row_sum(jnp.exp(logits - top)))
        losses = weights * (log_total - row_sum(hit * logits))
        first = (iota((1, width), 1) == 0.0).astype(FULL)
        r.vgrad[6:7] += first * column_sum(losses)
        share = weights / r.weight_sum[:, :1]
        logit_grad = ((jnp.exp(logits - log_total) - hit) * share).astype(LOW)
        r.logit_grad[image_span] = logit_grad
        pooled_grad = jnp.zeros((slots, width), FULL)
        for group in range(self.groups):
            part = logit_grad[:, group * padded : (group + 1) * padded]
            pooled_grad = pooled_grad + dot(part, self.class_block(group)[...], NT)
        r.image_high[...], r.image_rest[...] = halves(pooled_grad)

        def image_rows(index):
            owner = r.cols[strip_rows(index), 0:1]
            member_rows = (iota((strip, slots), 1) == owner).astype(LOW)
            return dot(member_rows, r.image_high[...]) + dot(member_rows, r.image_rest[...])

        def weigh(index):
            product = image_rows(index) * r.low[strip_rows(index)].astype(FULL)
            r.score_heads[:, tile(index, strip)] = fine_dot(marks_low, product, NT)

        loop(strips, weigh)
        weight_grad = r.score_heads[...]
        mean = self.image_spread(pooling * weight_grad, segment, jnp.sum, 0.0)
        r.score_heads[...] = pooling * (weight_grad - mean) * HEAD ** (-0.5)

        def strip_back(index):
            rows, lanes = strip_rows(index), tile(index, strip)
            high, rest = halves(r.score_heads[:, lanes])
            score_rows = dot(high, marks_low, TN) + dot(rest, marks_low, TN)
            pool_rows = dot(r.pool_heads[:, lanes].astype(LOW), marks_low, TN)
            r.vgrad[5:6] += column_sum(score_rows * r.low[rows].astype(FULL))
            final_grad = pool_rows * image_rows(index) + score_rows * probe
            shape, scale = normal(r.stream[rows], -1)
            r.vgrad[2:3] += column_sum(final_grad * shape)
            residual_grad = normal_back(final_grad * self.gain(2), shape, scale, -1)
            r.stream[rows] = residual_grad
            r.low[rows] = residual_grad.astype(LOW)

        loop(strips, strip_back)

    def class_back(self):
        r = self.r
        padded = r.g_cls.shape[-1]
        for group in range(self.groups):
            part = r.logit_grad[:, group * padded : (group + 1) * padded]
            self.class_block(group)[...] = dot(r.pooled[...], part, TN).astype(LOW)

    def active_back(self, index):
        at = tile(index, 256)
        upstream = dot(self.r.low[...], self.w_down[at], NT)
        upward = self.upward[:, at].astype(FULL)
        bend = curve(upward)
        squared = upward * upward
        slope = 0.5 * (1.0 + bend) + (0.5 * 0.7978845608) * upward * (1.0 - bend * bend) * (
            1.0 + (3 * 0.044715) * squared
        )
        self.upward[:, at] = (upstream * slope).astype(LOW)

    def down_weight(self, index):
        at = tile(index, 256)
        self.w_down[at] = dot(self.active[:, at], self.r.low[...], TN).astype(LOW)

    def second_back(self, pack):
        r, span = self.r, self.span(pack)
        upstream = dot(self.upward[span], self.w_up[...], NT)
        shape = r.shape_second[span].astype(FULL)
        r.vgrad[1:2] += column_sum(upstream * shape)
        back = normal_back(upstream * self.gain(1), shape, r.cols[span, 2:3], -1)
        total = r.stream[span] + back
        r.stream[span] = total
        r.low[span] = total.astype(LOW)

    def up_weight(self, index, part):
        rows, columns = tile(index, 256), pl.ds(part * COLUMNS, COLUMNS)
        self.w_up[rows, columns] = dot(self.r.hidden[:, rows], self.upward[:, columns], TN).astype(LOW)

    def mixed_back(self, pack):
        r, span = self.r, self.span(pack)
        r.hidden[span] = dot(r.low[span], self.w_out[...], NT).astype(LOW)

    def out_weight(self, index):
        at = tile(index, 256)
        self.w_out[at] = dot(self.r.mixed[at], self.r.low[...]).astype(LOW)

    def attend_back(self, pack):
        r, span = self.r, self.span(pack)
        self.mask(pack)
        r.mixed[:, span] = r.hidden[span].T
        count = self.head_count

        def head_back(grad, part, head, at):
            own = tile(head, HEAD)
            shape = r.shape_heads[at, span].astype(FULL)
            scale = r.scale_heads[pl.ds(part * count + head, 1), span]
            term = grad * shape
            for low in range(0, self.tokens, 128):
                r.gacc[at] += term[:, low : low + 128]
            back = normal_back(grad * r.gains[own, 3 + part : 4 + part], shape, scale, 0)
            r.joined[at, span] = back.astype(LOW)

        def one_head(head):
            parts = self.head_parts(head, span)
            query, key, value = (r.joined[at, span] for at in parts)
            mixed_grad = r.mixed[tile(head, HEAD), span]
            scores = dot(key, query, TN) * HEAD ** (-0.5) + r.mask[...]
            attention = jnp.exp(scores - r.log_total[pl.ds(head, 1), span])
            prob_grad = dot(value, mixed_grad, TN)
            mean = column_sum(attention * prob_grad)
            score_grad = (attention * (prob_grad - mean)).astype(LOW)
            r.joined[parts[2], span] = dot(mixed_grad, attention.astype(LOW), NT).astype(LOW)
            head_back(dot(key, score_grad) * HEAD ** (-0.5), 0, head, parts[0])
            head_back(dot(query, score_grad, NT) * HEAD ** (-0.5), 1, head, parts[1])

        loop(count, one_head)

    def first_back(self, pack):
        r, span = self.r, self.span(pack)
        upstream = dot(r.joined[:, span].T, self.w_qkv[...], NT)
        shape = r.shape_first[span].astype(FULL)
        r.vgrad[0:1] += column_sum(upstream * shape)
        back = normal_back(upstream * self.gain(0), shape, r.cols[span, 1:2], -1)
        r.low[span] = (r.stream[span] + back).astype(LOW)

    def qkv_weight(self, index):
        rows = tile(index, 256)
        turned = self.r.normed[:, rows].T
        for part in range(3):
            columns = pl.ds(part * COLUMNS, COLUMNS)
            self.w_qkv[rows, columns] = dot(turned, self.r.joined[columns], NT).astype(LOW)

    def embed_weight(self):
        r, width = self.r, self.width

        def one(index):
            at = tile(index, 256)
            self.w_embed[at] = dot(r.patches[:, at], r.low[...], TN).astype(LOW)

        loop(width // 256, one)
        self.w_embed[width:] = dot(r.pos[...], r.low[...], TN).astype(LOW)

    def head_gains(self):
        r, width = self.r, self.width
        for part in range(2):
            r.vgrad[3 + part : 4 + part] = column_sum(r.gacc[part * width : (part + 1) * width].T)


def kernel(dims, names, pieces, class_pieces, *refs):
    r = types.SimpleNamespace(**dict(zip(names, refs)))
    place = Place(dims)
    barrier = pltpu.get_barrier_semaphore()
    pl.semaphore_wait(barrier, place.tell(barrier))
    courier = Courier(place, r.send, r.recv)
    layer = Layer(r, place, dims)
    z, y, x, core = (place.at[axis] for axis in "zyxc")
    shards = [r.w_embed, r.w_qkv, r.w_out, r.w_up, r.w_down]
    full = [r.g_embed, r.g_qkv, r.g_out, r.g_up, r.g_down]
    pairs = [r.p_embed, r.p_qkv, r.p_out, r.p_up, r.p_down]
    owned = [r.o_embed, r.o_qkv, r.o_out, r.o_up, r.o_down]
    order = (0, 1, 2, 3, 4)

    arriving = []
    for shard, pair in zip(shards, pairs):
        rows, half = shard.shape[0], shard.shape[1] // CORES
        at = pl.ds(pl.multiple_of(core * rows, 8), rows)
        other = pl.ds(pl.multiple_of((1 - core) * half, 128), half)
        arriving.append(courier.start("c", 1, shard.at[:, other], pair.at[at]))
        pair[at] = shard[:, pl.ds(pl.multiple_of(core * half, 128), half)]
    r.g_vec[z, y, x, core] = jnp.zeros((8, 128), FULL)
    count = r.vectors.shape[1]
    r.g_vec[z, y, x, core, pl.ds(0, 6), pl.ds(0, count)] = r.vectors[...].astype(LOW).astype(FULL)
    wide = r.weights.shape[1]
    own = layer.member_index * layer.slots
    lanes = lax.broadcasted_iota(jnp.int32, r.weights.shape, 1)
    inside = (lanes >= own) & (lanes < own + layer.slots)
    counted = column_sum(jnp.where(inside, r.weights[...], 0).astype(FULL))
    r.g_vec[z, y, x, core, pl.ds(6, 1), pl.ds(0, wide)] = counted
    block = r.g_cls.at[x, core, z, y]
    block[...] = jnp.zeros(block.shape, LOW)
    block[:, pl.ds(0, r.w_cls.shape[1])] = r.w_cls[...].astype(LOW)

    def matrix_view(piece, core):
        index, rows, columns, _ = piece
        half = full[index].shape[-1] // CORES
        across = pl.ds(pl.multiple_of(core * half + columns[0], 128), columns[1])
        return lambda z, y, x: full[index].at[z, y, x, pl.ds(*rows), across]

    def class_view(piece, core):
        return lambda z, y, x: r.g_cls.at[x, core, z, y, pl.ds(*piece[1])]

    spreads = [Spread(courier, lambda z, y, x: r.g_vec.at[z, y, x, core], "xy")]
    ready, last = {}, {}
    for piece in pieces:
        ready.setdefault(len(spreads), piece[0]) if piece[0] not in ready.values() else None
        last[piece[0]] = len(spreads)
        spreads.append(Spread(courier, matrix_view(piece, core), piece[3]))
    for piece in class_pieces:
        last[5] = len(spreads)
        spreads.append(Spread(courier, class_view(piece, core), piece[3]))

    def begin(position):
        if position in ready:
            index = ready[position]
            arriving[index].wait_recv()
            half = pairs[index].shape[1]
            across = pl.ds(pl.multiple_of(core * half, 128), half)
            full[index][z, y, x, :, across] = pairs[index][...].astype(LOW)
        spreads[position].begin()

    lag = (-2, 0, 2, 4, 6)
    actions = (
        begin,
        lambda i: spreads[i].middle(1),
        lambda i: spreads[i].middle(2),
        lambda i: spreads[i].middle(3),
        lambda i: spreads[i].done(),
    )
    turns = iter(range(lag[0], len(spreads) + lag[-1]))
    gathered = [0]

    def turn(times=1):
        for now in itertools.islice(turns, times):
            for late, action in zip(lag, actions):
                if 0 <= now - late < len(spreads):
                    action(now - late)
            gathered[0] = now - lag[-1] + 1

    def until(index):
        while gathered[0] <= last[index]:
            turn()

    turn(3)
    for pack in range(layer.packs):
        layer.place_rows(pack)
        turn()
    until(0)
    layer.read_vectors()
    for pack in range(layer.packs):
        layer.embed(pack)
        turn()
    until(1)
    for pack in range(layer.packs):
        layer.project(pack)
        layer.attend(pack)
        turn()
    until(2)
    for pack in range(layer.packs):
        layer.join(pack)
    turn()
    until(3)
    tiles = layer.hidden_units // 256
    loop(tiles, layer.widen)
    turn()
    until(4)
    loop(layer.width // 256, layer.narrow)
    until(5)

    for pack in range(layer.packs):
        layer.classify(pack)
    courier.finish()
    layer.class_back()
    left = {index: sum(piece[0] == index for piece in pieces) for index in order}
    closing = {}

    def keep(piece):
        index, rows, columns, _ = piece

        def finish(total):
            pairs[index][pl.ds(*rows), pl.ds(*columns)] = total
            left[index] -= 1
            if left[index]:
                return
            count, half = owned[index].shape[0], owned[index].shape[1] // CORES
            across = pl.ds(pl.multiple_of(core * half, 128), half)
            other = pairs[index].at[pl.ds(pl.multiple_of((1 - core) * count, 8), count)]
            closing[index] = courier.start("c", 1, other, owned[index].at[:, across])
            owned[index][:, across] = pairs[index][pl.ds(pl.multiple_of(core * count, 8), count)]

        return finish

    def keep_class(piece):
        def finish(total):
            r.o_cls[pl.ds(*piece[1])] = total[:, : r.o_cls.shape[1]]

        return finish

    under_way = []

    def send_class():
        padded = r.g_cls.shape[-1]
        for piece in class_pieces:
            pool = Pool(r.pool_cls, "xzy", piece[1], 0, padded, padded)

            def view(core, piece=piece):
                return class_view(piece, core)(ALL, ALL, ALL)

            fold = Fold(courier, view, piece[3], pool, keep_class(piece))
            fold.begin()
            under_way.append(fold)

    def send_matrix(index, pool_ref, at):
        mine = [piece for piece in pieces if piece[0] == index]
        stack = pool_ref.shape[-2] // mine[0][1][1]
        spots, total = [], 0
        for position, (_, rows, columns, _) in enumerate(mine):
            if position % stack == 0:
                total += columns[1]
            spots.append(((position % stack * rows[1], rows[1]), at + total - columns[1]))
        folds = []
        for piece, (rows, column) in zip(mine, spots):
            width = piece[2][1]
            pool = Pool(pool_ref, "zyx", rows, column, column + total, width)

            def view(core, piece=piece):
                return matrix_view(piece, core)(ALL, ALL, ALL)

            fold = Fold(courier, view, piece[3], pool, keep(piece))
            fold.begin()
            folds.append(fold)
        under_way.extend(folds)
        return folds

    def pump(times=1, abreast=4):
        for _ in range(times):
            for fold in list(under_way[:abreast]):
                if fold.advance():
                    under_way.remove(fold)

    def drain(folds):
        while any(fold in under_way for fold in folds):
            pump()

    def free(which):
        pl.semaphore_wait(r.free.at[which], place.tell(r.free.at[which]))

    send_class()
    loop(tiles // 2, layer.active_back)
    pump()
    loop(tiles // 2, lambda index: layer.active_back(index + tiles // 2))
    pump()
    loop(tiles, layer.down_weight)
    free(0)
    down_folds = send_matrix(4, r.active, 0)
    pump()
    for pack in range(layer.packs):
        layer.second_back(pack)
        pump()
    for part in range(layer.hidden_units // COLUMNS):
        loop(layer.width // 256, lambda index: layer.up_weight(index, part))
        pump()
    free(1)
    send_matrix(3, r.upward, 0)
    for pack in range(layer.packs):
        layer.mixed_back(pack)
    pump()
    loop(layer.width // 256, layer.out_weight)
    send_matrix(2, r.pool_out, 0)
    for pack in range(layer.packs):
        layer.attend_back(pack)
        pump()
    for pack in range(layer.packs):
        layer.first_back(pack)
        pump()
    loop(layer.width // 256, layer.qkv_weight)
    drain(down_folds)
    courier.sent([copy for fold in down_folds for copy in fold.copies])
    free(2)
    half = full[1].shape[-1] // CORES
    send_matrix(1, r.active, 0)
    layer.embed_weight()
    send_matrix(0, r.active, 2 * half)
    layer.head_gains()
    lanes = iota((1, layer.width), 1)
    devices = dims["x"] * dims["y"] * dims["z"] * CORES
    r.vgrad[6:7] += jnp.where(lanes == 1.0, r.weight_sum[:, :1] / devices, 0.0)

    strips = []
    at = 0
    for index in order:
        rows, wide = shards[index].shape
        for low in range(0, wide, COLUMNS):
            strips.append((index, pl.ds(low, COLUMNS), rows, at))
            at += rows
    total_rows = at
    moments = [
        (r.m_embed, r.v_embed), (r.m_qkv, r.v_qkv), (r.m_out, r.v_out), (r.m_up, r.v_up),
        (r.m_down, r.v_down), (r.m_vectors, r.v_vectors), (r.m_cls, r.v_cls),
    ]
    outs = [
        (r.embed_new, r.embed_first, r.embed_second), (r.qkv_new, r.qkv_first, r.qkv_second),
        (r.out_new, r.out_first, r.out_second), (r.up_new, r.up_first, r.up_second),
        (r.down_new, r.down_first, r.down_second),
        (r.vectors_new, r.vectors_first, r.vectors_second), (r.cls_new, r.cls_first, r.cls_second),
    ]
    loads = []
    for position, (index, columns, rows, at) in enumerate(strips):
        for which in range(2):
            loads.append(
                pltpu.make_async_copy(
                    moments[index][which].at[:, columns],
                    r.stream.at[pl.ds(at + which * total_rows, rows)],
                    r.local.at[len(loads)],
                )
            )
            loads[-1].start()
    vec_total = Total(courier, (r.vec_c, r.vec_x, r.vec_y, r.vec_z))
    vec_total.send("c", r.vgrad[...])
    for before, after in zip("cxyz", "xyz "):
        pump()
        vec_sum = vec_total.receive(before)
        if after != " ":
            vec_total.send(after, vec_sum)
    while under_way:
        pump()
    for index in order:
        closing[index].wait_recv()
    for load in loads:
        load.wait()

    vec_count = r.vectors.shape[1]
    device = ((z * dims["y"] + y) * dims["x"] + x) * CORES + core
    at_row = lax.broadcasted_iota(jnp.int32, (layer.width, 128), 0)
    at_lane = lax.broadcasted_iota(jnp.int32, (layer.width, 128), 1)
    chosen = ((at_row == device * vec_count + at_lane) & (at_lane < vec_count)).astype(FULL)
    picked = jnp.dot(vec_sum, chosen, precision=highest, preferred_element_type=FULL)
    vec_grad = picked[:6, :vec_count]
    mats = list(zip(owned + [r.o_cls], shards + [r.w_cls]))
    parts = [squares(grad[...]) for grad, _ in mats] + [squares(weight[...]) for _, weight in mats]
    block = jnp.concatenate(parts + [wide_rows(r.vectors[...]), jnp.zeros((6, 128), FULL)], axis=0)
    block = Total(courier, (r.one_c, r.one_x, r.one_y, r.one_z)).through(block)
    sums = row_sum(block)
    vec_squares = row_sum(vec_sum * vec_sum)
    r.loss[...] = vec_sum[6:7, :2]
    clip_norm = jnp.sqrt(column_sum(sums[:6]) + column_sum(vec_squares[:6]))
    r.clip[...] = clip_norm
    factor = jnp.minimum(1.0, clip_limit / clip_norm)
    partial = {index: jnp.zeros((1, 128), FULL) for index in order}
    stores = []

    def store(source, target):
        copy = pltpu.make_async_copy(source, target, r.local.at[len(loads) + len(stores)])
        copy.start()
        stores.append(copy)

    for index, columns, rows, at in strips:
        spot = [pl.ds(at + which * total_rows, rows) for which in range(2)]
        first, second = moments_step(
            owned[index][:, columns] * factor, r.stream[spot[0]], r.stream[spot[1]]
        )
        update = update_of(first, second, shards[index][:, columns])
        owned[index][:, columns] = update
        partial[index] = partial[index] + squares(update)
        for which, value in enumerate((first, second)):
            r.stream[spot[which]] = value
            store(r.stream.at[spot[which]], outs[index][1 + which].at[:, columns])
    first, second = moments_step(r.o_cls[...] * factor, r.m_cls[...], r.v_cls[...])
    r.cls_first[...], r.cls_second[...] = first, second
    class_update = update_of(first, second, r.w_cls[...])
    r.o_cls[...] = class_update
    first, second = moments_step(vec_grad * factor, r.m_vectors[...], r.v_vectors[...])
    r.vectors_first[...], r.vectors_second[...] = first, second
    vec_update = update_of(first, second, r.vectors[...])
    parts = [partial[index] for index in order] + [squares(class_update), wide_rows(vec_update)]
    block = jnp.concatenate(parts + [jnp.zeros((4, 128), FULL)], axis=0)
    block = Total(courier, (r.two_c, r.two_x, r.two_y, r.two_z)).through(block)
    grown = jnp.sqrt(row_sum(block))[:12]
    weight_norms = jnp.sqrt(sums[6:18])
    r.norms[:, 0:1] = weight_norms
    r.norms[:, 1:2] = grown
    ratios = learn_rate * (weight_norms / grown)
    for index, columns, rows, at in strips:
        update = owned[index][:, columns]
        owned[index][:, columns] = shards[index][:, columns] - ratios[index : index + 1] * update
        store(owned[index].at[:, columns], outs[index][0].at[:, columns])
    r.cls_new[...] = r.w_cls[...] - ratios[5:6] * r.o_cls[...]
    r.vectors_new[...] = r.vectors[...] - ratios[6:12] * vec_update
    for copy in stores:
        copy.wait()
    courier.finish()


WEIGHTS = ("embed", "qkv", "out", "up", "down", "vectors", "cls")


def kernel_body(
    dims, patches, heights, widths, labels, res_weights, *params_moments
):
    X, Y, Z = (dims[axis] for axis in "xyz")
    params, moments = params_moments[:7], params_moments[7:]
    mats, w_cls = params[:5], params[6]
    blocks = [(CORES * w.shape[0], w.shape[1] // CORES) for w in mats]
    pieces = pieces_of(blocks)
    padded = -(-w_cls.shape[1] // 128) * 128
    class_rows = w_cls.shape[0]
    class_pieces = [
        (5, rows, columns, ("xy", "yx")[turn])
        for turn, (rows, columns) in enumerate(cut(class_rows, padded, 2))
    ]
    packs, tokens, width = patches.shape
    rows = packs * tokens
    chips = X * Y * Z
    hidden_units = mats[3].shape[1]
    heads = width // HEAD
    images = packs * heights.shape[1]
    vmem = pl.BlockSpec(memory_space=pltpu.VMEM)
    anywhere = pl.BlockSpec(memory_space=pl.ANY)
    inputs = {"patches": patches.reshape(rows, width), "heights": heights, "widths": widths}
    inputs.update(labels=labels, weights=res_weights)
    specs = [vmem] * 5
    for name, param in zip(WEIGHTS, params):
        inputs["vectors" if name == "vectors" else "w_" + name] = param
        specs.append(vmem)
    for position, name in enumerate(WEIGHTS):
        inputs["m_" + name], inputs["v_" + name] = moments[2 * position : 2 * position + 2]
        specs += [anywhere if position < 5 else vmem] * 2
    outs = {"loss": (1, 2), "clip": (1, 1), "norms": (12, 2)}
    out_specs = [vmem] * 3
    for position, (name, param) in enumerate(zip(WEIGHTS, params)):
        for kind in ("_new", "_first", "_second"):
            outs[name + kind] = param.shape
            out_specs.append(anywhere if position < 5 else vmem)
    scratch = {}
    for name, param, block in zip(WEIGHTS, mats, blocks):
        scratch["g_" + name] = pltpu.VMEM((Z, Y, X, block[0], param.shape[1]), LOW)
        scratch["p_" + name] = pltpu.VMEM(block, FULL)
        scratch["o_" + name] = pltpu.VMEM(param.shape, FULL)
    scratch["o_cls"] = pltpu.VMEM(w_cls.shape, FULL)
    scratch["g_cls"] = pltpu.VMEM((X, CORES, Z, Y, class_rows, padded), LOW)
    scratch["g_vec"] = pltpu.VMEM((Z, Y, X, CORES, 8, 128), FULL)
    scratch["pool_cls"] = pltpu.VMEM((X, Z, Y, class_rows, 2 * padded), LOW)
    scratch["pool_out"] = pltpu.VMEM((Z, Y, X) + (blocks[2][0], 2 * blocks[2][1]), LOW)
    low_rows = ("normed", "hidden", "shape_first", "shape_second", "low")
    scratch.update({name: pltpu.VMEM((rows, width), LOW) for name in low_rows})
    scratch["pos"] = pltpu.VMEM((rows, 2 * POS), LOW)
    scratch["cols"] = pltpu.VMEM((rows, 128), FULL)
    scratch["segment"] = pltpu.VMEM((packs, tokens), FULL)
    scratch["stream"] = pltpu.VMEM((rows, width), FULL)
    scratch["turned"] = pltpu.VMEM((width, tokens), FULL)
    scratch["joined"] = pltpu.VMEM((3 * width, rows), LOW)
    scratch["shape_heads"] = pltpu.VMEM((2 * width, rows), LOW)
    scratch["scale_heads"] = pltpu.VMEM((2 * heads, rows), FULL)
    scratch["log_total"] = pltpu.VMEM((heads, rows), FULL)
    scratch["mixed"] = pltpu.VMEM((width, rows), LOW)
    scratch["mask"] = pltpu.VMEM((tokens, tokens), FULL)
    wide = (Z, Y, X, rows // chips, hidden_units)
    scratch["upward"], scratch["active"] = pltpu.VMEM(wide, LOW), pltpu.VMEM(wide, LOW)
    scratch["vec"], scratch["vgrad"] = pltpu.VMEM((8, width), FULL), pltpu.VMEM((8, width), FULL)
    scratch["gains"] = pltpu.VMEM((width, 8), FULL)
    scratch["gacc"] = pltpu.VMEM((2 * width, 128), FULL)
    scratch["weight_sum"] = pltpu.VMEM((1, 128), FULL)
    scratch["pooled"] = pltpu.VMEM((images, width), LOW)
    for name in ("pool_heads", "score_heads"):
        scratch[name] = pltpu.VMEM((16, tokens), FULL)
    for name in ("image_high", "image_rest"):
        scratch[name] = pltpu.VMEM((heights.shape[1], width), LOW)
    scratch["logit_grad"] = pltpu.VMEM((images, X * CORES * padded), LOW)
    for name, shape in (("vec_", (8, width)), ("one_", (24, 128)), ("two_", (16, 128))):
        for axis, slots in zip("cxyz", total_slots(dims, shape)):
            scratch[name + axis] = slots
    peers = (X - 1) + (Y - 1) + (Z - 1) + 1
    count = (len(pieces) + len(class_pieces)) * (2 * peers + X - 1 + Y - 1)
    count += 10 + 3 * peers + 2 * peers
    scratch["send"] = pltpu.SemaphoreType.DMA((count,))
    scratch["recv"] = pltpu.SemaphoreType.DMA((count,))
    scratch["local"] = pltpu.SemaphoreType.DMA((5 * sum(w.shape[1] // COLUMNS for w in mats),))
    scratch["free"] = pltpu.SemaphoreType.REGULAR((3,))
    names = list(inputs) + list(outs) + list(scratch)
    loss_terms, clip_norm, *updated = pl.pallas_call(
        functools.partial(kernel, dims, names, pieces, class_pieces),
        out_shape=[jax.ShapeDtypeStruct(shape, FULL) for shape in outs.values()],
        in_specs=specs,
        out_specs=out_specs,
        scratch_shapes=list(scratch.values()),
        compiler_params=pltpu.CompilerParams(
            collective_id=0, has_side_effects=True, vmem_limit_bytes=(64 << 20) - 4096
        ),
    )(*inputs.values())
    return (loss_terms.reshape(2), clip_norm.reshape(()), *updated)


def chip_dims(mesh):
    across, along = mesh.shape["mp"] // CORES, mesh.shape["dp"]
    return {"x": across, "y": across, "z": along // across}


def fits(mesh, width):
    devices = mesh.shape["dp"] * mesh.shape["mp"]
    dims = chip_dims(mesh)
    same = dims["x"] * dims["y"] * dims["z"] * CORES == devices
    return same and width % (8 * devices) == 0 and width // devices * CORES % 16 == 0


def solution(mesh):
    placed = (
        P(None, ("dp", "mp"), None),
        P(None, ("dp", "mp")),
        P(None, ("dp", "mp")),
        P(None, "dp"),
        P(None, "dp"),
        P(("dp", "mp"), None),
        P(("dp", "mp"), None),
        P(("dp", "mp"), None),
        P(("dp", "mp"), None),
        P(("dp", "mp"), None),
        P(None, ("dp", "mp")),
        P("dp", "mp"),
        P(("dp", "mp"), None),
        P(("dp", "mp"), None),
        P(("dp", "mp"), None),
        P(("dp", "mp"), None),
        P(("dp", "mp"), None),
        P(("dp", "mp"), None),
        P(("dp", "mp"), None),
        P(("dp", "mp"), None),
        P(("dp", "mp"), None),
        P(("dp", "mp"), None),
        P(None, ("dp", "mp")),
        P(None, ("dp", "mp")),
        P("dp", "mp"),
        P("dp", "mp"),
    )
    run = body
    if fits(mesh, 768):
        run = functools.partial(kernel_body, chip_dims(mesh))
    return jax.shard_map(
        run,
        mesh=mesh,
        in_specs=placed,
        out_specs=(
            P(),
            P(),
            P(),
            P(("dp", "mp"), None),
            P(("dp", "mp"), None),
            P(("dp", "mp"), None),
            P(("dp", "mp"), None),
            P(("dp", "mp"), None),
            P(("dp", "mp"), None),
            P(("dp", "mp"), None),
            P(("dp", "mp"), None),
            P(("dp", "mp"), None),
            P(("dp", "mp"), None),
            P(("dp", "mp"), None),
            P(("dp", "mp"), None),
            P(("dp", "mp"), None),
            P(("dp", "mp"), None),
            P(("dp", "mp"), None),
            P(None, ("dp", "mp")),
            P(None, ("dp", "mp")),
            P(None, ("dp", "mp")),
            P("dp", "mp"),
            P("dp", "mp"),
            P("dp", "mp"),
        ),
        check_vma=False,
    )
```

```python
import functools
import itertools
import types

import jax
import jax.numpy as jnp
from jax import lax
from jax.experimental import pallas as pl
from jax.experimental.pallas import tpu as pltpu
from jax.sharding import PartitionSpec as P

HEAD = 64
POS = 128
STEP = 10


epsilon = 1e-06
clip_limit = 0.01
learn_rate = 0.3
beta_first = 0.9
beta_second = 0.999
weight_decay = 0.01
adam_floor = 1e-08
highest = lax.Precision.HIGHEST
excluded = -1e30


def merged_2(part, axis, combine):
    gathered = jax.tree.map(lambda a: lax.all_gather(a, axis), part)

    def take(source):
        return jax.tree.map(lambda a: lax.dynamic_index_in_dim(a, source, 0, False), gathered)

    return lax.fori_loop(
        1, lax.axis_size(axis), lambda source, state: combine(state, take(source)), take(0)
    )


def layer_norm(values, scales):
    center = values - jnp.mean(values, axis=-1, keepdims=True)
    spread = jnp.mean(center * center, axis=-1, keepdims=True)
    return center * lax.rsqrt(spread + epsilon) * scales


def norm_back(values, scales, upstream):
    result, pullback = jax.vjp(layer_norm, values, scales)
    return pullback(upstream)


def outer_dot(left, right):
    return lax.dot_general(
        left, right, (((0,), (0,)), ((), ())), preferred_element_type=jnp.float32
    )


def inner_dot(left, right):
    return lax.dot_general(
        left, right, (((1,), (1,)), ((), ())), preferred_element_type=jnp.float32
    )


def layout(heights, widths, row_count):
    lengths = heights * widths
    image_ends = jnp.cumsum(lengths)
    starts = image_ends - lengths
    places = jnp.arange(row_count, dtype=jnp.int32)
    slot_ids = jnp.arange(heights.shape[0], dtype=jnp.int32)
    segment = jnp.sum((places[:, None] >= image_ends[None, :]).astype(jnp.int32), axis=1)
    member = segment[None, :] == slot_ids[:, None]
    member_int = member.T.astype(jnp.int32)
    within = places - jnp.sum(member_int * starts[None, :], axis=1)
    across = jnp.maximum(jnp.sum(member_int * widths[None, :], axis=1), 1)
    upright = jnp.maximum(jnp.sum(member_int * heights[None, :], axis=1), 1)
    col_pos = within % across * POS // across
    row_pos = within // across * POS // upright
    pos_table = jnp.arange(POS, dtype=jnp.int32)
    pos_rows = jnp.concatenate(
        [col_pos[:, None] == pos_table[None, :], row_pos[:, None] == pos_table[None, :]], axis=1
    )
    return (segment, member, pos_rows)


def block_scores(queries, key_rows, segment):
    scores = jnp.einsum(
        "thd,shd->hts", queries, key_rows, preferred_element_type=jnp.float32
    ) * HEAD ** (-0.5)
    same_image = segment[:, None] == segment[None, :]
    return (queries, jnp.where(same_image[None], scores, excluded))


def attend(queries, key_rows, value_rows, segment):
    block_rows = min(512, queries.shape[0])

    def one_block(block_index):
        query_block, scores = block_scores(queries, key_rows, segment)
        top_score = jnp.max(scores, axis=-1, keepdims=True)
        exp_scores = jnp.exp(scores - top_score)
        exp_total = jnp.sum(exp_scores, axis=-1, keepdims=True)
        attention = (exp_scores / exp_total).astype(jnp.bfloat16)
        result = jnp.einsum(
            "hts,shd->thd", attention, value_rows, preferred_element_type=jnp.float32
        )
        return (result.astype(jnp.bfloat16), (top_score + jnp.log(exp_total))[..., 0])

    mixed_heads, log_total = lax.map(one_block, jnp.arange(queries.shape[0] // block_rows))
    return (mixed_heads.reshape(queries.shape), log_total)


def attend_back(queries, key_rows, value_rows, segment, log_total, mixed_grad):
    block_rows = min(512, queries.shape[0])

    def one_block(running, block_index):
        key_grad, value_grad = running
        query_block, scores = block_scores(queries, key_rows, segment)
        attention = jnp.exp(scores - log_total[block_index][..., None])
        value_grad = value_grad + jnp.einsum(
            "hts,thd->shd",
            attention.astype(jnp.bfloat16),
            mixed_grad,
            preferred_element_type=jnp.float32,
        )
        prob_grad = jnp.einsum(
            "thd,shd->hts", mixed_grad, value_rows, preferred_element_type=jnp.float32
        )
        score_grad = (
            attention * (prob_grad - jnp.sum(attention * prob_grad, axis=-1, keepdims=True))
        ).astype(jnp.bfloat16)
        query_grad = jnp.einsum(
            "hts,shd->thd", score_grad, key_rows, preferred_element_type=jnp.float32
        ) * HEAD ** (-0.5)
        key_grad = key_grad + jnp.einsum(
            "hts,thd->shd", score_grad, query_block, preferred_element_type=jnp.float32
        ) * HEAD ** (-0.5)
        return ((key_grad, value_grad), query_grad)

    zero_grad = jnp.zeros(key_rows.shape, jnp.float32)
    sums, query_grad = lax.scan(
        one_block, (zero_grad, zero_grad), jnp.arange(queries.shape[0] // block_rows)
    )
    return (query_grad.reshape(queries.shape), sums[0], sums[1])


def layer_forward(weights_low, vector_low, patch_rows, heights, widths):
    embed, joined_w, out_w, up_w, down_w = weights_low
    vectors = vector_low.astype(jnp.float32)
    row_count, pixel_count = patch_rows.shape
    model_width = embed.shape[1]
    head_count = model_width // HEAD
    head_shape = (row_count, head_count, HEAD)
    segment, member, pos_rows = layout(heights, widths, row_count)
    pos_low = pos_rows.astype(jnp.bfloat16)
    embedded = jnp.dot(
        patch_rows, embed[:pixel_count], preferred_element_type=jnp.float32
    ) + jnp.dot(pos_low, embed[pixel_count:], preferred_element_type=jnp.float32)
    normed = layer_norm(embedded, vectors[0]).astype(jnp.bfloat16)
    joined = jnp.dot(normed, joined_w, preferred_element_type=jnp.float32)
    query_pre = joined[:, :model_width].reshape(head_shape)
    key_pre = joined[:, model_width : 2 * model_width].reshape(head_shape)
    queries = layer_norm(query_pre, vectors[3].reshape(head_count, HEAD)).astype(jnp.bfloat16)
    key_rows = layer_norm(key_pre, vectors[4].reshape(head_count, HEAD)).astype(jnp.bfloat16)
    value_rows = joined[:, 2 * model_width :].reshape(head_shape).astype(jnp.bfloat16)
    mixed_heads, log_total = attend(queries, key_rows, value_rows, segment)
    mixed_flat = mixed_heads.reshape(row_count, model_width)
    second = embedded + jnp.dot(mixed_flat, out_w, preferred_element_type=jnp.float32)
    hidden = layer_norm(second, vectors[1]).astype(jnp.bfloat16)
    upward = jnp.dot(hidden, up_w, preferred_element_type=jnp.float32)
    active = jax.nn.gelu(upward).astype(jnp.bfloat16)
    residual = second + jnp.dot(active, down_w, preferred_element_type=jnp.float32)
    final_heads = layer_norm(residual, vectors[2]).astype(jnp.bfloat16).reshape(head_shape)
    probe_low = vector_low[5].reshape(head_count, HEAD)
    probe_scores = jnp.einsum(
        "thd,hd->th", final_heads, probe_low, preferred_element_type=jnp.float32
    ) * HEAD ** (-0.5)
    masked = jnp.where(member[:, :, None], probe_scores[None], excluded)
    pooling = jax.nn.softmax(masked, axis=1) * member[:, :, None].astype(jnp.float32)
    pool_low = pooling.astype(jnp.bfloat16)
    pooled = jnp.einsum("ith,thd->ihd", pool_low, final_heads, preferred_element_type=jnp.float32)
    saved = (
        patch_rows,
        pos_low,
        member,
        segment,
        embedded,
        normed,
        query_pre,
        key_pre,
        queries,
        key_rows,
        value_rows,
        log_total,
        mixed_flat,
        second,
        hidden,
        upward,
        active,
        residual,
        final_heads,
        pooling,
        pool_low,
    )
    return (pooled.reshape(-1, model_width).astype(jnp.bfloat16), saved)


def layer_backward(weights_low, vector_low, saved, pooled_grad):
    (
        patch_rows,
        pos_low,
        member,
        segment,
        embedded,
        normed,
        query_pre,
        key_pre,
        queries,
        key_rows,
        value_rows,
        log_total,
        mixed_flat,
        second,
        hidden,
        upward,
        active,
        residual,
        final_heads,
        pooling,
        pool_low,
    ) = saved
    embed, joined_w, out_w, up_w, down_w = weights_low
    vectors = vector_low.astype(jnp.float32)
    row_count, head_count = (final_heads.shape[0], final_heads.shape[1])
    model_width = head_count * HEAD
    image_grad = pooled_grad.reshape(-1, head_count, HEAD)
    final_wide = final_heads.astype(jnp.float32)
    weight_grad = jnp.einsum("ihd,thd->ith", image_grad, final_wide, precision=highest) * member[
        :, :, None
    ].astype(jnp.float32)
    score_grad = pooling * (weight_grad - jnp.sum(pooling * weight_grad, axis=1, keepdims=True))
    score_grad = jnp.sum(score_grad, axis=0) * HEAD ** (-0.5)
    probe = vectors[5].reshape(head_count, HEAD)
    final_grad = (
        jnp.einsum("ith,ihd->thd", pool_low.astype(jnp.float32), image_grad, precision=highest)
        + score_grad[:, :, None] * probe[None]
    )
    probe_grad = jnp.einsum("th,thd->hd", score_grad, final_wide, precision=highest)
    residual_grad, gain_final = norm_back(
        residual, vectors[2], final_grad.reshape(row_count, model_width)
    )
    down_in = residual_grad.astype(jnp.bfloat16)
    down_grad = outer_dot(active, down_in)
    active_grad = inner_dot(down_in, down_w)
    upward_grad = jax.vjp(jax.nn.gelu, upward)[1](active_grad)[0].astype(jnp.bfloat16)
    up_grad = outer_dot(hidden, upward_grad)
    second_back, gain_second = norm_back(second, vectors[1], inner_dot(upward_grad, up_w))
    second_grad = residual_grad + second_back
    out_in = second_grad.astype(jnp.bfloat16)
    out_grad = outer_dot(mixed_flat, out_in)
    mixed_grad = inner_dot(out_in, out_w).astype(jnp.bfloat16).reshape(row_count, head_count, HEAD)
    query_grad, key_grad, value_grad = attend_back(
        queries, key_rows, value_rows, segment, log_total, mixed_grad
    )
    query_back, gain_query = norm_back(query_pre, vectors[3].reshape(head_count, HEAD), query_grad)
    key_back, gain_key = norm_back(key_pre, vectors[4].reshape(head_count, HEAD), key_grad)
    joined_grad = jnp.concatenate(
        [
            query_back.reshape(row_count, model_width),
            key_back.reshape(row_count, model_width),
            value_grad.reshape(row_count, model_width),
        ],
        axis=1,
    ).astype(jnp.bfloat16)
    joined_w_grad = outer_dot(normed, joined_grad)
    first_back, gain_first = norm_back(embedded, vectors[0], inner_dot(joined_grad, joined_w))
    embed_in = (second_grad + first_back).astype(jnp.bfloat16)
    embed_grad = jnp.concatenate(
        [outer_dot(patch_rows, embed_in), outer_dot(pos_low, embed_in)], axis=0
    )
    vector_grad = jnp.stack(
        [
            gain_first,
            gain_second,
            gain_final,
            gain_query.reshape(model_width),
            gain_key.reshape(model_width),
            probe_grad.reshape(model_width),
        ]
    )
    return (embed_grad, joined_w_grad, out_grad, up_grad, down_grad, vector_grad)


def reduce_grads(fresh):
    return (
        lax.psum_scatter(fresh[0], ("dp", "mp"), scatter_dimension=0, tiled=True),
        lax.psum_scatter(fresh[1], ("dp", "mp"), scatter_dimension=0, tiled=True),
        lax.psum_scatter(fresh[2], ("dp", "mp"), scatter_dimension=0, tiled=True),
        lax.psum_scatter(fresh[3], ("dp", "mp"), scatter_dimension=0, tiled=True),
        lax.psum_scatter(fresh[4], ("dp", "mp"), scatter_dimension=0, tiled=True),
        lax.psum_scatter(fresh[5], ("dp", "mp"), scatter_dimension=1, tiled=True),
    )


def combine_stats(earlier, later_one):
    top_score = jnp.maximum(earlier[0], later_one[0])
    exp_total = earlier[1] * jnp.exp(earlier[0] - top_score) + later_one[1] * jnp.exp(
        later_one[0] - top_score
    )
    return (top_score, exp_total, earlier[2] + later_one[2])


def lamb_update(weight, gradient, moment_one, moment_two, factor):
    gradient = gradient * factor
    moment_one = beta_first * moment_one + (1.0 - beta_first) * gradient
    moment_two = beta_second * moment_two + (1.0 - beta_second) * gradient * gradient
    update = (
        moment_one
        / (1.0 - beta_first**STEP)
        / (jnp.sqrt(moment_two / (1.0 - beta_second**STEP)) + adam_floor)
        + weight_decay * weight
    )
    return (moment_one, moment_two, update)


def body(
    patches,
    heights,
    widths,
    labels,
    res_weights,
    w_embed,
    w_qkv,
    w_out,
    w_up,
    w_down,
    vectors,
    w_cls,
    m_embed,
    v_embed,
    m_qkv,
    v_qkv,
    m_out,
    v_out,
    m_up,
    v_up,
    m_down,
    v_down,
    m_vectors,
    v_vectors,
    m_cls,
    v_cls,
):
    gathered = (
        lax.all_gather(w_embed.astype(jnp.bfloat16), ("dp", "mp"), axis=0, tiled=True),
        lax.all_gather(w_qkv.astype(jnp.bfloat16), ("dp", "mp"), axis=0, tiled=True),
        lax.all_gather(w_out.astype(jnp.bfloat16), ("dp", "mp"), axis=0, tiled=True),
        lax.all_gather(w_up.astype(jnp.bfloat16), ("dp", "mp"), axis=0, tiled=True),
        lax.all_gather(w_down.astype(jnp.bfloat16), ("dp", "mp"), axis=0, tiled=True),
        lax.all_gather(vectors.astype(jnp.bfloat16), ("dp", "mp"), axis=1, tiled=True),
    )
    weights_low = gathered[:5]
    vector_low = gathered[5]
    class_low = lax.all_gather(w_cls.astype(jnp.bfloat16), "dp", axis=0, tiled=True)
    member_index = lax.axis_index("mp")
    slot_count = heights.shape[1]
    own_start = member_index * slot_count
    own_weights = lax.dynamic_slice_in_dim(res_weights, own_start, slot_count, 1).astype(
        jnp.float32
    )
    weight_sum = lax.psum(jnp.sum(own_weights), ("dp", "mp"))
    class_count = class_low.shape[1]
    class_ids = member_index * class_count + jnp.arange(class_count, dtype=jnp.int32)
    loss_local = jnp.zeros((), jnp.float32)
    class_grad = jnp.zeros(class_low.shape, jnp.float32)
    summed = None
    for micro_index in range(patches.shape[0]):
        pooled, saved = layer_forward(
            weights_low, vector_low, patches[micro_index], heights[micro_index], widths[micro_index]
        )
        group_rows = lax.all_gather(pooled, "mp", axis=0, tiled=True)
        logits = jnp.dot(group_rows, class_low, preferred_element_type=jnp.float32)
        label_hit = labels[micro_index][:, None] == class_ids[None, :]
        top_score = jnp.max(logits, axis=1)
        exp_total = jnp.sum(jnp.exp(logits - top_score[:, None]), axis=1)
        picked = jnp.sum(jnp.where(label_hit, logits, 0.0), axis=1)
        merged = merged_2((top_score, exp_total, picked), "mp", combine_stats)
        log_total = merged[0] + jnp.log(merged[1])
        group_weights = res_weights[micro_index].astype(jnp.float32)
        weighted = group_weights * (log_total - merged[2])
        loss_local = loss_local + jnp.sum(
            lax.dynamic_slice_in_dim(weighted, own_start, slot_count, 0)
        )
        logit_grad = (
            (jnp.exp(logits - log_total[:, None]) - label_hit.astype(jnp.float32))
            * (group_weights / weight_sum)[:, None]
        ).astype(jnp.bfloat16)
        class_grad = class_grad + outer_dot(group_rows, logit_grad)
        pooled_grad = lax.psum_scatter(
            inner_dot(logit_grad, class_low), "mp", scatter_dimension=0, tiled=True
        )
        fresh = layer_backward(weights_low, vector_low, saved, pooled_grad)
        summed = fresh if summed is None else jax.tree.map(jnp.add, summed, fresh)
    summed = reduce_grads(summed)
    class_shard = lax.psum_scatter(class_grad, "dp", scatter_dimension=0, tiled=True)
    params = (w_embed, w_qkv, w_out, w_up, w_down, vectors, w_cls)
    moments = (
        (m_embed, v_embed),
        (m_qkv, v_qkv),
        (m_out, v_out),
        (m_up, v_up),
        (m_down, v_down),
        (m_vectors, v_vectors),
        (m_cls, v_cls),
    )
    gradients = (summed[0], summed[1], summed[2], summed[3], summed[4], summed[5], class_shard)
    matrix_order = (0, 1, 2, 3, 4, 6)
    grad_squares = jnp.concatenate(
        [
            jnp.stack(
                [jnp.sum(gradients[position] * gradients[position]) for position in matrix_order]
            ),
            jnp.sum(gradients[5] * gradients[5], axis=1),
        ]
    )
    square_sums, loss_total = lax.psum((grad_squares, loss_local), ("dp", "mp"))
    clip_norm = jnp.sqrt(jnp.sum(square_sums))
    factor = jnp.minimum(1.0, clip_limit / clip_norm)
    updated = [
        lamb_update(
            params[position],
            gradients[position],
            moments[position][0],
            moments[position][1],
            factor,
        )
        for position in range(7)
    ]
    matrix_parts = jnp.stack(
        [
            jnp.stack(
                [
                    jnp.sum(params[position] * params[position]),
                    jnp.sum(updated[position][2] * updated[position][2]),
                ]
            )
            for position in matrix_order
        ]
    )
    vector_parts = jnp.stack(
        [jnp.sum(params[5] * params[5], axis=1), jnp.sum(updated[5][2] * updated[5][2], axis=1)],
        axis=1,
    )
    norms = jnp.sqrt(lax.psum(jnp.concatenate([matrix_parts, vector_parts], axis=0), ("dp", "mp")))
    ratios = norms[:, 0] / norms[:, 1]
    outputs = [jnp.stack([loss_total, weight_sum]), clip_norm, norms]
    for position in range(7):
        if position == 5:
            ratio = ratios[6:][:, None]
        else:
            ratio = ratios[matrix_order.index(position)]
        moment_one, moment_two, update = updated[position]
        outputs += [params[position] - learn_rate * ratio * update, moment_one, moment_two]
    return tuple(outputs)


MESH_ID = pl.DeviceIdType.MESH
CORES = 2
ALL = slice(None)
LOW = jnp.bfloat16
FULL = jnp.float32
NN = (((1,), (0,)), ((), ()))
NT = (((1,), (1,)), ((), ()))
TN = (((0,), (0,)), ((), ()))
COLUMNS = 768
SCORE_SCALE = HEAD ** (-0.5) * 1.4426950408889634
FOLD_LAG = 4
NEWEST_FIRST = 1
ENTER = 1
GATHER_LAGS = (-2, 0, 2, 4, 6)
PIECE_SIZE = 9216
MOST_PIECES = 6
WIDE = 3
ACROSS = 0
HEADS_AT_ONCE = 3
NORMS_AT_ONCE = 6
STRIP = 256


class Place:
    def __init__(self, dims):
        self.sizes = dict(dims, c=CORES)
        dp, mp = lax.axis_index("dp"), lax.axis_index("mp")
        wide = self.sizes["y"]
        self.at = {"z": dp // wide, "y": dp % wide, "x": mp // CORES, "c": mp % CORES}

    def source(self, axis, step):
        size = self.sizes[axis]
        return (self.at[axis] + (size - step) % size) % size

    def peer(self, steps):
        at = {axis: self.source(axis, -steps.get(axis, 0)) for axis in "zyxc"}
        return (at["z"] * self.sizes["y"] + at["y"], at["x"] * CORES + at["c"])

    def steps(self, axis):
        return range(1, self.sizes[axis])

    def lines(self):
        return [{axis: step} for axis in "cxyz" for step in self.steps(axis)]

    def plane(self):
        ranges = (range(self.sizes[axis]) for axis in "yxc")
        return [dict(zip("yxc", steps)) for steps in itertools.product(*ranges) if any(steps)]

    def tell(self, semaphore, peers):
        for steps in peers:
            pl.semaphore_signal(
                semaphore, inc=1, device_id=self.peer(steps), device_id_type=MESH_ID
            )
        return len(peers)


class Courier:
    def __init__(self, place, send, recv):
        self.place, self.send, self.recv, self.open, self.count = place, send, recv, [], 0

    def start(self, steps, source, target):
        slot = self.count
        self.count += 1
        copy = pltpu.make_async_remote_copy(
            src_ref=source,
            dst_ref=target,
            send_sem=self.send.at[slot],
            recv_sem=self.recv.at[slot],
            device_id=self.place.peer(steps),
            device_id_type=MESH_ID,
        )
        copy.start()
        self.open.append(copy)
        return copy

    def sent(self, copies):
        for copy in copies:
            copy.wait_send()
            self.open = [other for other in self.open if other is not copy]

    def finish(self):
        self.sent(list(self.open))


class Spread:
    def __init__(self, courier, view, order):
        self.courier, self.place, self.view, self.order = courier, courier.place, view, order
        self.relayed = []

    def part(self, stage, **fixed):
        where = {axis: self.place.at[axis] for axis in "xyz"}
        for axis in self.order[:stage]:
            where[axis] = ALL
        where.update(fixed)
        return self.view(**where)

    def send(self, stage):
        axis, part = self.order[stage], self.part(stage)
        self.coming = [
            self.courier.start({axis: step}, part, part) for step in self.place.steps(axis)
        ]

    def relay(self, part):
        self.relayed.append(self.courier.start({"c": 1}, part, part))

    def begin(self):
        self.send(0)

    def middle(self, stage):
        for copy in self.coming:
            copy.wait_recv()
        if stage < 3:
            self.send(stage)
        if stage == 1:
            self.relay(self.part(1))
            return
        axis = self.order[stage - 1]
        for step in self.place.steps(axis):
            self.relay(self.part(stage - 1, **{axis: self.place.source(axis, step)}))

    def done(self):
        for copy in self.relayed:
            copy.wait_recv()


class Pool:
    def __init__(self, ref, axes, rows, held, rest, width):
        self.ref, self.axes, self.rows, self.marks, self.width = ref, axes, rows, (held, rest), width

    def at(self, half, **where):
        key = tuple(where.get(axis, ALL) for axis in self.axes)
        return self.ref.at[key + (pl.ds(*self.rows), pl.ds(self.marks[half], self.width))]


class Fold:
    def __init__(self, courier, view, order, pool, finish):
        self.courier, self.place, self.view, self.order = courier, courier.place, view, order
        self.pool, self.finish, self.copies, self.stage, self.due = pool, finish, [], 0, None

    def start(self, axis, step, source, target):
        copy = self.courier.start({axis: step}, source, target)
        self.copies.append(copy)
        self.coming.append(copy)

    def landing(self, stage, step):
        where = {axis: self.place.sizes[axis] - 1 for axis in self.order[: stage - 1]}
        where[self.order[stage - 1]] = step - 1
        return self.pool.at(1, **where)

    def send(self, stage):
        axis = self.order[stage - 1]
        fixed = place_of(self.place, self.order[: stage - 1])
        self.coming = []
        for step in self.place.steps(axis):
            source = self.pool.at(0, **{axis: self.place.source(axis, -step)}, **fixed)
            self.start(axis, step, source, self.landing(stage, step))

    def begin(self):
        self.coming = []
        self.start("c", 1, self.view(1 - self.place.at["c"]), self.pool.at(0))

    def advance(self):
        for copy in self.coming:
            copy.wait_recv()
        stage, place = self.stage, self.place
        self.stage += 1
        if stage == 3:
            here = self.pool.at(0, **place_of(place, self.order))
            total = here[...].astype(FULL)
            for step in place.steps(self.order[2]):
                total = total + self.landing(3, step)[...].astype(FULL)
            self.finish(total)
            return True
        here = self.pool.at(0, **place_of(place, self.order[:stage]))
        if stage == 0:
            came = [self.view(place.at["c"])]
        else:
            came = [self.landing(stage, step) for step in place.steps(self.order[stage - 1])]

        def one(lead, carry):
            total = here[lead].astype(FULL)
            for part in came:
                total = total + part[lead].astype(FULL)
            here[lead] = total.astype(LOW)
            return carry

        lax.fori_loop(0, here.shape[0], one, 0)
        self.send(stage + 1)
        return False


def place_of(place, axes):
    return {axis: place.at[axis] for axis in axes}


class Total:
    def __init__(self, courier, plane_slots, line_slots):
        self.courier, self.place = courier, courier.place
        self.stages = [
            (plane_slots, self.place.plane()),
            (line_slots, [{"z": step} for step in self.place.steps("z")]),
        ]

    def send(self, stage, block):
        slots, peers = self.stages[stage]
        at, sizes = self.place.at, self.place.sizes
        index = at["z"] if stage else (at["y"] * sizes["x"] + at["x"]) * CORES + at["c"]
        mine = slots.at[index]
        mine[...] = block
        self.coming = [self.courier.start(steps, mine, mine) for steps in peers]

    def receive(self, stage):
        for copy in self.coming:
            copy.wait_recv()
        slots = self.stages[stage][0]
        total = slots[0]
        for index in range(1, slots.shape[0]):
            total = total + slots[index]
        return total

    def through(self, block):
        for stage in range(2):
            self.send(stage, block)
            block = self.receive(stage)
        return block


def cut_rows(rows, width, parts):
    size = rows // parts
    return [((part * size, size), (0, width)) for part in range(parts)]


def cut(rows, width, parts):
    units = width // 128
    if units % parts and rows % (16 * parts) == 0:
        return cut_rows(rows, width, parts)
    marks = [units * part // parts * 128 for part in range(parts + 1)]
    return [((0, rows), (low, high - low)) for low, high in zip(marks, marks[1:]) if high > low]


def pieces_of(blocks):
    found = []
    for index, (rows, width) in enumerate(blocks):
        parts = max(2, min(MOST_PIECES, rows * width // PIECE_SIZE))
        for row_range, column_range in cut(rows, width, parts):
            found.append((index, row_range, column_range, ("zxy", "zyx")[len(found) % 2]))
    across = [at for at, piece in enumerate(found) if piece[0] == WIDE][:ACROSS]
    for turn, at in enumerate(across):
        found[at] = found[at][:3] + (("xyz", "yxz")[turn % 2],)
    return found


def dot(left, right, form=NN):
    return lax.dot_general(left, right, form, preferred_element_type=FULL)


def halves(values):
    high = values.astype(LOW)
    return high, (values - high.astype(FULL)).astype(LOW)


def fine_dot(left, values, form):
    high, rest = halves(values)
    return dot(left, high, form) + dot(left, rest, form)


def iota(shape, axis):
    return lax.broadcasted_iota(jnp.int32, shape, axis).astype(FULL)


def normal(values, axis):
    center = values - jnp.mean(values, axis=axis, keepdims=True)
    scale = lax.rsqrt(jnp.mean(center * center, axis=axis, keepdims=True) + epsilon)
    return center * scale, scale


def normal_back(upstream, shape, scale, axis):
    mean = jnp.mean(upstream, axis=axis, keepdims=True)
    along = jnp.mean(upstream * shape, axis=axis, keepdims=True)
    return scale * (upstream - mean - shape * along)


def column_sum(values):
    return jnp.sum(values, axis=0, keepdims=True)


def row_sum(values):
    return jnp.sum(values, axis=1, keepdims=True)


def squares(values):
    total = jnp.zeros((1, 128), FULL)
    for low in range(0, values.shape[1], 128):
        part = values[:, low : low + 128]
        part = column_sum(part * part)
        if part.shape[1] < 128:
            part = jnp.concatenate([part, jnp.zeros((1, 128 - part.shape[1]), FULL)], axis=1)
        total = total + part
    return total


def wide_rows(values):
    squared = values * values
    rest = jnp.zeros((squared.shape[0], 128 - squared.shape[1]), FULL)
    return jnp.concatenate([squared, rest], axis=1)


def moments_step(gradient, moment_one, moment_two):
    first = beta_first * moment_one + (1.0 - beta_first) * gradient
    second = beta_second * moment_two + (1.0 - beta_second) * gradient * gradient
    return first, second


def update_of(first, second, weight):
    return (
        first
        / (1.0 - beta_first**STEP)
        / (jnp.sqrt(second / (1.0 - beta_second**STEP)) + adam_floor)
        + weight_decay * weight
    )


def loop(count, body):
    def one(index, carry):
        body(index)
        return carry

    lax.fori_loop(0, count, one, 0)


def tile(index, size):
    return pl.ds(pl.multiple_of(index * size, size), size)


class Layer:
    def __init__(self, r, place, dims):
        self.r, self.place = r, place
        self.rows, self.width = r.patches.shape
        self.packs, self.slots = r.heights.shape
        self.tokens = self.rows // self.packs
        self.head_count = self.width // HEAD
        self.hidden_units = r.g_up.shape[-1]
        self.groups = dims["x"] * CORES
        self.member_index = place.at["x"] * CORES + place.at["c"]
        self.w_embed = r.g_embed.reshape(-1, self.width)
        self.w_qkv = r.g_qkv.reshape(self.width, 3 * self.width)
        self.w_out = r.g_out.reshape(self.width, self.width)
        self.w_up = r.g_up.reshape(self.width, self.hidden_units)
        self.w_down = r.g_down.reshape(self.hidden_units, self.width)
        self.upward = r.upward.reshape(self.rows, self.hidden_units)
        self.active = r.active.reshape(self.rows, self.hidden_units)
        self.joined = r.joined.reshape(3 * self.width, self.rows)
        self.shape_heads = r.shape_heads.reshape(2 * self.width, self.rows)
        self.shape_second = r.shape_second.reshape(self.rows, self.width)

    def span(self, pack):
        return pl.ds(pack * self.tokens, self.tokens)

    def gain(self, row):
        return self.r.vec[row : row + 1]

    def class_block(self, group):
        block = self.r.g_cls.at[group // CORES, group % CORES]
        return block.reshape(self.width, block.shape[-1])

    def head_marks(self):
        return (
            jnp.floor((iota((16, self.width), 1) + 0.5) / HEAD) == iota((16, self.width), 0)
        ).astype(FULL)

    def place_rows(self, pack):
        r, tokens, slots = self.r, self.tokens, self.slots
        high = r.heights[pack : pack + 1].astype(FULL)
        wide = r.widths[pack : pack + 1].astype(FULL)
        lengths = high * wide
        square = (slots, slots)
        below, beside = iota(square, 0), iota(square, 1)
        ends_column = row_sum(jnp.where(beside <= below, lengths, 0.0))
        length_column = row_sum(jnp.where(beside == below, lengths, 0.0))
        ends = column_sum(jnp.where(below <= beside, length_column, 0.0))
        spots = iota((tokens, slots), 0)
        segment = row_sum((spots >= ends).astype(FULL))
        member = (iota((tokens, slots), 1) == segment).astype(FULL)
        within = spots[:, :1] - row_sum(member * (ends - lengths))
        across = jnp.maximum(row_sum(member * wide), 1.0)
        upright = jnp.maximum(row_sum(member * high), 1.0)
        line = jnp.floor((within + 0.5) / across)
        column = within - line * across
        table = iota((tokens, POS), 1)
        span = self.span(pack)
        r.pos[span, :POS] = (jnp.floor((column * POS + 0.5) / across) == table).astype(LOW)
        r.pos[span, POS:] = (jnp.floor((line * POS + 0.5) / upright) == table).astype(LOW)
        r.cols[span, 0:1] = segment
        r.segment[pack : pack + 1] = column_sum((iota((slots, tokens), 1) >= ends_column).astype(FULL))

    def read_vectors(self):
        r = self.r
        blocks = r.g_vec[...].reshape(-1, 8, 128)
        count = blocks.shape[0]
        share = self.width // count
        wide = iota((128, self.width), 1)
        owner = jnp.floor((wide[:1] + 0.5) / share)
        spread = (wide - owner * share == iota((128, self.width), 0)).astype(LOW)
        everywhere = dot(blocks.reshape(count * 8, 128).astype(LOW), spread).reshape(count, 8, self.width)
        mine = lax.broadcasted_iota(jnp.int32, (count, 1, self.width), 0).astype(FULL) == owner[None]
        r.vec[...] = jnp.sum(jnp.where(mine, everywhere, 0.0), axis=0)
        r.gains[...] = r.vec[...].T
        total = jnp.sum(blocks, axis=0)[6:7]
        r.weight_sum[...] = jnp.broadcast_to(row_sum(total), (1, 128))
        r.vgrad[...] = jnp.zeros(r.vgrad.shape, FULL)

    def embed(self, pack):
        r, span = self.r, self.span(pack)
        embedded = dot(r.patches[span], self.w_embed[: self.width])
        embedded = embedded + dot(r.pos[span], self.w_embed[self.width :])
        shape, scale = normal(embedded, -1)
        r.stream[span] = embedded
        r.shape_first[span] = shape.astype(LOW)
        r.cols[span, 1:2] = scale
        r.normed[span] = (shape * self.gain(0)).astype(LOW)

    def project(self, pack):
        r, span, width = self.r, self.span(pack), self.width
        for part in range(3):
            joined = dot(r.normed[span], self.w_qkv[:, part * width : (part + 1) * width])
            if part == 2:
                self.joined[2 * width :, span] = joined.T.astype(LOW)
                continue
            r.turned[...] = joined.T

            def some_heads(group, part=part):
                heads = [group * NORMS_AT_ONCE + member for member in range(NORMS_AT_ONCE)]
                owns = [tile(head, HEAD) for head in heads]
                found = [normal(r.turned[own], 0) for own in owns]
                gains = [r.gains[own, 3 + part : 4 + part] for own in owns]
                results = [shape * gain for (shape, _), gain in zip(found, gains)]
                for head, (shape, scale), result in zip(heads, found, results):
                    at = pl.ds(pl.multiple_of(part * width + head * HEAD, HEAD), HEAD)
                    self.shape_heads[at, span] = shape.astype(LOW)
                    r.scale_heads[pl.ds(part * self.head_count + head, 1), span] = scale
                    self.joined[at, span] = result.astype(LOW)

            loop(self.head_count // NORMS_AT_ONCE, some_heads)

    def mask(self, pack):
        r = self.r
        same = r.cols[self.span(pack), 0:1] == r.segment[pack : pack + 1]
        r.mask[...] = jnp.where(same, 0.0, excluded)

    def head_parts(self, head, span):
        starts = (part * self.width + head * HEAD for part in range(3))
        return [pl.ds(pl.multiple_of(start, HEAD), HEAD) for start in starts]

    def attend(self, pack):
        r, span = self.r, self.span(pack)
        self.mask(pack)

        def some_heads(group):
            heads = [group * HEADS_AT_ONCE + member for member in range(HEADS_AT_ONCE)]
            loaded = [[self.joined[at, span] for at in self.head_parts(head, span)] for head in heads]
            mask = r.mask[...]
            scores = [dot(key, query, TN) * SCORE_SCALE + mask for query, key, _ in loaded]
            tops = [jnp.max(score, axis=0, keepdims=True) for score in scores]
            grown = [jnp.exp2(score - top) for score, top in zip(scores, tops)]
            totals = [column_sum(part) for part in grown]
            shares = [(part * (1.0 / total)).astype(LOW) for part, total in zip(grown, totals)]
            mixed = [dot(parts[2], share).astype(LOW) for parts, share in zip(loaded, shares)]
            for head, top, total, result in zip(heads, tops, totals, mixed):
                r.log_total[pl.ds(head, 1), span] = top + jnp.log2(total)
                r.mixed[tile(head, HEAD), span] = result

        loop(self.head_count // HEADS_AT_ONCE, some_heads)

    def join(self, pack):
        r, span = self.r, self.span(pack)
        second = r.stream[span] + dot(r.mixed[:, span], self.w_out[...], TN)
        shape, scale = normal(second, -1)
        r.stream[span] = second
        self.shape_second[span] = shape.astype(LOW)
        r.cols[span, 2:3] = scale
        r.hidden[span] = (shape * self.gain(1)).astype(LOW)

    def widen(self, index):
        at = tile(index, 256)
        upward = dot(self.r.hidden[...], self.w_up[:, at])
        squared = upward * upward
        bent = 0.5 + 0.5 * jnp.tanh(upward * (0.7978845608 + 0.7978845608 * 0.044715 * squared))
        active = upward * bent
        steep = 2.0 * 0.7978845608 + 6.0 * 0.7978845608 * 0.044715 * squared
        self.active[:, at] = active.astype(LOW)
        self.upward[:, at] = (bent + active * (1.0 - bent) * steep).astype(LOW)

    def narrow(self, index):
        at = tile(index, 256)
        self.r.stream[:, at] += dot(self.active[...], self.w_down[:, at])

    def own_slots(self, ref, pack):
        wide = ref.shape[1]
        row = jnp.broadcast_to(ref[pack : pack + 1].astype(FULL), (self.slots, wide))
        own = self.member_index * self.slots
        lanes = lax.broadcasted_iota(jnp.int32, row.shape, 1)
        places = lax.broadcasted_iota(jnp.int32, row.shape, 0)
        return row_sum(jnp.where(lanes == own + places, row, 0.0))

    def image_spread(self, values, segment, reduce, start):
        out = jnp.full(values.shape, start, FULL)
        for slot in range(self.slots):
            inside = segment == float(slot)
            one = reduce(jnp.where(inside, values, start if reduce is jnp.max else 0.0), axis=1, keepdims=True)
            out = jnp.where(inside, one, out)
        return out

    def classify(self):
        r, slots, width, packs = self.r, self.slots, self.width, self.packs
        strip = STRIP
        per_pack = self.tokens // strip
        strips = packs * per_pack

        def finish_norm(index):
            rows = tile(index, strip)
            shape, _ = normal(r.stream[rows], -1)
            r.low[rows] = (shape * self.gain(2)).astype(LOW)

        loop(strips, finish_norm)
        marks = self.head_marks()
        marks_low = marks.astype(LOW)
        probe = self.gain(5)
        probe_marks = (marks * probe).astype(LOW)
        finals = [r.low[self.span(pack)] for pack in range(packs)]
        scores = [dot(probe_marks, final, NT) for final in finals]
        scores = jnp.concatenate(scores, axis=0) * HEAD ** (-0.5)
        tall = (marks.shape[0], self.tokens)
        segment = [jnp.broadcast_to(r.segment[pack : pack + 1], tall) for pack in range(packs)]
        segment = jnp.concatenate(segment, axis=0)
        top = self.image_spread(scores, segment, jnp.max, excluded)
        grown = jnp.where(segment < float(slots), jnp.exp(scores - top), 0.0)
        pooling = grown / jnp.maximum(self.image_spread(grown, segment, jnp.sum, 1.0), 1e-30)
        pool_wide = pooling.astype(LOW).astype(FULL)
        r.pool_heads[...] = pool_wide
        for pack, final in enumerate(finals):
            member = (r.segment[pack : pack + 1] == iota((slots, self.tokens), 0)).astype(FULL)
            first = pack * marks.shape[0]
            stacked = [
                member * pool_wide[first + head : first + head + 1] for head in range(self.head_count)
            ]
            stacked = dot(jnp.concatenate(stacked, axis=0).astype(LOW), final)
            pooled = jnp.zeros((slots, width), FULL)
            for head in range(self.head_count):
                pooled = pooled + stacked[head * slots : (head + 1) * slots] * marks[head : head + 1]
            r.pooled[pack * slots : (pack + 1) * slots] = pooled.astype(LOW)
        pooled = r.pooled[...]
        padded, classes = r.g_cls.shape[-1], r.w_cls.shape[1]
        logits = [dot(pooled, self.class_block(group)[...]) for group in range(self.groups)]
        logits = jnp.concatenate(logits, axis=1)
        lanes = iota(logits.shape, 1)
        block = jnp.floor((lanes + 0.5) / padded)
        within = lanes - block * padded
        logits = jnp.where(within < classes, logits, excluded)
        labels, weights = (
            jnp.concatenate([self.own_slots(ref, pack) for pack in range(packs)], axis=0)
            for ref in (r.labels, r.weights)
        )
        hit = block * classes + within == labels
        hit = (hit & (within < classes)).astype(FULL)
        top = jnp.max(logits, axis=1, keepdims=True)
        log_total = top + jnp.log(row_sum(jnp.exp(logits - top)))
        losses = weights * (log_total - row_sum(hit * logits))
        first = (iota((1, width), 1) == 0.0).astype(FULL)
        r.vgrad[6:7] += first * column_sum(losses)
        share = weights / r.weight_sum[:, :1]
        logit_grad = ((jnp.exp(logits - log_total) - hit) * share).astype(LOW)
        r.logit_grad[...] = logit_grad
        pooled_grad = jnp.zeros((packs * slots, width), FULL)
        for group in range(self.groups):
            part = logit_grad[:, group * padded : (group + 1) * padded]
            pooled_grad = pooled_grad + dot(part, self.class_block(group)[...], NT)
        r.image_high[...], r.image_rest[...] = halves(pooled_grad)

        def strip_spots(index):
            pack = index // per_pack
            heads = pl.ds(pl.multiple_of(pack * marks.shape[0], 16), marks.shape[0])
            images = pl.ds(pl.multiple_of(pack * slots, 16), slots)
            return tile(index, strip), heads, images, tile(index % per_pack, strip)

        def image_rows(rows, images):
            member_rows = (iota((strip, slots), 1) == r.cols[rows, 0:1]).astype(LOW)
            return dot(member_rows, r.image_high[images]) + dot(member_rows, r.image_rest[images])

        def weigh(index):
            rows, heads, images, lanes = strip_spots(index)
            product = image_rows(rows, images) * r.low[rows].astype(FULL)
            r.score_heads[heads, lanes] = fine_dot(marks_low, product, NT)

        loop(strips, weigh)
        weight_grad = r.score_heads[...]
        mean = self.image_spread(pooling * weight_grad, segment, jnp.sum, 0.0)
        r.score_heads[...] = pooling * (weight_grad - mean) * HEAD ** (-0.5)

        def strip_back(index):
            rows, heads, images, lanes = strip_spots(index)
            high, rest = halves(r.score_heads[heads, lanes])
            score_rows = dot(high, marks_low, TN) + dot(rest, marks_low, TN)
            pool_rows = dot(r.pool_heads[heads, lanes].astype(LOW), marks_low, TN)
            r.vgrad[5:6] += column_sum(score_rows * r.low[rows].astype(FULL))
            final_grad = pool_rows * image_rows(rows, images) + score_rows * probe
            shape, scale = normal(r.stream[rows], -1)
            r.vgrad[2:3] += column_sum(final_grad * shape)
            residual_grad = normal_back(final_grad * self.gain(2), shape, scale, -1)
            r.stream[rows] = residual_grad
            r.low[rows] = residual_grad.astype(LOW)

        loop(strips, strip_back)

    def class_back(self):
        r = self.r
        r.turned[...] = jnp.zeros(r.turned.shape, FULL)
        padded = r.g_cls.shape[-1]
        for group in range(self.groups):
            part = r.logit_grad[:, group * padded : (group + 1) * padded]
            self.class_block(group)[...] = dot(r.pooled[...], part, TN).astype(LOW)

    def active_back(self, index):
        at = tile(index, 256)
        upstream = dot(self.r.low[...], self.w_down[at], NT)
        self.upward[:, at] = (upstream * self.upward[:, at].astype(FULL)).astype(LOW)

    def down_weight(self, index):
        at = tile(index, 256)
        self.w_down[at] = dot(self.active[:, at], self.r.low[...], TN).astype(LOW)

    def second_back(self, pack):
        r, span = self.r, self.span(pack)
        upstream = dot(self.upward[span], self.w_up[...], NT)
        shape = self.shape_second[span].astype(FULL)
        r.vgrad[1:2] += column_sum(upstream * shape)
        back = normal_back(upstream * self.gain(1), shape, r.cols[span, 2:3], -1)
        total = r.stream[span] + back
        r.stream[span] = total
        r.low[span] = total.astype(LOW)

    def up_weight(self, index, part):
        rows, columns = tile(index, 256), pl.ds(part * COLUMNS, COLUMNS)
        self.w_up[rows, columns] = dot(self.r.hidden[:, rows], self.upward[:, columns], TN).astype(LOW)

    def mixed_back(self, pack):
        r, span = self.r, self.span(pack)
        r.hidden[span] = dot(r.low[span], self.w_out[...], NT).astype(LOW)

    def out_weight(self, index):
        at = tile(index, 256)
        self.w_out[at] = dot(self.r.mixed[at], self.r.low[...]).astype(LOW)

    def attend_back(self, pack):
        r, span = self.r, self.span(pack)
        self.mask(pack)
        r.mixed[:, span] = r.hidden[span].T
        count = self.head_count

        def some_heads(group):
            heads = [group * HEADS_AT_ONCE + member for member in range(HEADS_AT_ONCE)]
            places = [self.head_parts(head, span) for head in heads]
            loaded = [[self.joined[at, span] for at in place] for place in places]
            mixed_grads = [r.mixed[tile(head, HEAD), span] for head in heads]
            log_totals = [r.log_total[pl.ds(head, 1), span] for head in heads]
            norms = []
            for part in range(2):
                for head, place in zip(heads, places):
                    shape = self.shape_heads[place[part], span].astype(FULL)
                    scale = r.scale_heads[pl.ds(part * count + head, 1), span]
                    gain = r.gains[tile(head, HEAD), 3 + part : 4 + part]
                    norms.append((shape, scale, gain))
            mask = r.mask[...]
            scores = [dot(key, query, TN) * SCORE_SCALE + mask for query, key, _ in loaded]
            shares = [jnp.exp2(score - log_total) for score, log_total in zip(scores, log_totals)]
            share_grads = [dot(parts[2], grad, TN) for parts, grad in zip(loaded, mixed_grads)]
            means = [column_sum(share * grad) for share, grad in zip(shares, share_grads)]
            score_grads = [
                (share * (grad - mean)).astype(LOW)
                for share, grad, mean in zip(shares, share_grads, means)
            ]
            value_grads = [
                dot(grad, share.astype(LOW), NT) for grad, share in zip(mixed_grads, shares)
            ]
            grads = [dot(parts[1], grad) for parts, grad in zip(loaded, score_grads)]
            grads += [dot(parts[0], grad, NT) for parts, grad in zip(loaded, score_grads)]
            grads = [grad * HEAD ** (-0.5) for grad in grads]
            terms = [grad * shape for grad, (shape, _, _) in zip(grads, norms)]
            backs = [
                normal_back(grad * gain, shape, scale, 0)
                for grad, (shape, scale, gain) in zip(grads, norms)
            ]
            for place, grad in zip(places, value_grads):
                self.joined[place[2], span] = grad.astype(LOW)
            at = 0
            for part in range(2):
                lanes = pl.ds(part * 128, 128)
                for head, place in zip(heads, places):
                    term = terms[at]
                    term = sum(term[:, low : low + 128] for low in range(0, self.tokens, 128))
                    r.turned[tile(head, HEAD), lanes] += term
                    self.joined[place[part], span] = backs[at].astype(LOW)
                    at += 1

        loop(count // HEADS_AT_ONCE, some_heads)

    def first_back(self, pack):
        r, span = self.r, self.span(pack)
        upstream = dot(self.joined[:, span].T, self.w_qkv[...], NT)
        shape = r.shape_first[span].astype(FULL)
        r.vgrad[0:1] += column_sum(upstream * shape)
        back = normal_back(upstream * self.gain(0), shape, r.cols[span, 1:2], -1)
        r.low[span] = (r.stream[span] + back).astype(LOW)

    def qkv_weight(self, index):
        rows = tile(index, 256)
        turned = self.r.normed[:, rows].T
        for part in range(3):
            columns = pl.ds(part * COLUMNS, COLUMNS)
            self.w_qkv[rows, columns] = dot(turned, self.joined[columns], NT).astype(LOW)

    def embed_weight(self):
        r, width = self.r, self.width

        def one(index):
            at = tile(index, 256)
            self.w_embed[at] = dot(r.patches[:, at], r.low[...], TN).astype(LOW)

        loop(width // 256, one)
        self.w_embed[width:] = dot(r.pos[...], r.low[...], TN).astype(LOW)

    def head_gains(self):
        r = self.r
        for part in range(2):
            sums = r.turned[:, part * 128 : (part + 1) * 128]
            r.vgrad[3 + part : 4 + part] = column_sum(sums.T)


def kernel(dims, names, pieces, class_pieces, spots, *refs):
    r = types.SimpleNamespace(**dict(zip(names, refs)))
    place = Place(dims)
    barrier = pltpu.get_barrier_semaphore()
    greeted = place.plane() + [{"z": step} for step in place.steps("z")]
    pl.semaphore_wait(barrier, place.tell(barrier, greeted))
    courier = Courier(place, r.send, r.recv)
    layer = Layer(r, place, dims)
    z, y, x, core = (place.at[axis] for axis in "zyxc")
    shards = [r.w_embed, r.w_qkv, r.w_out, r.w_up, r.w_down]
    full = [r.g_embed, r.g_qkv, r.g_out, r.g_up, r.g_down]
    pairs = [r.p_embed, r.p_qkv, r.p_out, r.p_up, r.p_down]
    owned = [r.o_embed, r.o_qkv, r.o_out, r.o_up, r.o_down]
    order = (0, 1, 2, 3, 4)

    arriving = []
    for shard, pair in zip(shards, pairs):
        rows, half = shard.shape[0], shard.shape[1] // CORES
        at = pl.ds(pl.multiple_of(core * rows, 8), rows)
        other = pl.ds(pl.multiple_of((1 - core) * half, 128), half)
        arriving.append(courier.start({"c": 1}, shard.at[:, other], pair.at[at]))
        pair[at] = shard[:, pl.ds(pl.multiple_of(core * half, 128), half)]
    r.g_vec[z, y, x, core] = jnp.zeros((8, 128), FULL)
    count = r.vectors.shape[1]
    r.g_vec[z, y, x, core, pl.ds(0, 6), pl.ds(0, count)] = r.vectors[...].astype(LOW).astype(FULL)
    wide = r.weights.shape[1]
    own = layer.member_index * layer.slots
    lanes = lax.broadcasted_iota(jnp.int32, r.weights.shape, 1)
    inside = (lanes >= own) & (lanes < own + layer.slots)
    counted = column_sum(jnp.where(inside, r.weights[...], 0).astype(FULL))
    r.g_vec[z, y, x, core, pl.ds(6, 1), pl.ds(0, wide)] = counted
    block = r.g_cls.at[x, core, z, y]
    block[...] = jnp.zeros(block.shape, LOW)
    block[:, pl.ds(0, r.w_cls.shape[1])] = r.w_cls[...].astype(LOW)

    def matrix_view(piece, core):
        index, rows, columns, _ = piece
        half = full[index].shape[-1] // CORES
        across = pl.ds(pl.multiple_of(core * half + columns[0], 128), columns[1])
        return lambda z, y, x: full[index].at[z, y, x, pl.ds(*rows), across]

    def class_view(piece, core):
        return lambda z, y, x: r.g_cls.at[x, core, z, y, pl.ds(*piece[1])]

    spreads = [Spread(courier, lambda z, y, x: r.g_vec.at[z, y, x, core], "zxy")]
    ready, last = {}, {}
    sequence = [piece for piece in pieces if piece[0] < 4] + class_pieces
    sequence += [piece for piece in pieces if piece[0] == 4]
    for piece in sequence:
        index = piece[0]
        if index < 5 and index not in last:
            ready[len(spreads)] = index
        last[index] = len(spreads)
        view = matrix_view(piece, core) if index < 5 else class_view(piece, core)
        spreads.append(Spread(courier, view, piece[3]))

    def begin(position):
        if position in ready:
            index = ready[position]
            arriving[index].wait_recv()
            half = pairs[index].shape[1]
            across = pl.ds(pl.multiple_of(core * half, 128), half)
            full[index][z, y, x, :, across] = pairs[index][...].astype(LOW)
        spreads[position].begin()

    lag = GATHER_LAGS
    actions = (
        begin,
        lambda i: spreads[i].middle(1),
        lambda i: spreads[i].middle(2),
        lambda i: spreads[i].middle(3),
        lambda i: spreads[i].done(),
    )
    turns = iter(range(lag[0], len(spreads) + lag[-1]))
    gathered = [0]

    def turn(times=1):
        for now in itertools.islice(turns, times):
            for late, action in zip(lag, actions):
                if 0 <= now - late < len(spreads):
                    action(now - late)
            gathered[0] = now - lag[-1] + 1

    def until(index):
        while gathered[0] <= last[index]:
            turn()

    turn(3)
    for pack in range(layer.packs):
        layer.place_rows(pack)
        turn()
    until(0)
    layer.read_vectors()
    for pack in range(layer.packs):
        layer.embed(pack)
        turn()
    until(1)
    for pack in range(layer.packs):
        layer.project(pack)
        turn()
        layer.attend(pack)
        turn()
    until(2)
    for pack in range(layer.packs):
        layer.join(pack)
    turn()
    until(3)
    tiles = layer.hidden_units // 256
    for index in range(4):
        loop(tiles // 4, lambda step: layer.widen(step + tiles // 4 * index))
        turn()
    until(5)
    until(4)
    loop(layer.width // 256, layer.narrow)

    layer.classify()
    courier.finish()
    layer.class_back()
    left = {index: sum(piece[0] == index for piece in pieces) for index in order}
    closing = {}

    def keep(piece):
        index, rows, columns, _ = piece

        def finish(total):
            pairs[index][pl.ds(*rows), pl.ds(*columns)] = total
            left[index] -= 1
            if left[index]:
                return
            count, half = owned[index].shape[0], owned[index].shape[1] // CORES
            across = pl.ds(pl.multiple_of(core * half, 128), half)
            other = pairs[index].at[pl.ds(pl.multiple_of((1 - core) * count, 8), count)]
            closing[index] = courier.start({"c": 1}, other, owned[index].at[:, across])
            owned[index][:, across] = pairs[index][pl.ds(pl.multiple_of(core * count, 8), count)]

        return finish

    def keep_class(piece):
        def finish(total):
            r.o_cls[pl.ds(*piece[1])] = total[:, : r.o_cls.shape[1]]

        return finish

    under_way = []
    clock = {"now": 0, "last": 0}

    def send_class():
        padded = r.g_cls.shape[-1]
        for piece in class_pieces:
            pool = Pool(r.pool_cls, "xzy", piece[1], 0, padded, padded)

            def view(core, piece=piece):
                return class_view(piece, core)(ALL, ALL, ALL)

            fold = Fold(courier, view, piece[3][::-1], pool, keep_class(piece))
            fold.begin()
            fold.entry = clock["last"] = max(clock["now"], clock["last"]) + 1
            under_way.append(fold)

    def send_matrix(index, pool_ref):
        mine = [piece for piece in pieces if piece[0] == index]
        stack = pool_ref.shape[-2] // mine[0][1][1]
        spots, total = [], 0
        for position, (_, rows, columns, _) in enumerate(mine):
            if position % stack == 0:
                start, total = total, total + max(p[2][1] for p in mine[position : position + stack])
            spots.append(((position % stack * rows[1], rows[1]), start))
        folds = []
        for piece, (rows, column) in zip(mine, spots):
            width = piece[2][1]
            pool = Pool(pool_ref, "zyx", rows, column, column + total, width)

            def view(core, piece=piece):
                return matrix_view(piece, core)(ALL, ALL, ALL)

            fold = Fold(courier, view, piece[3][::-1], pool, keep(piece))
            fold.begin()
            fold.entry = clock["last"] = max(clock["now"], clock["last"]) + 1
            folds.append(fold)
        under_way.extend(folds)

    def pump(times=1):
        for _ in range(times):
            clock["now"] += 1
            for fold in list(under_way)[:: NEWEST_FIRST]:
                if fold.due is None and fold.entry <= clock["now"]:
                    fold.due = clock["now"]
                if fold.due is not None and fold.due <= clock["now"]:
                    fold.due = clock["now"] + FOLD_LAG
                    if fold.advance():
                        under_way.remove(fold)

    def free(which):
        pl.semaphore_wait(r.free.at[which], place.tell(r.free.at[which], place.lines()))

    send_class()
    for index in range(3):
        loop(tiles // 3, lambda step: layer.active_back(step + tiles // 3 * index))
        pump()
    for index in range(3):
        loop(tiles // 3, lambda step: layer.down_weight(step + tiles // 3 * index))
        pump()
    free(0)
    send_matrix(4, r.active)
    for pack in range(layer.packs):
        layer.second_back(pack)
        pump()
    for part in range(layer.hidden_units // COLUMNS):
        loop(layer.width // 256, lambda index: layer.up_weight(index, part))
        pump()
    free(1)
    send_matrix(3, r.upward)
    for pack in range(layer.packs):
        layer.mixed_back(pack)
    pump()
    loop(layer.width // 256, layer.out_weight)
    send_matrix(2, r.shape_second)
    pump()
    for pack in range(layer.packs):
        layer.attend_back(pack)
        pump(2)
    for pack in range(layer.packs):
        layer.first_back(pack)
        pump()
    loop(layer.width // 256, layer.qkv_weight)
    free(2)
    send_matrix(1, r.joined)
    pump()
    layer.embed_weight()
    send_matrix(0, r.shape_heads)
    layer.head_gains()
    lanes = iota((1, layer.width), 1)
    devices = dims["x"] * dims["y"] * dims["z"] * CORES
    r.vgrad[6:7] += jnp.where(lanes == 1.0, r.weight_sum[:, :1] / devices, 0.0)

    strips = []
    at = 0
    for index in order:
        rows, wide = shards[index].shape
        for low in range(0, wide, COLUMNS):
            strips.append((index, pl.ds(low, COLUMNS), rows, at))
            at += rows
    total_rows = at
    moments = [
        (r.m_embed, r.v_embed), (r.m_qkv, r.v_qkv), (r.m_out, r.v_out), (r.m_up, r.v_up),
        (r.m_down, r.v_down), (r.m_vectors, r.v_vectors), (r.m_cls, r.v_cls),
    ]
    loads = []
    for position, (index, columns, rows, at) in enumerate(strips):
        for which in range(2):
            loads.append(
                pltpu.make_async_copy(
                    moments[index][which].at[:, columns],
                    r.stream.at[pl.ds(at + which * total_rows, rows)],
                    r.local.at[len(loads)],
                )
            )
            loads[-1].start()
    vec_total = Total(courier, r.vec_plane, r.vec_line)
    vec_total.send(0, r.vgrad[...])
    pump(2)
    vec_total.send(1, vec_total.receive(0))
    while under_way:
        pump()
    vec_sum = vec_total.receive(1)
    for index in order:
        closing[index].wait_recv()
    for load in loads:
        load.wait()

    def put(name, value):
        at, shape = spots[name]
        r.small[pl.ds(at, shape[0]), pl.ds(0, shape[1])] = value

    vec_count = r.vectors.shape[1]
    device = ((z * dims["y"] + y) * dims["x"] + x) * CORES + core
    at_row = lax.broadcasted_iota(jnp.int32, (layer.width, 128), 0)
    at_lane = lax.broadcasted_iota(jnp.int32, (layer.width, 128), 1)
    chosen = ((at_row == device * vec_count + at_lane) & (at_lane < vec_count)).astype(FULL)
    picked = jnp.dot(vec_sum, chosen, precision=highest, preferred_element_type=FULL)
    vec_grad = picked[:6, :vec_count]
    mats = list(zip(owned + [r.o_cls], shards + [r.w_cls]))
    parts = [squares(grad[...]) for grad, _ in mats] + [squares(weight[...]) for _, weight in mats]
    block = jnp.concatenate(parts + [wide_rows(r.vectors[...]), jnp.zeros((6, 128), FULL)], axis=0)
    block = Total(courier, r.one_plane, r.one_line).through(block)
    sums = row_sum(block)
    vec_squares = row_sum(vec_sum * vec_sum)
    put("loss", vec_sum[6:7, :2])
    clip_norm = jnp.sqrt(column_sum(sums[:6]) + column_sum(vec_squares[:6]))
    put("clip", clip_norm)
    factor = jnp.minimum(1.0, clip_limit / clip_norm)
    partial = {index: jnp.zeros((1, 128), FULL) for index in order}
    stores = []

    def store(source, at, rows):
        target = r.state.at[pl.ds(at, rows)]
        copy = pltpu.make_async_copy(source, target, r.local.at[len(loads) + len(stores)])
        copy.start()
        stores.append(copy)

    for index, columns, rows, at in strips:
        spot = [pl.ds(at + which * total_rows, rows) for which in range(2)]
        first, second = moments_step(
            owned[index][:, columns] * factor, r.stream[spot[0]], r.stream[spot[1]]
        )
        update = update_of(first, second, shards[index][:, columns])
        owned[index][:, columns] = update
        partial[index] = partial[index] + squares(update)
        for which, value in enumerate((first, second)):
            r.stream[spot[which]] = value
            store(r.stream.at[spot[which]], at + which * total_rows, rows)
    first, second = moments_step(r.o_cls[...] * factor, r.m_cls[...], r.v_cls[...])
    put("cls_first", first)
    put("cls_second", second)
    class_update = update_of(first, second, r.w_cls[...])
    r.o_cls[...] = class_update
    first, second = moments_step(vec_grad * factor, r.m_vectors[...], r.v_vectors[...])
    put("vectors_first", first)
    put("vectors_second", second)
    vec_update = update_of(first, second, r.vectors[...])
    parts = [partial[index] for index in order] + [squares(class_update), wide_rows(vec_update)]
    block = jnp.concatenate(parts + [jnp.zeros((4, 128), FULL)], axis=0)
    block = Total(courier, r.two_plane, r.two_line).through(block)
    grown = jnp.sqrt(row_sum(block))[:12]
    weight_norms = jnp.sqrt(sums[6:18])
    put("norms", jnp.concatenate([weight_norms, grown], axis=1))
    ratios = learn_rate * (weight_norms / grown)
    for index, columns, rows, at in strips:
        update = owned[index][:, columns]
        owned[index][:, columns] = shards[index][:, columns] - ratios[index : index + 1] * update
        store(owned[index].at[:, columns], at + 2 * total_rows, rows)
    put("cls_new", r.w_cls[...] - ratios[5:6] * r.o_cls[...])
    put("vectors_new", r.vectors[...] - ratios[6:12] * vec_update)
    for copy in stores:
        copy.wait()
    courier.finish()


def hand_out(shapes, spots, state, small, *outs):
    total = sum(shape[0] * shape[1] // COLUMNS for shape in shapes)
    at = 0
    for index, (rows, wide) in enumerate(shapes):
        for low in range(0, wide, COLUMNS):
            for which, part in enumerate((2, 0, 1)):
                out = outs[3 + 3 * index + which]
                out[:, pl.ds(low, COLUMNS)] = state[pl.ds(part * total + at, rows)]
            at += rows
    for out, (at, shape) in zip(outs[:3] + outs[18:], spots.values()):
        out[...] = small[pl.ds(at, shape[0]), pl.ds(0, shape[1])]


KINDS = ("_new", "_first", "_second")
WEIGHTS = ("embed", "qkv", "out", "up", "down", "vectors", "cls")


def kernel_body(
    dims, patches, heights, widths, labels, res_weights, *params_moments
):
    X, Y, Z = (dims[axis] for axis in "xyz")
    params, moments = params_moments[:7], params_moments[7:]
    mats, w_cls = params[:5], params[6]
    blocks = [(CORES * w.shape[0], w.shape[1] // CORES) for w in mats]
    pieces = pieces_of(blocks)
    padded = -(-w_cls.shape[1] // 128) * 128
    class_rows = w_cls.shape[0]
    class_pieces = [
        (5, rows, columns, ("zxy", "zyx")[turn])
        for turn, (rows, columns) in enumerate(cut_rows(class_rows, padded, 2))
    ]
    packs, tokens, width = patches.shape
    rows = packs * tokens
    chips = X * Y * Z
    hidden_units = mats[3].shape[1]
    heads = width // HEAD
    images = packs * heights.shape[1]
    vmem = pl.BlockSpec(memory_space=pltpu.VMEM)
    anywhere = pl.BlockSpec(memory_space=pl.ANY)
    inputs = {"patches": patches.reshape(rows, width), "heights": heights, "widths": widths}
    inputs.update(labels=labels, weights=res_weights)
    specs = [vmem] * 5
    for name, param in zip(WEIGHTS, params):
        inputs["vectors" if name == "vectors" else "w_" + name] = param
        specs.append(vmem)
    for position, name in enumerate(WEIGHTS):
        inputs["m_" + name], inputs["v_" + name] = moments[2 * position : 2 * position + 2]
        specs += [anywhere if position < 5 else vmem] * 2
    small = {"loss": (1, 2), "clip": (1, 1), "norms": (12, 2)}
    for name, param in zip(WEIGHTS[5:], params[5:]):
        small.update({name + kind: param.shape for kind in KINDS})
    spots, tall = {}, 0
    for name, shape in small.items():
        spots[name] = (tall, shape)
        tall += -(-shape[0] // 8) * 8
    strips = sum(w.shape[0] * w.shape[1] // COLUMNS for w in mats)
    outs = {"state": (3 * strips, COLUMNS), "small": (tall, padded)}
    out_specs = [anywhere, vmem]
    scratch = {}
    for name, param, block in zip(WEIGHTS, mats, blocks):
        scratch["g_" + name] = pltpu.VMEM((Z, Y, X, block[0], param.shape[1]), LOW)
        scratch["p_" + name] = pltpu.VMEM(block, FULL)
        scratch["o_" + name] = pltpu.VMEM(param.shape, FULL)
    scratch["o_cls"] = pltpu.VMEM(w_cls.shape, FULL)
    scratch["g_cls"] = pltpu.VMEM((X, CORES, Z, Y, class_rows, padded), LOW)
    scratch["g_vec"] = pltpu.VMEM((Z, Y, X, CORES, 8, 128), FULL)
    scratch["pool_cls"] = pltpu.VMEM((X, Z, Y, class_rows, 2 * padded), LOW)
    scratch["shape_second"] = pltpu.VMEM((Z, Y, X, rows // chips, width), LOW)
    low_rows = ("normed", "hidden", "shape_first", "low")
    scratch.update({name: pltpu.VMEM((rows, width), LOW) for name in low_rows})
    scratch["pos"] = pltpu.VMEM((rows, 2 * POS), LOW)
    scratch["cols"] = pltpu.VMEM((rows, 128), FULL)
    scratch["segment"] = pltpu.VMEM((packs, tokens), FULL)
    scratch["stream"] = pltpu.VMEM((rows, width), FULL)
    scratch["turned"] = pltpu.VMEM((width, tokens), FULL)
    scratch["joined"] = pltpu.VMEM((Z, Y, X, 3 * width // chips, rows), LOW)
    scratch["shape_heads"] = pltpu.VMEM((Z, Y, X, 2 * width // chips, rows), LOW)
    scratch["scale_heads"] = pltpu.VMEM((2 * heads, rows), FULL)
    scratch["log_total"] = pltpu.VMEM((heads, rows), FULL)
    scratch["mixed"] = pltpu.VMEM((width, rows), LOW)
    scratch["mask"] = pltpu.VMEM((tokens, tokens), FULL)
    wide = (Z, Y, X, rows // chips, hidden_units)
    scratch["upward"], scratch["active"] = pltpu.VMEM(wide, LOW), pltpu.VMEM(wide, LOW)
    scratch["vec"], scratch["vgrad"] = pltpu.VMEM((8, width), FULL), pltpu.VMEM((8, width), FULL)
    scratch["gains"] = pltpu.VMEM((width, 8), FULL)
    scratch["weight_sum"] = pltpu.VMEM((1, 128), FULL)
    scratch["pooled"] = pltpu.VMEM((images, width), LOW)
    for name in ("pool_heads", "score_heads"):
        scratch[name] = pltpu.VMEM((16 * packs, tokens), FULL)
    for name in ("image_high", "image_rest"):
        scratch[name] = pltpu.VMEM((images, width), LOW)
    scratch["logit_grad"] = pltpu.VMEM((images, X * CORES * padded), LOW)
    for name, shape in (("vec_", (8, width)), ("one_", (24, 128)), ("two_", (16, 128))):
        scratch[name + "plane"] = pltpu.VMEM((X * Y * CORES,) + shape, FULL)
        scratch[name + "line"] = pltpu.VMEM((Z,) + shape, FULL)
    peers = (X - 1) + (Y - 1) + (Z - 1) + 1
    count = (1 + len(pieces) + len(class_pieces)) * 3 * peers
    count += 10 + 3 * (X * Y * CORES - 1 + Z - 1) + 2 * peers
    scratch["send"] = pltpu.SemaphoreType.DMA((count,))
    scratch["recv"] = pltpu.SemaphoreType.DMA((count,))
    scratch["local"] = pltpu.SemaphoreType.DMA((5 * sum(w.shape[1] // COLUMNS for w in mats),))
    scratch["free"] = pltpu.SemaphoreType.REGULAR((3,))
    names = list(inputs) + list(outs) + list(scratch)
    state, rest = pl.pallas_call(
        functools.partial(kernel, dims, names, pieces, class_pieces, spots),
        out_shape=[jax.ShapeDtypeStruct(shape, FULL) for shape in outs.values()],
        in_specs=specs,
        out_specs=out_specs,
        scratch_shapes=list(scratch.values()),
        compiler_params=pltpu.CompilerParams(
            collective_id=0, has_side_effects=True, vmem_limit_bytes=(64 << 20) - 4096
        ),
    )(*inputs.values())
    shapes = [small["loss"], small["clip"], small["norms"]]
    for param in params:
        shapes += [param.shape] * 3
    loss_terms, clip_norm, *updated = pl.pallas_call(
        functools.partial(hand_out, [w.shape for w in mats], spots),
        out_shape=[jax.ShapeDtypeStruct(shape, FULL) for shape in shapes],
        in_specs=[vmem] * 2,
        out_specs=[vmem] * 24,
        compiler_params=pltpu.CompilerParams(vmem_limit_bytes=32 << 20),
    )(state, rest)
    return (loss_terms.reshape(2), clip_norm.reshape(()), *updated)


def chip_dims(mesh):
    across, along = mesh.shape["mp"] // CORES, mesh.shape["dp"]
    return {"x": across, "y": across, "z": along // across}


def fits(mesh, width):
    devices = mesh.shape["dp"] * mesh.shape["mp"]
    dims = chip_dims(mesh)
    same = dims["x"] * dims["y"] * dims["z"] * CORES == devices
    return same and width % (8 * devices) == 0 and width // devices * CORES % 16 == 0


def solution(mesh):
    placed = (
        P(None, ("dp", "mp"), None),
        P(None, ("dp", "mp")),
        P(None, ("dp", "mp")),
        P(None, "dp"),
        P(None, "dp"),
        P(("dp", "mp"), None),
        P(("dp", "mp"), None),
        P(("dp", "mp"), None),
        P(("dp", "mp"), None),
        P(("dp", "mp"), None),
        P(None, ("dp", "mp")),
        P("dp", "mp"),
        P(("dp", "mp"), None),
        P(("dp", "mp"), None),
        P(("dp", "mp"), None),
        P(("dp", "mp"), None),
        P(("dp", "mp"), None),
        P(("dp", "mp"), None),
        P(("dp", "mp"), None),
        P(("dp", "mp"), None),
        P(("dp", "mp"), None),
        P(("dp", "mp"), None),
        P(None, ("dp", "mp")),
        P(None, ("dp", "mp")),
        P("dp", "mp"),
        P("dp", "mp"),
    )
    run = body
    if fits(mesh, 768):
        run = functools.partial(kernel_body, chip_dims(mesh))
    return jax.shard_map(
        run,
        mesh=mesh,
        in_specs=placed,
        out_specs=(
            P(),
            P(),
            P(),
            P(("dp", "mp"), None),
            P(("dp", "mp"), None),
            P(("dp", "mp"), None),
            P(("dp", "mp"), None),
            P(("dp", "mp"), None),
            P(("dp", "mp"), None),
            P(("dp", "mp"), None),
            P(("dp", "mp"), None),
            P(("dp", "mp"), None),
            P(("dp", "mp"), None),
            P(("dp", "mp"), None),
            P(("dp", "mp"), None),
            P(("dp", "mp"), None),
            P(("dp", "mp"), None),
            P(("dp", "mp"), None),
            P(None, ("dp", "mp")),
            P(None, ("dp", "mp")),
            P(None, ("dp", "mp")),
            P("dp", "mp"),
            P("dp", "mp"),
            P("dp", "mp"),
        ),
        check_vma=False,
    )
```
